32 devices in a mesh: grp: 2 (over y), code: 4 (over z), rep: 4 (over x, core).
Axes of the slice: x: 2, y: 2, z: 4, core: 2. Of those that a mesh axis runs over, the one named last changes fastest.
Arguments:
- state_slab: float32 [8, 4, 128, 512], P(('grp', 'rep'), 'code'), parts along dimension 0, may hold values from -6 to 6
- previous_slab: float32 [8, 4, 128, 512], P(('grp', 'rep'), 'code'), parts along dimension 0, may hold values from -6 to 6
- previous_parity: float32 [8, 128, 2048], P(('grp', 'rep'), 'code'), parts along dimension 0, may hold values from -6 to 6
- generator: float32 [4, 4], replicated, as said below
- failed_ids: int32 [8, 2], P(('grp', 'rep')), parts along dimension 0, may hold values from 0 to 3, as said below
Outputs:
- new_parity: float32 [8, 128, 2048], P(('grp', 'rep'), 'code'), parts along dimension 0
- restored_state: float32 [8, 4, 128, 512], P(('grp', 'rep'), 'code'), parts along dimension 0
The draws below stay inside these ranges and needn't reach their ends.
There are 2 independent parts, one for each index of `grp`. The reference program is written for one: setup_inputs(seed, part) draws one part's arguments, and reference() takes and returns one part's arrays. A program takes and returns all parts, laid end to end along the dimension named above; an argument that names none is the same for every part. Nothing has to cross between parts.
Inputs may be any that keep to these rules, and one draw needn't show every extreme that they name: generator has first row all ones; for any two columns at cyclic distance at least 1 the Gram determinant of those columns is at least 2. `failed_ids`: the two failed members of a stripe differ, and their cyclic distance along the stripe is at least 1.
All inputs are finite; a program needn't handle non-finite values.
Results may differ from the reference program's by a relative error of at most 0.00007.
Values sent between devices are 32-bit elements; how exact they have to be, the bound alone decides.
No kernel may reach another device: no remote copies, remote signals or barrier semaphores. Data moves between devices by JAX's collectives and lax.ppermute only.
A program may use at most 64 MiB of HBM per device.

```python
import math
import jax
import jax.numpy as jnp
from jax import lax

SLAB_ROW_COUNT = 128
ENTRIES_PER_ROW = 512
PARITY_SPANS = 4
N_CODE = 4
N_REP = 4


def draw_generator(key, part):
    key = jax.random.fold_in(key, 5)
    key_angle, key_last = jax.random.split(key)
    spacing = 2.0 * math.pi / N_CODE
    jitter = jax.random.uniform(key_angle, (N_CODE,), jnp.float32, -spacing / 8.0, spacing / 8.0)
    angles = spacing * jnp.arange(N_CODE, dtype=jnp.float32) + jitter
    last_row = jax.random.normal(key_last, (N_CODE,), jnp.float32)
    rows = [jnp.ones((N_CODE,), jnp.float32), jnp.cos(angles), jnp.sin(angles), last_row]
    return jnp.stack(rows, axis=0)[:PARITY_SPANS]


def draw_failed_ids(key, part):
    key = jax.random.fold_in(key, 7)
    key_first, key_gap = jax.random.split(key)
    failed_one = jax.random.randint(key_first, (N_REP,), 0, N_CODE)
    quarter = N_CODE // 4
    gap = jax.random.randint(key_gap, (N_REP,), quarter, N_CODE - quarter + 1)
    second = (failed_one + gap) % N_CODE
    return jnp.stack([failed_one, second], axis=1).astype(jnp.int32)


def strengthened(array, key, source, target, blocks, factor):
    def block_of(position):
        return (jnp.arange(array.shape[position]) // (array.shape[position] // blocks)).reshape((-1,) + (1,) * (array.ndim - 1 - position))

    near = jax.random.permutation(key, blocks)[block_of(target)]
    other_side = (block_of(target) + blocks // 2) % blocks
    return jnp.where((block_of(source) == near) | (block_of(source) == other_side), factor * array, array)


def level_of(stream_key, extent, cuts, low, largest):
    loudness = 1.0
    for position, blocks in cuts:
        steps = jax.random.uniform(jax.random.fold_in(jax.random.fold_in(stream_key, 6), position), (blocks,), jnp.float32, low / len(cuts), largest / len(cuts))
        loudness = loudness * jnp.repeat(jnp.exp(steps), extent[position] // blocks).reshape((-1,) + (1,) * (len(extent) - 1 - position))
    return loudness


def gaussian(stream_key, extent, spread, reach, cuts=(), held_as=jnp.bfloat16):
    drawn = spread * jax.random.normal(stream_key, extent, jnp.float32)
    if cuts:
        drawn = drawn * level_of(stream_key, extent, cuts, -0.22, 0.18)
    return jnp.clip(drawn, -reach, reach).astype(held_as)


def gaussian_with(key, shape, spread, limit, pieces, heavy, kind=jnp.bfloat16):
    values = spread * jax.random.normal(key, shape, jnp.float32)
    if pieces:
        values = values * level_of(key, shape, pieces, -0.22, 0.18)
    return jnp.clip(strengthened(values, jax.random.fold_in(key, 3), *heavy), -limit, limit).astype(kind)


def setup_inputs(seed: int = 0, part: int = 0) -> dict:
    key_of = jax.random.split(jax.random.key(seed), 6)
    part_keys = jax.random.split(jax.random.fold_in(key_of[5], part), 6)
    return {
        "state_slab": gaussian_with(part_keys[0], (N_REP, N_CODE, SLAB_ROW_COUNT, ENTRIES_PER_ROW), 1.0, 6.0, ((0, 4), (1, 4)), (1, 2, 4, 2.0), jnp.float32),
        "previous_slab": gaussian_with(part_keys[1], (N_REP, N_CODE, SLAB_ROW_COUNT, ENTRIES_PER_ROW), 1.0, 6.0, ((0, 4), (1, 4)), (1, 2, 4, 2.0), jnp.float32),
        "previous_parity": gaussian(part_keys[2], (N_REP, SLAB_ROW_COUNT, PARITY_SPANS * ENTRIES_PER_ROW), 1.0, 6.0, ((0, 4), (1, 4)), jnp.float32),
        "generator": draw_generator(jax.random.fold_in(key_of[5], 71), part),
        "failed_ids": draw_failed_ids(jax.random.fold_in(jax.random.fold_in(key_of[5], part), 71), part),
    }


def solve_weights(failed_columns):
    col_first = failed_columns[..., 0]
    col_second = failed_columns[..., 1]
    gram_first = jnp.sum(col_first * col_first, axis=-1, keepdims=True)
    gram_cross = jnp.sum(col_first * col_second, axis=-1, keepdims=True)
    gram_second = jnp.sum(col_second * col_second, axis=-1, keepdims=True)
    determinant = gram_first * gram_second - gram_cross * gram_cross
    solve_first = (gram_second * col_first - gram_cross * col_second) / determinant
    solve_second = (gram_first * col_second - gram_cross * col_first) / determinant
    return jnp.stack([solve_first, solve_second], axis=-2)


def reference(state_slab, previous_slab, previous_parity, generator, failed_ids):
    highest_setting = lax.Precision.HIGHEST
    new_parity = jnp.einsum('jc,rcxy->rxjy', generator, state_slab, precision=highest_setting)
    column_ids = jnp.arange(N_CODE, dtype=jnp.int32)
    keep_mask = ((column_ids[None, :] != failed_ids[:, 0:1]) & (column_ids[None, :] != failed_ids[:, 1:2])).astype(jnp.float32)
    masked_generator = generator[None, :, :] * keep_mask[:, None, :]
    surviving_members = jnp.einsum('oln,onkt->oklt', masked_generator, previous_slab, precision=highest_setting)
    failed_pick = (column_ids[None, None, :] == failed_ids[:, :, None]).astype(jnp.float32)
    failed_columns = jnp.einsum('jc,rkc->rjk', generator, failed_pick, precision=highest_setting)
    weights = solve_weights(failed_columns)
    leftover_term = previous_parity.reshape(N_REP, SLAB_ROW_COUNT, PARITY_SPANS, ENTRIES_PER_ROW) - surviving_members
    rebuilt = jnp.einsum('rkj,rxjy->rkxy', weights, leftover_term, precision=highest_setting)
    is_first = (column_ids[None, :] == failed_ids[:, 0:1])[:, :, None, None]
    is_second = (column_ids[None, :] == failed_ids[:, 1:2])[:, :, None, None]
    restored_state = jnp.where(is_first, rebuilt[:, 0:1], jnp.where(is_second, rebuilt[:, 1:2], previous_slab))
    return new_parity.reshape(N_REP, SLAB_ROW_COUNT, PARITY_SPANS * ENTRIES_PER_ROW), restored_state
```

```python
import jax
import jax.numpy as jnp
from jax import lax
from jax.sharding import PartitionSpec as P


def local(state_slab, previous_slab, previous_parity, generator, failed_ids):
    position = lax.axis_index("code")
    code_count = lax.axis_size("code")
    slab_rows, width = state_slab.shape[2:]
    spans = generator.shape[0]
    own_rows = slab_rows // code_count
    earlier = previous_slab[0, 0]
    blocks = (code_count, own_rows, width)
    earlier_rows = lax.all_to_all(earlier.reshape(blocks), "code", 0, 0, tiled=True)
    current_rows = lax.all_to_all(state_slab.reshape(blocks), "code", 0, 0, tiled=True)

    column_ids = jnp.arange(code_count, dtype=jnp.int32)
    failed_one = failed_ids[0, 0]
    failed_two = failed_ids[0, 1]
    alive = ((column_ids != failed_one) & (column_ids != failed_two)).astype(jnp.float32)
    col_first = jnp.sum(jnp.where(column_ids == failed_one, generator, 0.0), axis=1)
    col_second = jnp.sum(jnp.where(column_ids == failed_two, generator, 0.0), axis=1)
    gram_first = jnp.sum(col_first * col_first)
    gram_cross = jnp.sum(col_first * col_second)
    gram_second = jnp.sum(col_second * col_second)
    determinant = gram_first * gram_second - gram_cross * gram_cross
    solve_first = (gram_second * col_first - gram_cross * col_second) / determinant
    solve_second = (gram_first * col_second - gram_cross * col_first) / determinant

    parity = previous_parity[0]
    leftover = [
        parity[:, j * width : (j + 1) * width]
        - jnp.sum((generator[j] * alive)[:, None, None] * earlier_rows, axis=0)
        for j in range(spans)
    ]
    rebuilt_first = sum(solve_first[j] * leftover[j] for j in range(spans))
    rebuilt_second = sum(solve_second[j] * leftover[j] for j in range(spans))
    outgoing = jnp.where(
        (column_ids == failed_one)[:, None, None], rebuilt_first[None], rebuilt_second[None]
    )
    incoming = lax.all_to_all(outgoing, "code", 0, 0, tiled=True)
    lost = (position == failed_one) | (position == failed_two)
    restored_state = jnp.where(lost, incoming.reshape(slab_rows, width), earlier)
    new_parity = jnp.concatenate(
        [jnp.sum(generator[j][:, None, None] * current_rows, axis=0) for j in range(spans)], axis=1
    )
    return (new_parity[None], restored_state[None, None])


def solution(mesh):
    placed = (
        P(("grp", "rep"), "code", None, None),
        P(("grp", "rep"), "code", None, None),
        P(("grp", "rep"), "code", None),
        P(),
        P(("grp", "rep"), None),
    )
    return jax.shard_map(
        local,
        mesh=mesh,
        in_specs=placed,
        out_specs=(P(("grp", "rep"), "code", None), P(("grp", "rep"), "code", None, None)),
        check_vma=False,
    )
```

```python
import jax
import jax.numpy as jnp
from jax import lax
from jax.experimental import pallas as pl
from jax.experimental.pallas import tpu as pltpu
from jax.sharding import PartitionSpec as P

IN_VMEM = pl.BlockSpec(memory_space=pltpu.VMEM)
IN_SMEM = pl.BlockSpec(memory_space=pltpu.SMEM)


def cost(arrays, outs, flops):
    total = sum(x.size * x.dtype.itemsize for x in arrays) + sum(4 * o.size for o in outs)
    return pl.CostEstimate(flops=flops, bytes_accessed=total, transcendentals=0)


def plan_kernel(ids_ref, generator_ref, parity_ref, base_ref, solve_ref, generator_rows_ref):
    spans, members = generator_ref.shape
    width = base_ref.shape[2]
    first, second = ids_ref[0, 0], ids_ref[0, 1]
    col_first = [generator_ref[j, first] for j in range(spans)]
    col_second = [generator_ref[j, second] for j in range(spans)]
    gram_first = sum(x * x for x in col_first)
    gram_cross = sum(x * y for x, y in zip(col_first, col_second))
    gram_second = sum(y * y for y in col_second)
    determinant = gram_first * gram_second - gram_cross * gram_cross

    def spread(value):
        return jnp.full((1, width), value, jnp.float32)

    over = spread(determinant)
    weights = [
        [spread(gram_second * x - gram_cross * y) / over for x, y in zip(col_first, col_second)],
        [spread(gram_first * y - gram_cross * x) / over for x, y in zip(col_first, col_second)],
    ]
    for k in range(2):
        base_ref[k] = sum(
            weights[k][j] * parity_ref[:, j * width : (j + 1) * width] for j in range(spans)
        )
    for c in range(members):
        alive = jnp.logical_and(first != c, second != c)
        for k in range(2):
            row = sum(
                weights[k][j] * jnp.where(alive, generator_ref[j, c], 0.0) for j in range(spans)
            )
            solve_ref[k * members + c : k * members + c + 1, :] = row
        for j in range(spans):
            generator_rows_ref[j * members + c : j * members + c + 1, :] = spread(
                generator_ref[j, c]
            )


def rebuild_kernel(ids_ref, base_ref, solve_ref, rows_ref, out_ref):
    members = rows_ref.shape[0]
    first, second = ids_ref[0, 0], ids_ref[0, 1]
    for k, target in enumerate((first, second)):
        total = base_ref[k]
        for c in range(members):
            i = k * members + c
            total = total - solve_ref[i : i + 1, :] * rows_ref[c]
        out_ref[target] = total


def parity_kernel(generator_rows_ref, rows_ref, out_ref):
    members, _, width = rows_ref.shape
    for j in range(generator_rows_ref.shape[0] // members):
        total = None
        for c in range(members):
            i = j * members + c
            term = generator_rows_ref[i : i + 1, :] * rows_ref[c]
            total = term if total is None else total + term
        out_ref[:, j * width : (j + 1) * width] = total


def call(kernel, specs, outs, args, flops):
    return pl.pallas_call(
        kernel,
        in_specs=specs,
        out_specs=jax.tree.map(lambda _: IN_VMEM, outs),
        out_shape=outs,
        cost_estimate=cost(args, jax.tree.leaves(outs), flops),
    )(*args)


def local(state_slab, previous_slab, previous_parity, generator, failed_ids):
    position = lax.axis_index("code")
    members = lax.axis_size("code")
    slab_rows, width = state_slab.shape[2:]
    spans = generator.shape[0]
    own_rows = slab_rows // members
    earlier = previous_slab[0, 0]
    blocks = (members, own_rows, width)

    def floats(*shape):
        return jax.ShapeDtypeStruct(shape, jnp.float32)

    earlier_rows = lax.all_to_all(earlier.reshape(blocks), "code", 0, 0, tiled=True)
    current_rows = lax.all_to_all(state_slab.reshape(blocks), "code", 0, 0, tiled=True)
    base, solve_rows, generator_rows = call(
        plan_kernel,
        [IN_SMEM, IN_SMEM, IN_VMEM],
        (floats(2, own_rows, width), floats(2 * members, width), floats(spans * members, width)),
        (failed_ids, generator, previous_parity[0]),
        4 * spans * own_rows * width,
    )
    outgoing = call(
        rebuild_kernel,
        [IN_SMEM, IN_VMEM, IN_VMEM, IN_VMEM],
        floats(*blocks),
        (failed_ids, base, solve_rows, earlier_rows),
        4 * slab_rows * width,
    )
    incoming = lax.all_to_all(outgoing, "code", 0, 0, tiled=True)
    new_parity = call(
        parity_kernel,
        [IN_VMEM, IN_VMEM],
        floats(own_rows, spans * width),
        (generator_rows, current_rows),
        2 * spans * slab_rows * width,
    )
    lost = (position == failed_ids[0, 0]) | (position == failed_ids[0, 1])
    restored_state = jnp.where(lost, incoming.reshape(slab_rows, width), earlier)
    return (new_parity[None], restored_state[None, None])


def solution(mesh):
    placed = (
        P(("grp", "rep"), "code", None, None),
        P(("grp", "rep"), "code", None, None),
        P(("grp", "rep"), "code", None),
        P(),
        P(("grp", "rep"), None),
    )
    return jax.shard_map(
        local,
        mesh=mesh,
        in_specs=placed,
        out_specs=(P(("grp", "rep"), "code", None), P(("grp", "rep"), "code", None, None)),
        check_vma=False,
    )
```

```python
import jax
import jax.numpy as jnp
from jax import lax
from jax.experimental import pallas as pl
from jax.experimental.pallas import tpu as pltpu
from jax.sharding import PartitionSpec as P

IN_VMEM = pl.BlockSpec(memory_space=pltpu.VMEM)
IN_SMEM = pl.BlockSpec(memory_space=pltpu.SMEM)
ANYWHERE = pl.BlockSpec(memory_space=pl.ANY)

DIRECT_MEMBERS = 8


def wrap(index, members):
    return lax.rem(index + 2 * members, members)


def plan_kernel(ids_ref, generator_ref, parity_ref, base_ref, solve_ref, generator_rows_ref):
    spans, members = generator_ref.shape
    width = base_ref.shape[2]
    first, second = ids_ref[0, 0], ids_ref[0, 1]
    col_first = [generator_ref[j, first] for j in range(spans)]
    col_second = [generator_ref[j, second] for j in range(spans)]
    gram_first = sum(x * x for x in col_first)
    gram_cross = sum(x * y for x, y in zip(col_first, col_second))
    gram_second = sum(y * y for y in col_second)
    determinant = gram_first * gram_second - gram_cross * gram_cross

    def spread(value):
        return jnp.full((1, width), value, jnp.float32)

    over = spread(determinant)
    weights = [
        [spread(gram_second * x - gram_cross * y) / over for x, y in zip(col_first, col_second)],
        [spread(gram_first * y - gram_cross * x) / over for x, y in zip(col_first, col_second)],
    ]
    for k in range(2):
        base_ref[k] = sum(
            weights[k][j] * parity_ref[:, j * width : (j + 1) * width] for j in range(spans)
        )
    for c in range(members):
        alive = jnp.logical_and(first != c, second != c)
        for k in range(2):
            row = sum(
                weights[k][j] * jnp.where(alive, generator_ref[j, c], 0.0) for j in range(spans)
            )
            solve_ref[k * members + c : k * members + c + 1, :] = row
        for j in range(spans):
            generator_rows_ref[j * members + c : j * members + c + 1, :] = spread(
                generator_ref[j, c]
            )


def weigh(coefficient_ref, start, rows):
    total = None
    for member, block in rows:
        term = coefficient_ref[pl.ds(start + member, 1), :] * block
        total = term if total is None else total + term
    return total


def whole_rows(rows_ref):
    return [(c, rows_ref[c]) for c in range(rows_ref.shape[0])]


def shifted_rows(own_ref, refs):
    members = len(refs) + 1
    me = lax.axis_index("code")
    rows = [(me, own_ref[me])]
    return rows + [(wrap(me - s, members), ref[...]) for s, ref in enumerate(refs, 1)]


def rebuild_whole_kernel(ids_ref, base_ref, solve_ref, rows_ref, out_ref):
    rows = whole_rows(rows_ref)
    for k in range(2):
        out_ref[ids_ref[0, k]] = base_ref[k] - weigh(solve_ref, k * len(rows), rows)


def rebuild_shifted_kernel(ids_ref, base_ref, solve_ref, own_ref, *refs):
    members = own_ref.shape[0]
    rows = shifted_rows(own_ref, refs[: members - 1])
    outs = refs[members - 1 :]
    me = lax.axis_index("code")
    for k in range(2):
        rebuilt = base_ref[k] - weigh(solve_ref, k * members, rows)
        for s, out_ref in enumerate(outs):

            @pl.when(wrap(me + s, members) == ids_ref[0, k])
            def _():
                out_ref[...] = rebuilt


def parity_whole_kernel(generator_rows_ref, rows_ref, out_ref):
    parity_into(out_ref, generator_rows_ref, whole_rows(rows_ref))


def parity_shifted_kernel(generator_rows_ref, own_ref, *refs):
    parity_into(refs[-1], generator_rows_ref, shifted_rows(own_ref, refs[:-1]))


def parity_into(out_ref, generator_rows_ref, rows):
    width = generator_rows_ref.shape[1]
    for j in range(out_ref.shape[1] // width):
        out_ref[:, j * width : (j + 1) * width] = weigh(generator_rows_ref, j * len(rows), rows)


def cut_kernel(blocks_ref, *refs):
    outs, sems = refs[:-1], refs[-1]
    members = len(outs) + 1
    me = lax.axis_index("code")
    copies = [
        pltpu.make_async_copy(blocks_ref.at[wrap(me + s, members)], out, sems.at[s - 1])
        for s, out in enumerate(outs, 1)
    ]
    for copy in copies:
        copy.start()
    for copy in copies:
        copy.wait()


def restore_kernel(ids_ref, earlier_ref, *refs):
    pieces, out_ref = refs[:-1], refs[-1]
    members = len(pieces)
    me = lax.axis_index("code")
    lost = jnp.logical_or(me == ids_ref[0, 0], me == ids_ref[0, 1])

    @pl.when(lost)
    def _():
        for s, piece in enumerate(pieces):
            out_ref[wrap(me - s, members)] = piece[...]

    @pl.when(jnp.logical_not(lost))
    def _():
        out_ref[...] = earlier_ref[...]


def call(kernel, specs, outs, args, flops, **options):
    total = sum(x.size for x in args) + sum(o.size for o in jax.tree.leaves(outs))
    options.setdefault("out_specs", jax.tree.map(lambda _: IN_VMEM, outs))
    return pl.pallas_call(
        kernel,
        in_specs=specs,
        out_shape=outs,
        cost_estimate=pl.CostEstimate(flops=flops, bytes_accessed=4 * total, transcendentals=0),
        **options,
    )(*args)


def floats(*shape):
    return jax.ShapeDtypeStruct(shape, jnp.float32)


def send(pieces, members):
    return [
        lax.ppermute(piece, "code", [(d, (d + s) % members) for d in range(members)])
        for s, piece in enumerate(pieces, 1)
    ]


def cut(blocks):
    members = blocks.shape[0]
    return call(
        cut_kernel,
        [ANYWHERE],
        [floats(*blocks.shape[1:])] * (members - 1),
        (blocks,),
        0,
        out_specs=[ANYWHERE] * (members - 1),
        scratch_shapes=[pltpu.SemaphoreType.DMA((members - 1,))],
    )


def local(state_slab, previous_slab, previous_parity, generator, failed_ids):
    position = lax.axis_index("code")
    members = lax.axis_size("code")
    slab_rows, width = state_slab.shape[2:]
    spans = generator.shape[0]
    own_rows = slab_rows // members
    blocks = (members, own_rows, width)
    earlier = previous_slab.reshape(blocks)
    current = state_slab.reshape(blocks)
    direct = members <= DIRECT_MEMBERS

    if direct:
        earlier_rows = send(cut(earlier), members)
        current_rows = send(cut(current), members)
    else:
        earlier_rows = lax.all_to_all(earlier, "code", 0, 0, tiled=True)
        current_rows = lax.all_to_all(current, "code", 0, 0, tiled=True)
    base, solve_rows, generator_rows = call(
        plan_kernel,
        [IN_SMEM, IN_SMEM, IN_VMEM],
        (floats(2, own_rows, width), floats(2 * members, width), floats(spans * members, width)),
        (failed_ids, generator, previous_parity[0]),
        4 * spans * own_rows * width,
    )
    parity_shape = floats(own_rows, spans * width)
    rebuild_cost = 4 * slab_rows * width
    parity_cost = 2 * spans * slab_rows * width
    if direct:
        outgoing = call(
            rebuild_shifted_kernel,
            [IN_SMEM] + [IN_VMEM] * (members + 2),
            [floats(own_rows, width)] * members,
            (failed_ids, base, solve_rows, earlier, *earlier_rows),
            rebuild_cost,
        )
        incoming = send(outgoing[1:], members)
        new_parity = call(
            parity_shifted_kernel,
            [IN_VMEM] * (members + 1),
            parity_shape,
            (generator_rows, current, *current_rows),
            parity_cost,
        )
        restored_state = call(
            restore_kernel,
            [IN_SMEM] + [IN_VMEM] * (members + 1),
            floats(*blocks),
            (failed_ids, earlier, outgoing[0], *incoming),
            0,
        )
    else:
        outgoing = call(
            rebuild_whole_kernel,
            [IN_SMEM] + [IN_VMEM] * 3,
            floats(*blocks),
            (failed_ids, base, solve_rows, earlier_rows),
            rebuild_cost,
        )
        incoming = lax.all_to_all(outgoing, "code", 0, 0, tiled=True)
        new_parity = call(
            parity_whole_kernel,
            [IN_VMEM] * 2,
            parity_shape,
            (generator_rows, current_rows),
            parity_cost,
        )
        lost = (position == failed_ids[0, 0]) | (position == failed_ids[0, 1])
        restored_state = jnp.where(lost, incoming, earlier)
    return (new_parity[None], restored_state.reshape(state_slab.shape))


def solution(mesh):
    placed = (
        P(("grp", "rep"), "code", None, None),
        P(("grp", "rep"), "code", None, None),
        P(("grp", "rep"), "code", None),
        P(),
        P(("grp", "rep"), None),
    )
    return jax.shard_map(
        local,
        mesh=mesh,
        in_specs=placed,
        out_specs=(P(("grp", "rep"), "code", None), P(("grp", "rep"), "code", None, None)),
        check_vma=False,
    )
```

```python
import jax
import jax.numpy as jnp
from jax import lax
from jax.experimental import pallas as pl
from jax.experimental.pallas import tpu as pltpu
from jax.sharding import PartitionSpec as P

IN_VMEM = pl.BlockSpec(memory_space=pltpu.VMEM)
IN_SMEM = pl.BlockSpec(memory_space=pltpu.SMEM)
ANYWHERE = pl.BlockSpec(memory_space=pl.ANY)

DIRECT_MEMBERS = 8
KERNEL_VMEM = 8 * 2**20


def rounds_of(members):
    return range(members - 1, 0, -1)


def plan_kernel(ids_ref, generator_ref, parity_ref, base_ref, solve_ref, generator_rows_ref):
    spans, members = generator_ref.shape
    width = base_ref.shape[2]
    first, second = ids_ref[0, 0], ids_ref[0, 1]
    col_first = [generator_ref[j, first] for j in range(spans)]
    col_second = [generator_ref[j, second] for j in range(spans)]
    gram_first = sum(x * x for x in col_first)
    gram_cross = sum(x * y for x, y in zip(col_first, col_second))
    gram_second = sum(y * y for y in col_second)
    determinant = gram_first * gram_second - gram_cross * gram_cross

    def spread(value):
        return jnp.full((1, width), value, jnp.float32)

    over = spread(determinant)
    weights = [
        [spread(gram_second * x - gram_cross * y) / over for x, y in zip(col_first, col_second)],
        [spread(gram_first * y - gram_cross * x) / over for x, y in zip(col_first, col_second)],
    ]
    for k in range(2):
        base_ref[k] = sum(
            weights[k][j] * parity_ref[:, j * width : (j + 1) * width] for j in range(spans)
        )
    for c in range(members):
        alive = jnp.logical_and(first != c, second != c)
        for k in range(2):
            row = sum(
                weights[k][j] * jnp.where(alive, generator_ref[j, c], 0.0) for j in range(spans)
            )
            solve_ref[k * members + c : k * members + c + 1, :] = row
        for j in range(spans):
            generator_rows_ref[j * members + c : j * members + c + 1, :] = spread(
                generator_ref[j, c]
            )


def weigh(coefficient_ref, start, rows):
    total = None
    for member, block in rows:
        term = coefficient_ref[pl.ds(start + member, 1), :] * block
        total = term if total is None else total + term
    return total


def whole_rows(rows_ref):
    return [(c, rows_ref[c]) for c in range(rows_ref.shape[0])]


def paired_rows(own_ref, refs):
    me = lax.axis_index("code")
    rounds = rounds_of(own_ref.shape[0])
    return [(me, own_ref[me])] + [(me ^ r, ref[...]) for r, ref in zip(rounds, refs)]


def rebuild_whole_kernel(ids_ref, base_ref, solve_ref, rows_ref, out_ref):
    rows = whole_rows(rows_ref)
    for k in range(2):
        out_ref[ids_ref[0, k]] = base_ref[k] - weigh(solve_ref, k * len(rows), rows)


def rebuild_paired_kernel(ids_ref, base_ref, solve_ref, own_ref, *refs):
    members = own_ref.shape[0]
    rows = paired_rows(own_ref, refs[: members - 1])
    outs = refs[members - 1 :]
    me = lax.axis_index("code")
    for k in range(2):
        rebuilt = base_ref[k] - weigh(solve_ref, k * members, rows)
        for r, out_ref in zip((0, *rounds_of(members)), outs):

            @pl.when((me ^ r) == ids_ref[0, k])
            def _():
                out_ref[...] = rebuilt


def parity_kernel(generator_rows_ref, rows_ref, out_ref):
    rows = whole_rows(rows_ref)
    width = generator_rows_ref.shape[1]
    for j in range(out_ref.shape[1] // width):
        out_ref[:, j * width : (j + 1) * width] = weigh(generator_rows_ref, j * len(rows), rows)


def run_copies(pairs, sems):
    copies = [pltpu.make_async_copy(*pair, sems.at[i]) for i, pair in enumerate(pairs)]
    for copy in copies:
        copy.start()
    for copy in copies:
        copy.wait()


def cut_kernel(blocks_ref, *refs):
    outs, sems = refs[:-1], refs[-1]
    me = lax.axis_index("code")
    rounds = rounds_of(blocks_ref.shape[0])
    run_copies([(blocks_ref.at[me ^ r], out) for r, out in zip(rounds, outs)], sems)


def restore_kernel(ids_ref, earlier_ref, *refs):
    *pieces, out_ref, sems = refs
    members = len(pieces)
    me = lax.axis_index("code")
    lost = jnp.logical_or(me == ids_ref[0, 0], me == ids_ref[0, 1])

    @pl.when(lost)
    def _():
        places = [out_ref.at[me ^ r] for r in (0, *rounds_of(members))]
        run_copies(zip(pieces, places), sems)

    @pl.when(jnp.logical_not(lost))
    def _():
        run_copies([(earlier_ref, out_ref)], sems)


def call(kernel, specs, outs, args, flops, **options):
    total = sum(x.size for x in args) + sum(o.size for o in jax.tree.leaves(outs))
    options.setdefault("out_specs", jax.tree.map(lambda _: IN_VMEM, outs))
    return pl.pallas_call(
        kernel,
        in_specs=specs,
        out_shape=outs,
        compiler_params=pltpu.CompilerParams(vmem_limit_bytes=KERNEL_VMEM),
        cost_estimate=pl.CostEstimate(flops=flops, bytes_accessed=4 * total, transcendentals=0),
        **options,
    )(*args)


def floats(*shape):
    return jax.ShapeDtypeStruct(shape, jnp.float32)


def trade(pieces, members):
    return [
        lax.ppermute(piece, "code", [(d, d ^ r) for d in range(members)])
        for r, piece in zip(rounds_of(members), pieces)
    ]


def cut(blocks):
    others = blocks.shape[0] - 1
    return call(
        cut_kernel,
        [ANYWHERE],
        [floats(*blocks.shape[1:])] * others,
        (blocks,),
        0,
        scratch_shapes=[pltpu.SemaphoreType.DMA((others,))],
    )


def local(state_slab, previous_slab, previous_parity, generator, failed_ids):
    position = lax.axis_index("code")
    members = lax.axis_size("code")
    slab_rows, width = state_slab.shape[2:]
    spans = generator.shape[0]
    own_rows = slab_rows // members
    blocks = (members, own_rows, width)
    earlier = previous_slab.reshape(blocks)
    current = state_slab.reshape(blocks)
    direct = members <= DIRECT_MEMBERS and members & (members - 1) == 0

    if direct:
        earlier_rows = trade(cut(earlier), members)
    else:
        earlier_rows = lax.all_to_all(earlier, "code", 0, 0, tiled=True)
    current_rows = lax.all_to_all(current, "code", 0, 0, tiled=True)
    base, solve_rows, generator_rows = call(
        plan_kernel,
        [IN_SMEM, IN_SMEM, IN_VMEM],
        (floats(2, own_rows, width), floats(2 * members, width), floats(spans * members, width)),
        (failed_ids, generator, previous_parity[0]),
        4 * spans * own_rows * width,
    )
    rebuild_cost = 4 * slab_rows * width
    if direct:
        outgoing = call(
            rebuild_paired_kernel,
            [IN_SMEM] + [IN_VMEM] * (members + 2),
            [floats(own_rows, width)] * members,
            (failed_ids, base, solve_rows, earlier, *earlier_rows),
            rebuild_cost,
        )
        restored_state = call(
            restore_kernel,
            [IN_SMEM] + [IN_VMEM] * (members + 1),
            floats(*blocks),
            (failed_ids, earlier, outgoing[0], *trade(outgoing[1:], members)),
            0,
            out_specs=ANYWHERE,
            scratch_shapes=[pltpu.SemaphoreType.DMA((members,))],
        )
    else:
        outgoing = call(
            rebuild_whole_kernel,
            [IN_SMEM] + [IN_VMEM] * 3,
            floats(*blocks),
            (failed_ids, base, solve_rows, earlier_rows),
            rebuild_cost,
        )
        incoming = lax.all_to_all(outgoing, "code", 0, 0, tiled=True)
        lost = (position == failed_ids[0, 0]) | (position == failed_ids[0, 1])
        restored_state = jnp.where(lost, incoming, earlier)
    new_parity = call(
        parity_kernel,
        [IN_VMEM] * 2,
        floats(own_rows, spans * width),
        (generator_rows, current_rows),
        2 * spans * slab_rows * width,
    )
    return (new_parity[None], restored_state.reshape(state_slab.shape))


def solution(mesh):
    placed = (
        P(("grp", "rep"), "code", None, None),
        P(("grp", "rep"), "code", None, None),
        P(("grp", "rep"), "code", None),
        P(),
        P(("grp", "rep"), None),
    )
    return jax.shard_map(
        local,
        mesh=mesh,
        in_specs=placed,
        out_specs=(P(("grp", "rep"), "code", None), P(("grp", "rep"), "code", None, None)),
        check_vma=False,
    )
```

```python
import functools

import jax
import jax.numpy as jnp
from jax import lax
from jax.experimental import pallas as pl
from jax.experimental.pallas import tpu as pltpu
from jax.sharding import PartitionSpec as P

IN_VMEM = pl.BlockSpec(memory_space=pltpu.VMEM)
IN_SMEM = pl.BlockSpec(memory_space=pltpu.SMEM)
ANYWHERE = pl.BlockSpec(memory_space=pl.ANY)

DIRECT_MEMBERS = 8
KERNEL_VMEM = 8 * 2**20


def rounds_of(members):
    return range(members - 1, 0, -1)


def order_of(members, direct):
    if not direct:
        return list(range(members))
    me = lax.axis_index("code")
    return [me ^ r for r in (0, *rounds_of(members))]


def plan_kernel(direct, ids_ref, generator_ref, parity_ref, base_ref, table_ref):
    spans, members = generator_ref.shape
    width = base_ref.shape[2]
    first, second = ids_ref[0, 0], ids_ref[0, 1]
    col_first = [generator_ref[j, first] for j in range(spans)]
    col_second = [generator_ref[j, second] for j in range(spans)]
    gram_first = sum(x * x for x in col_first)
    gram_cross = sum(x * y for x, y in zip(col_first, col_second))
    gram_second = sum(y * y for y in col_second)
    determinant = gram_first * gram_second - gram_cross * gram_cross

    def spread(value):
        return jnp.full((1, width), value, jnp.float32)

    def put(row, value):
        table_ref[row : row + 1, :] = value

    over = spread(determinant)
    weights = [
        [spread(gram_second * x - gram_cross * y) / over for x, y in zip(col_first, col_second)],
        [spread(gram_first * y - gram_cross * x) / over for x, y in zip(col_first, col_second)],
    ]
    for k in range(2):
        base_ref[k] = sum(
            weights[k][j] * parity_ref[:, j * width : (j + 1) * width] for j in range(spans)
        )
    for i, c in enumerate(order_of(members, direct)):
        column = [generator_ref[j, c] for j in range(spans)]
        alive = jnp.logical_and(first != c, second != c)
        for k in range(2):
            put(
                k * members + i,
                sum(weights[k][j] * jnp.where(alive, column[j], 0.0) for j in range(spans)),
            )
        for j in range(spans):
            put((2 + j) * members + i, spread(column[j]))
        put((2 + spans) * members + i, spread(jnp.where(first == c, 1.0, 0.0)))
    me = lax.axis_index("code")
    lost = jnp.logical_or(first == me, second == me)
    put((3 + spans) * members, spread(jnp.where(lost, 1.0, 0.0)))


def weigh(table_ref, start, rows):
    total = None
    for i, block in enumerate(rows):
        term = table_ref[start + i : start + i + 1, :] * block
        total = term if total is None else total + term
    return total


def rebuilt_for(base_ref, table_ref, rows):
    members = len(rows)
    rebuilt = [base_ref[k] - weigh(table_ref, k * members, rows) for k in range(2)]
    picks = table_ref.shape[0] - 1 - members
    return [
        jnp.where(table_ref[picks + i : picks + i + 1, :] > 0.5, *rebuilt) for i in range(members)
    ]


def rebuild_whole_kernel(base_ref, table_ref, rows_ref, out_ref):
    rows = [rows_ref[c] for c in range(rows_ref.shape[0])]
    for c, block in enumerate(rebuilt_for(base_ref, table_ref, rows)):
        out_ref[c] = block


def parity_whole_kernel(table_ref, rows_ref, out_ref):
    parity_into(out_ref, table_ref, [rows_ref[c] for c in range(rows_ref.shape[0])])


def parity_into(out_ref, table_ref, rows):
    members, width = len(rows), table_ref.shape[1]
    for j in range(out_ref.shape[1] // width):
        out_ref[:, j * width : (j + 1) * width] = weigh(table_ref, (2 + j) * members, rows)


def cut_kernel(rounds, blocks_ref, *refs):
    outs, sems = refs[-1 - len(rounds) : -1], refs[-1]
    me = lax.axis_index("code")
    copies = [
        pltpu.make_async_copy(blocks_ref.at[me ^ r], out, sems.at[i])
        for i, (r, out) in enumerate(zip(rounds, outs))
    ]
    for copy in copies:
        copy.start()
    for copy in copies:
        copy.wait()


def rebuild_paired_kernel(base_ref, table_ref, *refs):
    rows, outs = refs[: len(refs) // 2], refs[len(refs) // 2 :]
    for out_ref, block in zip(outs, rebuilt_for(base_ref, table_ref, [r[...] for r in rows])):
        out_ref[...] = block


def parity_paired_kernel(table_ref, *refs):
    rows, out_ref, done_ref = refs[:-2], refs[-2], refs[-1]
    parity_into(out_ref, table_ref, [r[...] for r in rows])
    done_ref[...] = jnp.zeros(done_ref.shape, done_ref.dtype)


def restore_kernel(table_ref, earlier_ref, held_back_by, *refs):
    pieces, out_ref = refs[:-1], refs[-1]
    members = len(pieces)
    last = table_ref.shape[0] - 1
    lost = table_ref[last : last + 1, :] > 0.5
    for c, piece in zip(order_of(members, True), pieces):
        out_ref[c] = jnp.where(lost, piece[...], earlier_ref[c])


def call(kernel, specs, outs, args, flops, **options):
    total = sum(x.size for x in args) + sum(o.size for o in jax.tree.leaves(outs))
    return pl.pallas_call(
        kernel,
        in_specs=specs,
        out_specs=jax.tree.map(lambda _: IN_VMEM, outs),
        out_shape=outs,
        compiler_params=pltpu.CompilerParams(vmem_limit_bytes=KERNEL_VMEM),
        cost_estimate=pl.CostEstimate(flops=flops, bytes_accessed=4 * total, transcendentals=0),
        **options,
    )(*args)


def floats(*shape):
    return jax.ShapeDtypeStruct(shape, jnp.float32)


def trade(pieces, rounds, members):
    return [
        lax.ppermute(piece, "code", [(d, d ^ r) for d in range(members)])
        for r, piece in zip(rounds, pieces)
    ]


def cut(blocks, rounds, *held_back_by):
    return call(
        functools.partial(cut_kernel, rounds),
        [ANYWHERE] * (1 + len(held_back_by)),
        [floats(*blocks.shape[1:])] * len(rounds),
        (blocks, *held_back_by),
        0,
        scratch_shapes=[pltpu.SemaphoreType.DMA((len(rounds),))],
    )


def local(state_slab, previous_slab, previous_parity, generator, failed_ids):
    position = lax.axis_index("code")
    members = lax.axis_size("code")
    slab_rows, width = state_slab.shape[2:]
    spans = generator.shape[0]
    own_rows = slab_rows // members
    blocks = (members, own_rows, width)
    earlier = previous_slab.reshape(blocks)
    current = state_slab.reshape(blocks)
    direct = 4 <= members <= DIRECT_MEMBERS and members & (members - 1) == 0

    base, table = call(
        functools.partial(plan_kernel, direct),
        [IN_SMEM, IN_SMEM, IN_VMEM],
        (floats(2, own_rows, width), floats((3 + spans) * members + 1, width)),
        (failed_ids, generator, previous_parity[0]),
        4 * spans * own_rows * width,
    )
    parity_shape = floats(own_rows, spans * width)
    rebuild_cost = 4 * slab_rows * width
    parity_cost = 2 * spans * slab_rows * width
    if direct:
        rounds = list(rounds_of(members))
        block = floats(own_rows, width)
        own_earlier, *cut_earlier = cut(earlier, [0] + rounds)
        earlier_rows = trade(cut_earlier, rounds, members)
        own_current, *cut_current = cut(current, [0] + rounds, earlier_rows[0])
        outgoing = call(
            rebuild_paired_kernel,
            [IN_VMEM] * (members + 2),
            [block] * members,
            (base, table, own_earlier, *earlier_rows),
            rebuild_cost,
        )
        incoming = trade(outgoing[1:], rounds, members)
        current_rows = [own_current, *trade(cut_current, rounds, members)]
        new_parity, parity_done = call(
            parity_paired_kernel,
            [IN_VMEM] * (members + 1),
            (parity_shape, floats(8, 128)),
            (table, *current_rows),
            parity_cost,
        )
        restored_state = call(
            restore_kernel,
            [IN_VMEM, IN_VMEM, ANYWHERE] + [IN_VMEM] * members,
            floats(*blocks),
            (table, earlier, parity_done, outgoing[0], *incoming),
            0,
        )
    else:
        earlier_rows = lax.all_to_all(earlier, "code", 0, 0, tiled=True)
        current_rows = lax.all_to_all(current, "code", 0, 0, tiled=True)
        outgoing = call(
            rebuild_whole_kernel,
            [IN_VMEM] * 3,
            floats(*blocks),
            (base, table, earlier_rows),
            rebuild_cost,
        )
        incoming = lax.all_to_all(outgoing, "code", 0, 0, tiled=True)
        lost = (position == failed_ids[0, 0]) | (position == failed_ids[0, 1])
        restored_state = jnp.where(lost, incoming, earlier)
        new_parity = call(
            parity_whole_kernel,
            [IN_VMEM] * 2,
            parity_shape,
            (table, current_rows),
            parity_cost,
        )
    return (new_parity[None], restored_state.reshape(state_slab.shape))


def solution(mesh):
    placed = (
        P(("grp", "rep"), "code", None, None),
        P(("grp", "rep"), "code", None, None),
        P(("grp", "rep"), "code", None),
        P(),
        P(("grp", "rep"), None),
    )
    return jax.shard_map(
        local,
        mesh=mesh,
        in_specs=placed,
        out_specs=(P(("grp", "rep"), "code", None), P(("grp", "rep"), "code", None, None)),
        check_vma=False,
    )
```

```python
import functools

import jax
import jax.numpy as jnp
from jax import lax
from jax.experimental import pallas as pl
from jax.experimental.pallas import tpu as pltpu
from jax.sharding import PartitionSpec as P

IN_VMEM = pl.BlockSpec(memory_space=pltpu.VMEM)
IN_SMEM = pl.BlockSpec(memory_space=pltpu.SMEM)
ANYWHERE = pl.BlockSpec(memory_space=pl.ANY)

DIRECT_MEMBERS = 8
KERNEL_VMEM = 8 * 2**20


def rounds_of(members):
    return range(members - 1, 0, -1)


def order_of(members, direct):
    if not direct:
        return list(range(members))
    me = lax.axis_index("code")
    return [me ^ r for r in (0, *rounds_of(members))]


def plan_kernel(direct, ids_ref, generator_ref, parity_ref, base_ref, table_ref):
    spans, members = generator_ref.shape
    width = base_ref.shape[2]
    first, second = ids_ref[0, 0], ids_ref[0, 1]
    col_first = [generator_ref[j, first] for j in range(spans)]
    col_second = [generator_ref[j, second] for j in range(spans)]
    gram_first = sum(x * x for x in col_first)
    gram_cross = sum(x * y for x, y in zip(col_first, col_second))
    gram_second = sum(y * y for y in col_second)
    determinant = gram_first * gram_second - gram_cross * gram_cross

    def spread(value):
        return jnp.full((1, width), value, jnp.float32)

    def put(row, value):
        table_ref[row : row + 1, :] = value

    over = spread(determinant)
    weights = [
        [spread(gram_second * x - gram_cross * y) / over for x, y in zip(col_first, col_second)],
        [spread(gram_first * y - gram_cross * x) / over for x, y in zip(col_first, col_second)],
    ]
    for k in range(2):
        base_ref[k] = sum(
            weights[k][j] * parity_ref[:, j * width : (j + 1) * width] for j in range(spans)
        )
    for i, c in enumerate(order_of(members, direct)):
        column = [generator_ref[j, c] for j in range(spans)]
        alive = jnp.logical_and(first != c, second != c)
        for k in range(2):
            put(
                k * members + i,
                sum(weights[k][j] * jnp.where(alive, column[j], 0.0) for j in range(spans)),
            )
        for j in range(spans):
            put((2 + j) * members + i, spread(column[j]))
        put((2 + spans) * members + i, spread(jnp.where(first == c, 1.0, 0.0)))
    me = lax.axis_index("code")
    lost = jnp.logical_or(first == me, second == me)
    put((3 + spans) * members, spread(jnp.where(lost, 1.0, 0.0)))


def weigh(table_ref, start, rows):
    total = None
    for i, block in enumerate(rows):
        term = table_ref[start + i : start + i + 1, :] * block
        total = term if total is None else total + term
    return total


def rebuilt_for(base_ref, table_ref, rows):
    members = len(rows)
    rebuilt = [base_ref[k] - weigh(table_ref, k * members, rows) for k in range(2)]
    picks = table_ref.shape[0] - 1 - members
    return [
        jnp.where(table_ref[picks + i : picks + i + 1, :] > 0.5, *rebuilt) for i in range(members)
    ]


def rebuild_whole_kernel(base_ref, table_ref, rows_ref, out_ref):
    rows = [rows_ref[c] for c in range(rows_ref.shape[0])]
    for c, block in enumerate(rebuilt_for(base_ref, table_ref, rows)):
        out_ref[c] = block


def parity_whole_kernel(table_ref, rows_ref, out_ref):
    parity_into(out_ref, table_ref, [rows_ref[c] for c in range(rows_ref.shape[0])])


def parity_into(out_ref, table_ref, rows):
    members, width = len(rows), table_ref.shape[1]
    for j in range(out_ref.shape[1] // width):
        out_ref[:, j * width : (j + 1) * width] = weigh(table_ref, (2 + j) * members, rows)


def cut_kernel(rounds, blocks_ref, *refs):
    outs, sems = refs[-1 - len(rounds) : -1], refs[-1]
    me = lax.axis_index("code")
    copies = [
        pltpu.make_async_copy(blocks_ref.at[me ^ r], out, sems.at[i])
        for i, (r, out) in enumerate(zip(rounds, outs))
    ]
    for copy in copies:
        copy.start()
    for copy in copies:
        copy.wait()


def rebuild_paired_kernel(base_ref, table_ref, *refs):
    rows, outs = refs[: len(refs) // 2], refs[len(refs) // 2 :]
    for out_ref, block in zip(outs, rebuilt_for(base_ref, table_ref, [r[...] for r in rows])):
        out_ref[...] = block


def parity_paired_kernel(table_ref, *refs):
    rows, out_ref, done_ref = refs[:-2], refs[-2], refs[-1]
    parity_into(out_ref, table_ref, [r[...] for r in rows])
    done_ref[...] = jnp.zeros(done_ref.shape, done_ref.dtype)


def restore_kernel(table_ref, earlier_ref, held_back_by, *refs):
    pieces, out_ref = refs[:-1], refs[-1]
    members = len(pieces)
    last = table_ref.shape[0] - 1
    lost = table_ref[last : last + 1, :] > 0.5
    for c, piece in zip(order_of(members, True), pieces):
        out_ref[c] = jnp.where(lost, piece[...], earlier_ref[c])


def call(kernel, specs, outs, args, flops, **options):
    total = sum(x.size for x in args) + sum(o.size for o in jax.tree.leaves(outs))
    return pl.pallas_call(
        kernel,
        in_specs=specs,
        out_specs=jax.tree.map(lambda _: IN_VMEM, outs),
        out_shape=outs,
        compiler_params=pltpu.CompilerParams(vmem_limit_bytes=KERNEL_VMEM),
        cost_estimate=pl.CostEstimate(flops=flops, bytes_accessed=4 * total, transcendentals=0),
        **options,
    )(*args)


def floats(*shape):
    return jax.ShapeDtypeStruct(shape, jnp.float32)


def trade(pieces, rounds, members):
    return [
        lax.ppermute(piece, "code", [(d, d ^ r) for d in range(members)])
        for r, piece in zip(rounds, pieces)
    ]


def cut(blocks, rounds, *held_back_by):
    return call(
        functools.partial(cut_kernel, rounds),
        [ANYWHERE] * (1 + len(held_back_by)),
        [floats(*blocks.shape[1:])] * len(rounds),
        (pltpu.with_memory_space_constraint(blocks, pltpu.HBM), *held_back_by),
        0,
        scratch_shapes=[pltpu.SemaphoreType.DMA((len(rounds),))],
    )


def local(state_slab, previous_slab, previous_parity, generator, failed_ids):
    position = lax.axis_index("code")
    members = lax.axis_size("code")
    slab_rows, width = state_slab.shape[2:]
    spans = generator.shape[0]
    own_rows = slab_rows // members
    blocks = (members, own_rows, width)
    earlier = previous_slab.reshape(blocks)
    current = state_slab.reshape(blocks)
    direct = 4 <= members <= DIRECT_MEMBERS and members & (members - 1) == 0

    base, table = call(
        functools.partial(plan_kernel, direct),
        [IN_SMEM, IN_SMEM, IN_VMEM],
        (floats(2, own_rows, width), floats((3 + spans) * members + 1, width)),
        (failed_ids, generator, previous_parity[0]),
        4 * spans * own_rows * width,
    )
    parity_shape = floats(own_rows, spans * width)
    rebuild_cost = 4 * slab_rows * width
    parity_cost = 2 * spans * slab_rows * width
    if direct:
        rounds = list(rounds_of(members))
        block = floats(own_rows, width)
        own_earlier, *cut_earlier = cut(earlier, [0] + rounds)
        earlier_rows = trade(cut_earlier, rounds, members)
        own_current, *cut_current = cut(current, [0] + rounds, own_earlier)
        outgoing = call(
            rebuild_paired_kernel,
            [IN_VMEM] * (members + 2),
            [block] * members,
            (base, table, own_earlier, *earlier_rows),
            rebuild_cost,
        )
        incoming = trade(outgoing[1:], rounds, members)
        current_rows = [own_current, *trade(cut_current, rounds, members)]
        new_parity, parity_done = call(
            parity_paired_kernel,
            [IN_VMEM] * (members + 1),
            (parity_shape, floats(8, 128)),
            (table, *current_rows),
            parity_cost,
        )
        restored_state = call(
            restore_kernel,
            [IN_VMEM, IN_VMEM, ANYWHERE] + [IN_VMEM] * members,
            floats(*blocks),
            (table, earlier, parity_done, outgoing[0], *incoming),
            0,
        )
    else:
        earlier_rows = lax.all_to_all(earlier, "code", 0, 0, tiled=True)
        current_rows = lax.all_to_all(current, "code", 0, 0, tiled=True)
        outgoing = call(
            rebuild_whole_kernel,
            [IN_VMEM] * 3,
            floats(*blocks),
            (base, table, earlier_rows),
            rebuild_cost,
        )
        incoming = lax.all_to_all(outgoing, "code", 0, 0, tiled=True)
        lost = (position == failed_ids[0, 0]) | (position == failed_ids[0, 1])
        restored_state = jnp.where(lost, incoming, earlier)
        new_parity = call(
            parity_whole_kernel,
            [IN_VMEM] * 2,
            parity_shape,
            (table, current_rows),
            parity_cost,
        )
    return (new_parity[None], restored_state.reshape(state_slab.shape))


def solution(mesh):
    placed = (
        P(("grp", "rep"), "code", None, None),
        P(("grp", "rep"), "code", None, None),
        P(("grp", "rep"), "code", None),
        P(),
        P(("grp", "rep"), None),
    )
    return jax.shard_map(
        local,
        mesh=mesh,
        in_specs=placed,
        out_specs=(P(("grp", "rep"), "code", None), P(("grp", "rep"), "code", None, None)),
        check_vma=False,
    )
```

```python
import functools

import jax
import jax.numpy as jnp
from jax import lax
from jax.experimental import pallas as pl
from jax.experimental.pallas import tpu as pltpu
from jax.sharding import PartitionSpec as P

IN_VMEM = pl.BlockSpec(memory_space=pltpu.VMEM)
IN_SMEM = pl.BlockSpec(memory_space=pltpu.SMEM)
ANYWHERE = pl.BlockSpec(memory_space=pl.ANY)

DIRECT_MEMBERS = 8
KERNEL_VMEM = 8 * 2**20


def rounds_of(members):
    return range(members - 1, 0, -1)


def order_of(members, direct):
    if not direct:
        return list(range(members))
    me = lax.axis_index("code")
    return [me ^ r for r in (0, *rounds_of(members))]


def plan_kernel(direct, ids_ref, generator_ref, parity_ref, base_ref, table_ref):
    spans, members = generator_ref.shape
    width = base_ref.shape[2]
    first, second = ids_ref[0, 0], ids_ref[0, 1]
    col_first = [generator_ref[j, first] for j in range(spans)]
    col_second = [generator_ref[j, second] for j in range(spans)]
    gram_first = sum(x * x for x in col_first)
    gram_cross = sum(x * y for x, y in zip(col_first, col_second))
    gram_second = sum(y * y for y in col_second)
    determinant = gram_first * gram_second - gram_cross * gram_cross

    def spread(value):
        return jnp.full((1, width), value, jnp.float32)

    def put(row, value):
        table_ref[row : row + 1, :] = value

    over = spread(determinant)
    weights = [
        [spread(gram_second * x - gram_cross * y) / over for x, y in zip(col_first, col_second)],
        [spread(gram_first * y - gram_cross * x) / over for x, y in zip(col_first, col_second)],
    ]
    for k in range(2):
        base_ref[k] = sum(
            weights[k][j] * parity_ref[:, j * width : (j + 1) * width] for j in range(spans)
        )
    for i, c in enumerate(order_of(members, direct)):
        column = [generator_ref[j, c] for j in range(spans)]
        alive = jnp.logical_and(first != c, second != c)
        for k in range(2):
            put(
                k * members + i,
                sum(weights[k][j] * jnp.where(alive, column[j], 0.0) for j in range(spans)),
            )
        for j in range(spans):
            put((2 + j) * members + i, spread(column[j]))
        put((2 + spans) * members + i, spread(jnp.where(first == c, 1.0, 0.0)))
    me = lax.axis_index("code")
    lost = jnp.logical_or(first == me, second == me)
    put((3 + spans) * members, spread(jnp.where(lost, 1.0, 0.0)))


def weigh(table_ref, start, rows):
    total = None
    for i, block in enumerate(rows):
        term = table_ref[start + i : start + i + 1, :] * block
        total = term if total is None else total + term
    return total


def rebuilt_for(base_ref, table_ref, rows):
    members = len(rows)
    rebuilt = [base_ref[k] - weigh(table_ref, k * members, rows) for k in range(2)]
    picks = table_ref.shape[0] - 1 - members
    return [
        jnp.where(table_ref[picks + i : picks + i + 1, :] > 0.5, *rebuilt) for i in range(members)
    ]


def rebuild_whole_kernel(base_ref, table_ref, rows_ref, out_ref):
    rows = [rows_ref[c] for c in range(rows_ref.shape[0])]
    for c, block in enumerate(rebuilt_for(base_ref, table_ref, rows)):
        out_ref[c] = block


def parity_whole_kernel(table_ref, rows_ref, out_ref):
    parity_into(out_ref, table_ref, [rows_ref[c] for c in range(rows_ref.shape[0])])


def parity_into(out_ref, table_ref, rows):
    members, width = len(rows), table_ref.shape[1]
    for j in range(out_ref.shape[1] // width):
        out_ref[:, j * width : (j + 1) * width] = weigh(table_ref, (2 + j) * members, rows)


def cut_kernel(rounds, blocks_ref, *refs):
    outs, sems = refs[-1 - len(rounds) : -1], refs[-1]
    me = lax.axis_index("code")
    copies = [
        pltpu.make_async_copy(blocks_ref.at[me ^ r], out, sems.at[i])
        for i, (r, out) in enumerate(zip(rounds, outs))
    ]
    for copy in copies:
        copy.start()
    for copy in copies:
        copy.wait()


def rebuild_paired_kernel(base_ref, table_ref, *refs):
    rows, outs = refs[: len(refs) // 2], refs[len(refs) // 2 :]
    for out_ref, block in zip(outs, rebuilt_for(base_ref, table_ref, [r[...] for r in rows])):
        out_ref[...] = block


def parity_paired_kernel(table_ref, *refs):
    rows, out_ref, done_ref = refs[:-2], refs[-2], refs[-1]
    parity_into(out_ref, table_ref, [r[...] for r in rows])
    done_ref[...] = jnp.zeros(done_ref.shape, done_ref.dtype)


def restore_kernel(rounds, table_ref, *refs):
    count = len(rounds)
    arrived, own = refs[:count], refs[count : 2 * count]
    out_ref, stage_ref, sems = refs[-3:]
    me = lax.axis_index("code")
    last = table_ref.shape[0] - 1
    lost = table_ref[last : last + 1, :] > 0.5
    copies = []
    for i, r in enumerate(rounds):
        stage_ref[i] = jnp.where(lost, arrived[i][...], own[i][...])
        copies.append(
            pltpu.make_async_copy(stage_ref.at[i], out_ref.at[me ^ r], sems.at[i])
        )
        copies[-1].start()
    for copy in copies:
        copy.wait()


def call(kernel, specs, outs, args, flops, **options):
    total = sum(x.size for x in args) + sum(o.size for o in jax.tree.leaves(outs))
    options.setdefault("out_specs", jax.tree.map(lambda _: IN_VMEM, outs))
    return pl.pallas_call(
        kernel,
        in_specs=specs,
        out_shape=outs,
        compiler_params=pltpu.CompilerParams(vmem_limit_bytes=KERNEL_VMEM),
        cost_estimate=pl.CostEstimate(flops=flops, bytes_accessed=4 * total, transcendentals=0),
        **options,
    )(*args)


def floats(*shape):
    return jax.ShapeDtypeStruct(shape, jnp.float32)


def trade(pieces, rounds, members):
    return [
        lax.ppermute(piece, "code", [(d, d ^ r) for d in range(members)])
        for r, piece in zip(rounds, pieces)
    ]


def cut(blocks, rounds, *held_back_by):
    return call(
        functools.partial(cut_kernel, rounds),
        [ANYWHERE] * (1 + len(held_back_by)),
        [floats(*blocks.shape[1:])] * len(rounds),
        (blocks, *held_back_by),
        0,
        scratch_shapes=[pltpu.SemaphoreType.DMA((len(rounds),))],
    )


def restore(members, table, rounds, arrived, own, others=(), held_back_by=()):
    count = len(rounds)
    own_rows, width = own[0].shape
    extra = [*others, *held_back_by]
    return call(
        functools.partial(restore_kernel, rounds),
        [IN_VMEM] * (1 + 2 * count) + [ANYWHERE] * len(extra),
        floats(members, own_rows, width),
        (table, *arrived, *own, *extra),
        0,
        out_specs=ANYWHERE,
        scratch_shapes=[
            pltpu.VMEM((count, own_rows, width), jnp.float32),
            pltpu.SemaphoreType.DMA((count,)),
        ],
        input_output_aliases={1 + 2 * count: 0} if others else {},
    )


def local(state_slab, previous_slab, previous_parity, generator, failed_ids):
    position = lax.axis_index("code")
    members = lax.axis_size("code")
    slab_rows, width = state_slab.shape[2:]
    spans = generator.shape[0]
    own_rows = slab_rows // members
    blocks = (members, own_rows, width)
    earlier = previous_slab.reshape(blocks)
    current = state_slab.reshape(blocks)
    direct = 4 <= members <= DIRECT_MEMBERS and members & (members - 1) == 0

    base, table = call(
        functools.partial(plan_kernel, direct),
        [IN_SMEM, IN_SMEM, IN_VMEM],
        (floats(2, own_rows, width), floats((3 + spans) * members + 1, width)),
        (failed_ids, generator, previous_parity[0]),
        4 * spans * own_rows * width,
    )
    parity_shape = floats(own_rows, spans * width)
    rebuild_cost = 4 * slab_rows * width
    parity_cost = 2 * spans * slab_rows * width
    if direct:
        rounds = list(rounds_of(members))
        block = floats(own_rows, width)
        lead, rest = rounds[:1], rounds[1:]
        cut_lead = cut(pltpu.with_memory_space_constraint(earlier, pltpu.HBM), lead)
        own_earlier, *cut_rest = cut(earlier, [0] + rest, *cut_lead)
        cut_earlier = [*cut_lead, *cut_rest]
        earlier_rows = trade(cut_earlier, rounds, members)
        own_current, *cut_current = cut(current, [0] + rounds, own_earlier)
        outgoing = call(
            rebuild_paired_kernel,
            [IN_VMEM] * (members + 2),
            [block] * members,
            (base, table, own_earlier, *earlier_rows),
            rebuild_cost,
        )
        incoming = trade(outgoing[1:], rounds, members)
        current_rows = [own_current, *trade(cut_current, rounds, members)]
        new_parity, parity_done = call(
            parity_paired_kernel,
            [IN_VMEM] * (members + 1),
            (parity_shape, floats(8, 128)),
            (table, *current_rows),
            parity_cost,
        )
        slow = rounds.index(members // 2) + 1
        arrived, own = [outgoing[0], *incoming], [own_earlier, *cut_earlier]
        all_rounds = [0] + rounds
        quick = [i for i in range(members) if i != slow]
        first_blocks = restore(
            members,
            table,
            [all_rounds[i] for i in quick],
            [arrived[i] for i in quick],
            [own[i] for i in quick],
            held_back_by=[parity_done],
        )
        restored_state = restore(
            members, table, [all_rounds[slow]], [arrived[slow]], [own[slow]], [first_blocks]
        )
    else:
        earlier_rows = lax.all_to_all(earlier, "code", 0, 0, tiled=True)
        current_rows = lax.all_to_all(current, "code", 0, 0, tiled=True)
        outgoing = call(
            rebuild_whole_kernel,
            [IN_VMEM] * 3,
            floats(*blocks),
            (base, table, earlier_rows),
            rebuild_cost,
        )
        incoming = lax.all_to_all(outgoing, "code", 0, 0, tiled=True)
        lost = (position == failed_ids[0, 0]) | (position == failed_ids[0, 1])
        restored_state = jnp.where(lost, incoming, earlier)
        new_parity = call(
            parity_whole_kernel,
            [IN_VMEM] * 2,
            parity_shape,
            (table, current_rows),
            parity_cost,
        )
    return (new_parity[None], restored_state.reshape(state_slab.shape))


def solution(mesh):
    placed = (
        P(("grp", "rep"), "code", None, None),
        P(("grp", "rep"), "code", None, None),
        P(("grp", "rep"), "code", None),
        P(),
        P(("grp", "rep"), None),
    )
    return jax.shard_map(
        local,
        mesh=mesh,
        in_specs=placed,
        out_specs=(P(("grp", "rep"), "code", None), P(("grp", "rep"), "code", None, None)),
        check_vma=False,
    )
```

```python
import functools

import jax
import jax.numpy as jnp
from jax import lax
from jax.experimental import pallas as pl
from jax.experimental.pallas import tpu as pltpu
from jax.sharding import PartitionSpec as P

IN_VMEM = pl.BlockSpec(memory_space=pltpu.VMEM)
IN_SMEM = pl.BlockSpec(memory_space=pltpu.SMEM)
ANYWHERE = pl.BlockSpec(memory_space=pl.ANY)

DIRECT_MEMBERS = 8
KERNEL_VMEM = 8 * 2**20


def rounds_of(members):
    return range(members - 1, 0, -1)


def order_of(members, direct):
    if not direct:
        return list(range(members))
    me = lax.axis_index("code")
    return [me ^ r for r in (0, *rounds_of(members))]


def plan_kernel(direct, ids_ref, generator_ref, parity_ref, base_ref, table_ref):
    spans, members = generator_ref.shape
    width = base_ref.shape[2]
    first, second = ids_ref[0, 0], ids_ref[0, 1]
    col_first = [generator_ref[j, first] for j in range(spans)]
    col_second = [generator_ref[j, second] for j in range(spans)]
    gram_first = sum(x * x for x in col_first)
    gram_cross = sum(x * y for x, y in zip(col_first, col_second))
    gram_second = sum(y * y for y in col_second)
    determinant = gram_first * gram_second - gram_cross * gram_cross

    def spread(value):
        return jnp.full((1, width), value, jnp.float32)

    def put(row, value):
        table_ref[row : row + 1, :] = value

    over = spread(determinant)
    weights = [
        [spread(gram_second * x - gram_cross * y) / over for x, y in zip(col_first, col_second)],
        [spread(gram_first * y - gram_cross * x) / over for x, y in zip(col_first, col_second)],
    ]
    for k in range(2):
        base_ref[k] = sum(
            weights[k][j] * parity_ref[:, j * width : (j + 1) * width] for j in range(spans)
        )
    for i, c in enumerate(order_of(members, direct)):
        column = [generator_ref[j, c] for j in range(spans)]
        alive = jnp.logical_and(first != c, second != c)
        for k in range(2):
            put(
                k * members + i,
                sum(weights[k][j] * jnp.where(alive, column[j], 0.0) for j in range(spans)),
            )
        for j in range(spans):
            put((2 + j) * members + i, spread(column[j]))
        put((2 + spans) * members + i, spread(jnp.where(first == c, 1.0, 0.0)))
    me = lax.axis_index("code")
    lost = jnp.logical_or(first == me, second == me)
    put((3 + spans) * members, spread(jnp.where(lost, 1.0, 0.0)))


def weigh(table_ref, start, rows):
    total = None
    for i, block in enumerate(rows):
        term = table_ref[start + i : start + i + 1, :] * block
        total = term if total is None else total + term
    return total


def rebuilt_for(base_ref, table_ref, rows):
    members = len(rows)
    rebuilt = [base_ref[k] - weigh(table_ref, k * members, rows) for k in range(2)]
    picks = table_ref.shape[0] - 1 - members
    return [
        jnp.where(table_ref[picks + i : picks + i + 1, :] > 0.5, *rebuilt) for i in range(members)
    ]


def rebuild_whole_kernel(base_ref, table_ref, rows_ref, out_ref):
    rows = [rows_ref[c] for c in range(rows_ref.shape[0])]
    for c, block in enumerate(rebuilt_for(base_ref, table_ref, rows)):
        out_ref[c] = block


def parity_whole_kernel(table_ref, rows_ref, out_ref):
    parity_into(out_ref, table_ref, [rows_ref[c] for c in range(rows_ref.shape[0])])


def parity_into(out_ref, table_ref, rows):
    members, width = len(rows), table_ref.shape[1]
    for j in range(out_ref.shape[1] // width):
        out_ref[:, j * width : (j + 1) * width] = weigh(table_ref, (2 + j) * members, rows)


def cut_kernel(plan, *refs):
    outs, sems = refs[-1 - len(plan) : -1], refs[-1]
    me = lax.axis_index("code")
    copies = []
    for pieces, out in zip(plan, outs):
        for i, (operand, r) in enumerate(pieces):
            place = out if len(pieces) == 1 else out.at[i]
            source = refs[operand].at[me ^ r]
            copies.append(pltpu.make_async_copy(source, place, sems.at[len(copies)]))
    for copy in copies:
        copy.start()
    for copy in copies:
        copy.wait()


def rebuild_paired_kernel(base_ref, table_ref, current_ref, *refs):
    members = len(refs) // 2
    rows, outs, current_out_ref = refs[:members], refs[members:-1], refs[-1]
    for out_ref, block in zip(outs, rebuilt_for(base_ref, table_ref, [r[...] for r in rows])):
        out_ref[...] = block
    current_out_ref[...] = current_ref[...]


def parity_paired_kernel(table_ref, *refs):
    rows, out_ref, done_ref = refs[:-2], refs[-2], refs[-1]
    parity_into(out_ref, table_ref, [last_of(row) for row in rows])
    done_ref[...] = jnp.zeros(done_ref.shape, done_ref.dtype)


def first_of(ref):
    return ref[0] if len(ref.shape) == 3 else ref[...]


def last_of(ref):
    return ref[1] if len(ref.shape) == 3 else ref[...]


def restore_kernel(table_ref, earlier_ref, held_back_by, *refs):
    pieces, out_ref = refs[:-1], refs[-1]
    members = len(pieces)
    last = table_ref.shape[0] - 1
    lost = table_ref[last : last + 1, :] > 0.5
    for c, piece in zip(order_of(members, True), pieces):
        out_ref[c] = jnp.where(lost, first_of(piece), earlier_ref[c])


def call(kernel, specs, outs, args, flops, **options):
    total = sum(x.size for x in args) + sum(o.size for o in jax.tree.leaves(outs))
    return pl.pallas_call(
        kernel,
        in_specs=specs,
        out_specs=jax.tree.map(lambda _: IN_VMEM, outs),
        out_shape=outs,
        compiler_params=pltpu.CompilerParams(vmem_limit_bytes=KERNEL_VMEM),
        cost_estimate=pl.CostEstimate(flops=flops, bytes_accessed=4 * total, transcendentals=0),
        **options,
    )(*args)


def floats(*shape):
    return jax.ShapeDtypeStruct(shape, jnp.float32)


def trade(pieces, rounds, members):
    return [
        lax.ppermute(piece, "code", [(d, d ^ r) for d in range(members)])
        for r, piece in zip(rounds, pieces)
    ]


def cut(slabs, plan, *held_back_by):
    count = sum(len(pieces) for pieces in plan)
    block = slabs[0].shape[1:]
    return call(
        functools.partial(cut_kernel, plan),
        [ANYWHERE] * (len(slabs) + len(held_back_by)),
        [floats(*block) if len(p) == 1 else floats(len(p), *block) for p in plan],
        (*slabs, *held_back_by),
        0,
        scratch_shapes=[pltpu.SemaphoreType.DMA((count,))],
    )


def local(state_slab, previous_slab, previous_parity, generator, failed_ids):
    position = lax.axis_index("code")
    members = lax.axis_size("code")
    slab_rows, width = state_slab.shape[2:]
    spans = generator.shape[0]
    own_rows = slab_rows // members
    blocks = (members, own_rows, width)
    earlier = previous_slab.reshape(blocks)
    current = state_slab.reshape(blocks)
    direct = 4 <= members <= DIRECT_MEMBERS and members & (members - 1) == 0

    base, table = call(
        functools.partial(plan_kernel, direct),
        [IN_SMEM, IN_SMEM, IN_VMEM],
        (floats(2, own_rows, width), floats((3 + spans) * members + 1, width)),
        (failed_ids, generator, previous_parity[0]),
        4 * spans * own_rows * width,
    )
    parity_shape = floats(own_rows, spans * width)
    rebuild_cost = 4 * slab_rows * width
    parity_cost = 2 * spans * slab_rows * width
    if direct:
        rounds = list(rounds_of(members))
        block = floats(own_rows, width)
        pinned = [pltpu.with_memory_space_constraint(x, pltpu.HBM) for x in (earlier, current)]
        cut_all = cut(pinned, [[(slab, r)] for slab in range(2) for r in [0] + rounds])
        own_earlier, *cut_earlier = cut_all[:members]
        own_current, *cut_current, last_current = cut_all[members:]
        earlier_rows = trade(cut_earlier, rounds, members)
        current_rows = trade(cut_current, rounds[:-1], members)
        *outgoing, last_current = call(
            rebuild_paired_kernel,
            [IN_VMEM] * (members + 3),
            [block] * (members + 1),
            (base, table, last_current, own_earlier, *earlier_rows),
            rebuild_cost,
        )
        incoming = trade(outgoing[1:], rounds, members)
        current_rows = [own_current, *current_rows, *trade([last_current], rounds[-1:], members)]
        new_parity, parity_done = call(
            parity_paired_kernel,
            [IN_VMEM] * (members + 1),
            (parity_shape, floats(8, 128)),
            (table, *current_rows),
            parity_cost,
        )
        restored_state = call(
            restore_kernel,
            [IN_VMEM, IN_VMEM, ANYWHERE] + [IN_VMEM] * members,
            floats(*blocks),
            (table, earlier, parity_done, outgoing[0], *incoming),
            0,
        )
    else:
        earlier_rows = lax.all_to_all(earlier, "code", 0, 0, tiled=True)
        current_rows = lax.all_to_all(current, "code", 0, 0, tiled=True)
        outgoing = call(
            rebuild_whole_kernel,
            [IN_VMEM] * 3,
            floats(*blocks),
            (base, table, earlier_rows),
            rebuild_cost,
        )
        incoming = lax.all_to_all(outgoing, "code", 0, 0, tiled=True)
        lost = (position == failed_ids[0, 0]) | (position == failed_ids[0, 1])
        restored_state = jnp.where(lost, incoming, earlier)
        new_parity = call(
            parity_whole_kernel,
            [IN_VMEM] * 2,
            parity_shape,
            (table, current_rows),
            parity_cost,
        )
    return (new_parity[None], restored_state.reshape(state_slab.shape))


def solution(mesh):
    placed = (
        P(("grp", "rep"), "code", None, None),
        P(("grp", "rep"), "code", None, None),
        P(("grp", "rep"), "code", None),
        P(),
        P(("grp", "rep"), None),
    )
    return jax.shard_map(
        local,
        mesh=mesh,
        in_specs=placed,
        out_specs=(P(("grp", "rep"), "code", None), P(("grp", "rep"), "code", None, None)),
        check_vma=False,
    )
```

```python
import functools

import jax
import jax.numpy as jnp
from jax import lax
from jax.experimental import pallas as pl
from jax.experimental.pallas import tpu as pltpu
from jax.sharding import PartitionSpec as P

IN_VMEM = pl.BlockSpec(memory_space=pltpu.VMEM)
IN_SMEM = pl.BlockSpec(memory_space=pltpu.SMEM)
ANYWHERE = pl.BlockSpec(memory_space=pl.ANY)

DIRECT_MEMBERS = 8
KERNEL_VMEM = 8 * 2**20


def rounds_of(members):
    return range(members - 1, 0, -1)


def order_of(members, direct):
    if not direct:
        return list(range(members))
    me = lax.axis_index("code")
    return [me ^ r for r in (0, *rounds_of(members))]


def plan_kernel(direct, ids_ref, generator_ref, parity_ref, base_ref, table_ref):
    spans, members = generator_ref.shape
    width = base_ref.shape[2]
    first, second = ids_ref[0, 0], ids_ref[0, 1]
    col_first = [generator_ref[j, first] for j in range(spans)]
    col_second = [generator_ref[j, second] for j in range(spans)]
    gram_first = sum(x * x for x in col_first)
    gram_cross = sum(x * y for x, y in zip(col_first, col_second))
    gram_second = sum(y * y for y in col_second)
    determinant = gram_first * gram_second - gram_cross * gram_cross

    def spread(value):
        return jnp.full((1, width), value, jnp.float32)

    def put(row, value):
        table_ref[row : row + 1, :] = value

    over = spread(determinant)
    weights = [
        [spread(gram_second * x - gram_cross * y) / over for x, y in zip(col_first, col_second)],
        [spread(gram_first * y - gram_cross * x) / over for x, y in zip(col_first, col_second)],
    ]
    for k in range(2):
        base_ref[k] = sum(
            weights[k][j] * parity_ref[:, j * width : (j + 1) * width] for j in range(spans)
        )
    for i, c in enumerate(order_of(members, direct)):
        column = [generator_ref[j, c] for j in range(spans)]
        alive = jnp.logical_and(first != c, second != c)
        for k in range(2):
            put(
                k * members + i,
                sum(weights[k][j] * jnp.where(alive, column[j], 0.0) for j in range(spans)),
            )
        for j in range(spans):
            put((2 + j) * members + i, spread(column[j]))
        put((2 + spans) * members + i, spread(jnp.where(first == c, 1.0, 0.0)))
    me = lax.axis_index("code")
    lost = jnp.logical_or(first == me, second == me)
    put((3 + spans) * members, spread(jnp.where(lost, 1.0, 0.0)))


def weigh(table_ref, start, rows):
    total = None
    for i, block in enumerate(rows):
        term = table_ref[start + i : start + i + 1, :] * block
        total = term if total is None else total + term
    return total


def rebuilt_for(base_ref, table_ref, rows):
    members = len(rows)
    rebuilt = [base_ref[k] - weigh(table_ref, k * members, rows) for k in range(2)]
    picks = table_ref.shape[0] - 1 - members
    return [
        jnp.where(table_ref[picks + i : picks + i + 1, :] > 0.5, *rebuilt) for i in range(members)
    ]


def rebuild_whole_kernel(base_ref, table_ref, rows_ref, out_ref):
    rows = [rows_ref[c] for c in range(rows_ref.shape[0])]
    for c, block in enumerate(rebuilt_for(base_ref, table_ref, rows)):
        out_ref[c] = block


def parity_whole_kernel(table_ref, rows_ref, out_ref):
    parity_into(out_ref, table_ref, [rows_ref[c] for c in range(rows_ref.shape[0])])


def parity_into(out_ref, table_ref, rows):
    members, width = len(rows), table_ref.shape[1]
    for j in range(out_ref.shape[1] // width):
        out_ref[:, j * width : (j + 1) * width] = weigh(table_ref, (2 + j) * members, rows)


def rebuild_paired_kernel(base_ref, table_ref, *refs):
    rows, outs = refs[: len(refs) // 2], refs[len(refs) // 2 :]
    for out_ref, block in zip(outs, rebuilt_for(base_ref, table_ref, [r[...] for r in rows])):
        out_ref[...] = block


def parity_paired_kernel(table_ref, *refs):
    rows, out_ref, done_ref = refs[:-2], refs[-2], refs[-1]
    parity_into(out_ref, table_ref, [r[...] for r in rows])
    done_ref[...] = jnp.zeros(done_ref.shape, done_ref.dtype)


def restore_kernel(table_ref, earlier_ref, held_back_by, *refs):
    pieces, out_ref = refs[:-1], refs[-1]
    members = len(pieces)
    last = table_ref.shape[0] - 1
    lost = table_ref[last : last + 1, :] > 0.5
    for c, piece in zip(order_of(members, True), pieces):
        out_ref[c] = jnp.where(lost, piece[...], earlier_ref[c])


def call(kernel, specs, outs, args, flops, **options):
    total = sum(x.size for x in args) + sum(o.size for o in jax.tree.leaves(outs))
    return pl.pallas_call(
        kernel,
        in_specs=specs,
        out_specs=jax.tree.map(lambda _: IN_VMEM, outs),
        out_shape=outs,
        compiler_params=pltpu.CompilerParams(vmem_limit_bytes=KERNEL_VMEM),
        cost_estimate=pl.CostEstimate(flops=flops, bytes_accessed=4 * total, transcendentals=0),
        **options,
    )(*args)


def floats(*shape):
    return jax.ShapeDtypeStruct(shape, jnp.float32)


def trade(pieces, rounds, members):
    return [
        lax.ppermute(piece, "code", [(d, d ^ r) for d in range(members)])
        for r, piece in zip(rounds, pieces)
    ]


def cut(blocks, rounds):
    me = lax.axis_index("code")
    return [lax.dynamic_index_in_dim(blocks, me ^ r, 0, keepdims=False) for r in rounds]


def local(state_slab, previous_slab, previous_parity, generator, failed_ids):
    position = lax.axis_index("code")
    members = lax.axis_size("code")
    slab_rows, width = state_slab.shape[2:]
    spans = generator.shape[0]
    own_rows = slab_rows // members
    blocks = (members, own_rows, width)
    earlier = previous_slab.reshape(blocks)
    current = state_slab.reshape(blocks)
    direct = 4 <= members <= DIRECT_MEMBERS and members & (members - 1) == 0

    base, table = call(
        functools.partial(plan_kernel, direct),
        [IN_SMEM, IN_SMEM, IN_VMEM],
        (floats(2, own_rows, width), floats((3 + spans) * members + 1, width)),
        (failed_ids, generator, previous_parity[0]),
        4 * spans * own_rows * width,
    )
    parity_shape = floats(own_rows, spans * width)
    rebuild_cost = 4 * slab_rows * width
    parity_cost = 2 * spans * slab_rows * width
    if direct:
        rounds = list(rounds_of(members))
        block = floats(own_rows, width)
        own_earlier, *cut_earlier = cut(earlier, [0] + rounds)
        earlier_rows = trade(cut_earlier, rounds, members)
        own_current, *cut_current = cut(current, [0] + rounds)
        outgoing = call(
            rebuild_paired_kernel,
            [IN_VMEM] * (members + 2),
            [block] * members,
            (base, table, own_earlier, *earlier_rows),
            rebuild_cost,
        )
        incoming = trade(outgoing[1:], rounds, members)
        current_rows = [own_current, *trade(cut_current, rounds, members)]
        new_parity, parity_done = call(
            parity_paired_kernel,
            [IN_VMEM] * (members + 1),
            (parity_shape, floats(8, 128)),
            (table, *current_rows),
            parity_cost,
        )
        restored_state = call(
            restore_kernel,
            [IN_VMEM, IN_VMEM, ANYWHERE] + [IN_VMEM] * members,
            floats(*blocks),
            (table, earlier, parity_done, outgoing[0], *incoming),
            0,
        )
    else:
        earlier_rows = lax.all_to_all(earlier, "code", 0, 0, tiled=True)
        current_rows = lax.all_to_all(current, "code", 0, 0, tiled=True)
        outgoing = call(
            rebuild_whole_kernel,
            [IN_VMEM] * 3,
            floats(*blocks),
            (base, table, earlier_rows),
            rebuild_cost,
        )
        incoming = lax.all_to_all(outgoing, "code", 0, 0, tiled=True)
        lost = (position == failed_ids[0, 0]) | (position == failed_ids[0, 1])
        restored_state = jnp.where(lost, incoming, earlier)
        new_parity = call(
            parity_whole_kernel,
            [IN_VMEM] * 2,
            parity_shape,
            (table, current_rows),
            parity_cost,
        )
    return (new_parity[None], restored_state.reshape(state_slab.shape))


def solution(mesh):
    placed = (
        P(("grp", "rep"), "code", None, None),
        P(("grp", "rep"), "code", None, None),
        P(("grp", "rep"), "code", None),
        P(),
        P(("grp", "rep"), None),
    )
    return jax.shard_map(
        local,
        mesh=mesh,
        in_specs=placed,
        out_specs=(P(("grp", "rep"), "code", None), P(("grp", "rep"), "code", None, None)),
        check_vma=False,
    )
```

```python
import functools

import jax
import jax.numpy as jnp
from jax import lax
from jax.experimental import pallas as pl
from jax.experimental.pallas import tpu as pltpu
from jax.sharding import PartitionSpec as P

IN_VMEM = pl.BlockSpec(memory_space=pltpu.VMEM)
IN_SMEM = pl.BlockSpec(memory_space=pltpu.SMEM)
ANYWHERE = pl.BlockSpec(memory_space=pl.ANY)

DIRECT_MEMBERS = 8
KERNEL_VMEM = 8 * 2**20


def rounds_of(members):
    return range(members - 1, 0, -1)


def order_of(members, direct):
    if not direct:
        return list(range(members))
    me = lax.axis_index("code")
    return [me ^ r for r in (0, *rounds_of(members))]


def targets_of(members, direct):
    if not direct:
        return list(range(members))
    me = lax.axis_index("code")
    return [lax.rem(me + s, members) for s in range(members)]


def sources_of(members):
    me = lax.axis_index("code")
    return [lax.rem(me + members - s, members) for s in range(members)]


def plan_kernel(direct, ids_ref, generator_ref, parity_ref, base_ref, table_ref):
    spans, members = generator_ref.shape
    width = base_ref.shape[2]
    first, second = ids_ref[0, 0], ids_ref[0, 1]
    col_first = [generator_ref[j, first] for j in range(spans)]
    col_second = [generator_ref[j, second] for j in range(spans)]
    gram_first = sum(x * x for x in col_first)
    gram_cross = sum(x * y for x, y in zip(col_first, col_second))
    gram_second = sum(y * y for y in col_second)
    determinant = gram_first * gram_second - gram_cross * gram_cross

    def spread(value):
        return jnp.full((1, width), value, jnp.float32)

    def put(row, value):
        table_ref[row : row + 1, :] = value

    over = spread(determinant)
    weights = [
        [spread(gram_second * x - gram_cross * y) / over for x, y in zip(col_first, col_second)],
        [spread(gram_first * y - gram_cross * x) / over for x, y in zip(col_first, col_second)],
    ]
    for k in range(2):
        base_ref[k] = sum(
            weights[k][j] * parity_ref[:, j * width : (j + 1) * width] for j in range(spans)
        )
    for i, c in enumerate(order_of(members, direct)):
        column = [generator_ref[j, c] for j in range(spans)]
        alive = jnp.logical_and(first != c, second != c)
        for k in range(2):
            put(
                k * members + i,
                sum(weights[k][j] * jnp.where(alive, column[j], 0.0) for j in range(spans)),
            )
        for j in range(spans):
            put((2 + j) * members + i, spread(column[j]))
    for i, c in enumerate(targets_of(members, direct)):
        put((2 + spans) * members + i, spread(jnp.where(first == c, 1.0, 0.0)))
    me = lax.axis_index("code")
    lost = jnp.logical_or(first == me, second == me)
    put((3 + spans) * members, spread(jnp.where(lost, 1.0, 0.0)))


def weigh(table_ref, start, rows):
    total = None
    for i, block in enumerate(rows):
        term = table_ref[start + i : start + i + 1, :] * block
        total = term if total is None else total + term
    return total


def rebuilt_for(base_ref, table_ref, rows):
    members = len(rows)
    rebuilt = [base_ref[k] - weigh(table_ref, k * members, rows) for k in range(2)]
    picks = table_ref.shape[0] - 1 - members
    return [
        jnp.where(table_ref[picks + i : picks + i + 1, :] > 0.5, *rebuilt) for i in range(members)
    ]


def rebuild_whole_kernel(base_ref, table_ref, rows_ref, out_ref):
    rows = [rows_ref[c] for c in range(rows_ref.shape[0])]
    for c, block in enumerate(rebuilt_for(base_ref, table_ref, rows)):
        out_ref[c] = block


def parity_whole_kernel(table_ref, rows_ref, out_ref):
    parity_into(out_ref, table_ref, [rows_ref[c] for c in range(rows_ref.shape[0])])


def parity_into(out_ref, table_ref, rows):
    members, width = len(rows), table_ref.shape[1]
    for j in range(out_ref.shape[1] // width):
        out_ref[:, j * width : (j + 1) * width] = weigh(table_ref, (2 + j) * members, rows)


def rebuild_paired_kernel(base_ref, table_ref, *refs):
    rows, outs = refs[: len(refs) // 2], refs[len(refs) // 2 :]
    for out_ref, block in zip(outs, rebuilt_for(base_ref, table_ref, [r[...] for r in rows])):
        out_ref[...] = block


def parity_paired_kernel(table_ref, *refs):
    rows, out_ref, done_ref = refs[:-2], refs[-2], refs[-1]
    parity_into(out_ref, table_ref, [r[...] for r in rows])
    done_ref[...] = jnp.zeros(done_ref.shape, done_ref.dtype)


def restore_kernel(table_ref, earlier_ref, held_back_by, *refs):
    pieces, out_ref = refs[:-1], refs[-1]
    members = len(pieces)
    last = table_ref.shape[0] - 1
    lost = table_ref[last : last + 1, :] > 0.5
    for c, piece in zip(sources_of(members), pieces):
        out_ref[c] = jnp.where(lost, piece[...], earlier_ref[c])


def call(kernel, specs, outs, args, flops, **options):
    total = sum(x.size for x in args) + sum(o.size for o in jax.tree.leaves(outs))
    return pl.pallas_call(
        kernel,
        in_specs=specs,
        out_specs=jax.tree.map(lambda _: IN_VMEM, outs),
        out_shape=outs,
        compiler_params=pltpu.CompilerParams(vmem_limit_bytes=KERNEL_VMEM),
        cost_estimate=pl.CostEstimate(flops=flops, bytes_accessed=4 * total, transcendentals=0),
        **options,
    )(*args)


def floats(*shape):
    return jax.ShapeDtypeStruct(shape, jnp.float32)


def pass_on(pieces, members):
    return [
        lax.ppermute(piece, "code", [(d, (d + s) % members) for d in range(members)])
        for s, piece in enumerate(pieces, 1)
    ]


def trade(pieces, rounds, members):
    return [
        lax.ppermute(piece, "code", [(d, d ^ r) for d in range(members)])
        for r, piece in zip(rounds, pieces)
    ]


def cut(blocks, rounds):
    me = lax.axis_index("code")
    return [lax.dynamic_index_in_dim(blocks, me ^ r, 0, keepdims=False) for r in rounds]


def local(state_slab, previous_slab, previous_parity, generator, failed_ids):
    position = lax.axis_index("code")
    members = lax.axis_size("code")
    slab_rows, width = state_slab.shape[2:]
    spans = generator.shape[0]
    own_rows = slab_rows // members
    blocks = (members, own_rows, width)
    earlier = previous_slab.reshape(blocks)
    current = state_slab.reshape(blocks)
    direct = 4 <= members <= DIRECT_MEMBERS and members & (members - 1) == 0

    base, table = call(
        functools.partial(plan_kernel, direct),
        [IN_SMEM, IN_SMEM, IN_VMEM],
        (floats(2, own_rows, width), floats((3 + spans) * members + 1, width)),
        (failed_ids, generator, previous_parity[0]),
        4 * spans * own_rows * width,
    )
    parity_shape = floats(own_rows, spans * width)
    rebuild_cost = 4 * slab_rows * width
    parity_cost = 2 * spans * slab_rows * width
    if direct:
        rounds = list(rounds_of(members))
        block = floats(own_rows, width)
        own_earlier, *cut_earlier = cut(earlier, [0] + rounds)
        earlier_rows = trade(cut_earlier, rounds, members)
        own_current, *cut_current = cut(current, [0] + rounds)
        outgoing = call(
            rebuild_paired_kernel,
            [IN_VMEM] * (members + 2),
            [block] * members,
            (base, table, own_earlier, *earlier_rows),
            rebuild_cost,
        )
        incoming = pass_on(outgoing[1:], members)
        current_rows = [own_current, *trade(cut_current, rounds, members)]
        new_parity, parity_done = call(
            parity_paired_kernel,
            [IN_VMEM] * (members + 1),
            (parity_shape, floats(8, 128)),
            (table, *current_rows),
            parity_cost,
        )
        restored_state = call(
            restore_kernel,
            [IN_VMEM, IN_VMEM, ANYWHERE] + [IN_VMEM] * members,
            floats(*blocks),
            (table, earlier, parity_done, outgoing[0], *incoming),
            0,
        )
    else:
        earlier_rows = lax.all_to_all(earlier, "code", 0, 0, tiled=True)
        current_rows = lax.all_to_all(current, "code", 0, 0, tiled=True)
        outgoing = call(
            rebuild_whole_kernel,
            [IN_VMEM] * 3,
            floats(*blocks),
            (base, table, earlier_rows),
            rebuild_cost,
        )
        incoming = lax.all_to_all(outgoing, "code", 0, 0, tiled=True)
        lost = (position == failed_ids[0, 0]) | (position == failed_ids[0, 1])
        restored_state = jnp.where(lost, incoming, earlier)
        new_parity = call(
            parity_whole_kernel,
            [IN_VMEM] * 2,
            parity_shape,
            (table, current_rows),
            parity_cost,
        )
    return (new_parity[None], restored_state.reshape(state_slab.shape))


def solution(mesh):
    placed = (
        P(("grp", "rep"), "code", None, None),
        P(("grp", "rep"), "code", None, None),
        P(("grp", "rep"), "code", None),
        P(),
        P(("grp", "rep"), None),
    )
    return jax.shard_map(
        local,
        mesh=mesh,
        in_specs=placed,
        out_specs=(P(("grp", "rep"), "code", None), P(("grp", "rep"), "code", None, None)),
        check_vma=False,
    )
```

```python
import functools

import jax
import jax.numpy as jnp
from jax import lax
from jax.experimental import pallas as pl
from jax.experimental.pallas import tpu as pltpu
from jax.sharding import PartitionSpec as P

IN_VMEM = pl.BlockSpec(memory_space=pltpu.VMEM)
IN_SMEM = pl.BlockSpec(memory_space=pltpu.SMEM)
ANYWHERE = pl.BlockSpec(memory_space=pl.ANY)

DIRECT_MEMBERS = 8
KERNEL_VMEM = 8 * 2**20


def rounds_of(members):
    return range(members - 1, 0, -1)


def order_of(members, direct):
    if not direct:
        return list(range(members))
    me = lax.axis_index("code")
    return [me ^ r for r in (0, *rounds_of(members))]


def targets_of(members, direct):
    if not direct:
        return list(range(members))
    me = lax.axis_index("code")
    return [lax.rem(me + s, members) for s in range(members)]


def sources_of(members, direct):
    if not direct:
        return list(range(members))
    me = lax.axis_index("code")
    return [lax.rem(me + members - s, members) for s in range(members)]


def plan_kernel(direct, ids_ref, generator_ref, parity_ref, base_ref, table_ref):
    spans, members = generator_ref.shape
    width = base_ref.shape[2]
    first, second = ids_ref[0, 0], ids_ref[0, 1]
    col_first = [generator_ref[j, first] for j in range(spans)]
    col_second = [generator_ref[j, second] for j in range(spans)]
    gram_first = sum(x * x for x in col_first)
    gram_cross = sum(x * y for x, y in zip(col_first, col_second))
    gram_second = sum(y * y for y in col_second)
    determinant = gram_first * gram_second - gram_cross * gram_cross

    def spread(value):
        return jnp.full((1, width), value, jnp.float32)

    def put(row, value):
        table_ref[row : row + 1, :] = value

    over = spread(determinant)
    weights = [
        [spread(gram_second * x - gram_cross * y) / over for x, y in zip(col_first, col_second)],
        [spread(gram_first * y - gram_cross * x) / over for x, y in zip(col_first, col_second)],
    ]
    for k in range(2):
        base_ref[k] = sum(
            weights[k][j] * parity_ref[:, j * width : (j + 1) * width] for j in range(spans)
        )
    for i, c in enumerate(order_of(members, direct)):
        column = [generator_ref[j, c] for j in range(spans)]
        alive = jnp.logical_and(first != c, second != c)
        for k in range(2):
            put(
                k * members + i,
                sum(weights[k][j] * jnp.where(alive, column[j], 0.0) for j in range(spans)),
            )
    for i, c in enumerate(sources_of(members, direct)):
        for j in range(spans):
            put((2 + j) * members + i, spread(generator_ref[j, c]))
    for i, c in enumerate(targets_of(members, direct)):
        put((2 + spans) * members + i, spread(jnp.where(first == c, 1.0, 0.0)))
    me = lax.axis_index("code")
    lost = jnp.logical_or(first == me, second == me)
    put((3 + spans) * members, spread(jnp.where(lost, 1.0, 0.0)))


def weigh(table_ref, start, rows):
    total = None
    for i, block in enumerate(rows):
        term = table_ref[start + i : start + i + 1, :] * block
        total = term if total is None else total + term
    return total


def rebuilt_for(base_ref, table_ref, rows):
    members = len(rows)
    rebuilt = [base_ref[k] - weigh(table_ref, k * members, rows) for k in range(2)]
    picks = table_ref.shape[0] - 1 - members
    return [
        jnp.where(table_ref[picks + i : picks + i + 1, :] > 0.5, *rebuilt) for i in range(members)
    ]


def rebuild_whole_kernel(base_ref, table_ref, rows_ref, out_ref):
    rows = [rows_ref[c] for c in range(rows_ref.shape[0])]
    for c, block in enumerate(rebuilt_for(base_ref, table_ref, rows)):
        out_ref[c] = block


def parity_whole_kernel(table_ref, rows_ref, out_ref):
    parity_into(out_ref, table_ref, [rows_ref[c] for c in range(rows_ref.shape[0])])


def parity_into(out_ref, table_ref, rows):
    members, width = len(rows), table_ref.shape[1]
    for j in range(out_ref.shape[1] // width):
        out_ref[:, j * width : (j + 1) * width] = weigh(table_ref, (2 + j) * members, rows)


def rebuild_paired_kernel(base_ref, table_ref, *refs):
    rows, outs = refs[: len(refs) // 2], refs[len(refs) // 2 :]
    for out_ref, block in zip(outs, rebuilt_for(base_ref, table_ref, [r[...] for r in rows])):
        out_ref[...] = block


def parity_paired_kernel(table_ref, *refs):
    rows, out_ref, done_ref = refs[:-2], refs[-2], refs[-1]
    parity_into(out_ref, table_ref, [r[...] for r in rows])
    done_ref[...] = jnp.zeros(done_ref.shape, done_ref.dtype)


def restore_kernel(table_ref, earlier_ref, held_back_by, *refs):
    pieces, out_ref = refs[:-1], refs[-1]
    members = len(pieces)
    last = table_ref.shape[0] - 1
    lost = table_ref[last : last + 1, :] > 0.5
    for c, piece in zip(sources_of(members, True), pieces):
        out_ref[c] = jnp.where(lost, piece[...], earlier_ref[c])


def call(kernel, specs, outs, args, flops, **options):
    total = sum(x.size for x in args) + sum(o.size for o in jax.tree.leaves(outs))
    return pl.pallas_call(
        kernel,
        in_specs=specs,
        out_specs=jax.tree.map(lambda _: IN_VMEM, outs),
        out_shape=outs,
        compiler_params=pltpu.CompilerParams(vmem_limit_bytes=KERNEL_VMEM),
        cost_estimate=pl.CostEstimate(flops=flops, bytes_accessed=4 * total, transcendentals=0),
        **options,
    )(*args)


def floats(*shape):
    return jax.ShapeDtypeStruct(shape, jnp.float32)


def pass_on(pieces, members):
    return [
        lax.ppermute(piece, "code", [(d, (d + s) % members) for d in range(members)])
        for s, piece in enumerate(pieces, 1)
    ]


def trade(pieces, rounds, members):
    return [
        lax.ppermute(piece, "code", [(d, d ^ r) for d in range(members)])
        for r, piece in zip(rounds, pieces)
    ]


def cut(blocks, order):
    return [lax.dynamic_index_in_dim(blocks, c, 0, keepdims=False) for c in order]


def local(state_slab, previous_slab, previous_parity, generator, failed_ids):
    position = lax.axis_index("code")
    members = lax.axis_size("code")
    slab_rows, width = state_slab.shape[2:]
    spans = generator.shape[0]
    own_rows = slab_rows // members
    blocks = (members, own_rows, width)
    earlier = previous_slab.reshape(blocks)
    current = state_slab.reshape(blocks)
    direct = 4 <= members <= DIRECT_MEMBERS and members & (members - 1) == 0

    base, table = call(
        functools.partial(plan_kernel, direct),
        [IN_SMEM, IN_SMEM, IN_VMEM],
        (floats(2, own_rows, width), floats((3 + spans) * members + 1, width)),
        (failed_ids, generator, previous_parity[0]),
        4 * spans * own_rows * width,
    )
    parity_shape = floats(own_rows, spans * width)
    rebuild_cost = 4 * slab_rows * width
    parity_cost = 2 * spans * slab_rows * width
    if direct:
        rounds = list(rounds_of(members))
        block = floats(own_rows, width)
        own_earlier, *cut_earlier = cut(earlier, order_of(members, True))
        earlier_rows = trade(cut_earlier, rounds, members)
        own_current, *cut_current = cut(current, targets_of(members, True))
        outgoing = call(
            rebuild_paired_kernel,
            [IN_VMEM] * (members + 2),
            [block] * members,
            (base, table, own_earlier, *earlier_rows),
            rebuild_cost,
        )
        incoming = pass_on(outgoing[1:], members)
        current_rows = [own_current, *pass_on(cut_current, members)]
        new_parity, parity_done = call(
            parity_paired_kernel,
            [IN_VMEM] * (members + 1),
            (parity_shape, floats(8, 128)),
            (table, *current_rows),
            parity_cost,
        )
        restored_state = call(
            restore_kernel,
            [IN_VMEM, IN_VMEM, ANYWHERE] + [IN_VMEM] * members,
            floats(*blocks),
            (table, earlier, parity_done, outgoing[0], *incoming),
            0,
        )
    else:
        earlier_rows = lax.all_to_all(earlier, "code", 0, 0, tiled=True)
        current_rows = lax.all_to_all(current, "code", 0, 0, tiled=True)
        outgoing = call(
            rebuild_whole_kernel,
            [IN_VMEM] * 3,
            floats(*blocks),
            (base, table, earlier_rows),
            rebuild_cost,
        )
        incoming = lax.all_to_all(outgoing, "code", 0, 0, tiled=True)
        lost = (position == failed_ids[0, 0]) | (position == failed_ids[0, 1])
        restored_state = jnp.where(lost, incoming, earlier)
        new_parity = call(
            parity_whole_kernel,
            [IN_VMEM] * 2,
            parity_shape,
            (table, current_rows),
            parity_cost,
        )
    return (new_parity[None], restored_state.reshape(state_slab.shape))


def solution(mesh):
    placed = (
        P(("grp", "rep"), "code", None, None),
        P(("grp", "rep"), "code", None, None),
        P(("grp", "rep"), "code", None),
        P(),
        P(("grp", "rep"), None),
    )
    return jax.shard_map(
        local,
        mesh=mesh,
        in_specs=placed,
        out_specs=(P(("grp", "rep"), "code", None), P(("grp", "rep"), "code", None, None)),
        check_vma=False,
    )
```

```python
import functools

import jax
import jax.numpy as jnp
from jax import lax
from jax.experimental import pallas as pl
from jax.experimental.pallas import tpu as pltpu
from jax.sharding import PartitionSpec as P

IN_VMEM = pl.BlockSpec(memory_space=pltpu.VMEM)
IN_SMEM = pl.BlockSpec(memory_space=pltpu.SMEM)
ANYWHERE = pl.BlockSpec(memory_space=pl.ANY)

DIRECT_MEMBERS = 8
KERNEL_VMEM = 8 * 2**20


def partners_of(members):
    return list(range(1, members))


def shifts_of(members):
    return list(range(members)), [0, *range(members - 2, 0, -1), members - 1]


def met(members):
    me = lax.axis_index("code")
    return [me ^ r for r in [0] + partners_of(members)]


def ahead(members, shifts):
    me = lax.axis_index("code")
    return [lax.rem(me + s, members) for s in shifts]


def behind(members, shifts):
    me = lax.axis_index("code")
    return [lax.rem(me + members - s, members) for s in shifts]


def plan_kernel(direct, ids_ref, generator_ref, parity_ref, base_ref, table_ref):
    spans, members = generator_ref.shape
    width = base_ref.shape[2]
    first, second = ids_ref[0, 0], ids_ref[0, 1]
    col_first = [generator_ref[j, first] for j in range(spans)]
    col_second = [generator_ref[j, second] for j in range(spans)]
    gram_first = sum(x * x for x in col_first)
    gram_cross = sum(x * y for x, y in zip(col_first, col_second))
    gram_second = sum(y * y for y in col_second)
    determinant = gram_first * gram_second - gram_cross * gram_cross

    def spread(value):
        return jnp.full((1, width), value, jnp.float32)

    def put(row, value):
        table_ref[row : row + 1, :] = value

    over = spread(determinant)
    weights = [
        [spread(gram_second * x - gram_cross * y) / over for x, y in zip(col_first, col_second)],
        [spread(gram_first * y - gram_cross * x) / over for x, y in zip(col_first, col_second)],
    ]
    for k in range(2):
        base_ref[k] = sum(
            weights[k][j] * parity_ref[:, j * width : (j + 1) * width] for j in range(spans)
        )
    from_earlier = from_current = to_rebuilt = list(range(members))
    if direct:
        rebuilt_shifts, current_shifts = shifts_of(members)
        from_earlier = met(members)
        from_current = behind(members, current_shifts)
        to_rebuilt = ahead(members, rebuilt_shifts)
    for i, c in enumerate(from_earlier):
        column = [generator_ref[j, c] for j in range(spans)]
        alive = jnp.logical_and(first != c, second != c)
        for k in range(2):
            put(
                k * members + i,
                sum(weights[k][j] * jnp.where(alive, column[j], 0.0) for j in range(spans)),
            )
    for i, c in enumerate(from_current):
        for j in range(spans):
            put((2 + j) * members + i, spread(generator_ref[j, c]))
    for i, c in enumerate(to_rebuilt):
        put((2 + spans) * members + i, spread(jnp.where(first == c, 1.0, 0.0)))
    me = lax.axis_index("code")
    lost = jnp.logical_or(first == me, second == me)
    put((3 + spans) * members, spread(jnp.where(lost, 1.0, 0.0)))


def weigh(table_ref, start, rows):
    total = None
    for i, block in enumerate(rows):
        term = table_ref[start + i : start + i + 1, :] * block
        total = term if total is None else total + term
    return total


def rebuilt_for(base_ref, table_ref, rows):
    members = len(rows)
    rebuilt = [base_ref[k] - weigh(table_ref, k * members, rows) for k in range(2)]
    picks = table_ref.shape[0] - 1 - members
    return [
        jnp.where(table_ref[picks + i : picks + i + 1, :] > 0.5, *rebuilt) for i in range(members)
    ]


def rebuild_whole_kernel(base_ref, table_ref, rows_ref, out_ref):
    rows = [rows_ref[c] for c in range(rows_ref.shape[0])]
    for c, block in enumerate(rebuilt_for(base_ref, table_ref, rows)):
        out_ref[c] = block


def parity_whole_kernel(table_ref, rows_ref, out_ref):
    parity_into(out_ref, table_ref, [rows_ref[c] for c in range(rows_ref.shape[0])])


def parity_into(out_ref, table_ref, rows):
    members, width = len(rows), table_ref.shape[1]
    for j in range(out_ref.shape[1] // width):
        out_ref[:, j * width : (j + 1) * width] = weigh(table_ref, (2 + j) * members, rows)


def rebuild_paired_kernel(base_ref, table_ref, current_ref, *refs):
    members = len(refs) // 2
    rows, outs, current_out_ref = refs[:members], refs[members:-1], refs[-1]
    for out_ref, block in zip(outs, rebuilt_for(base_ref, table_ref, [r[...] for r in rows])):
        out_ref[...] = block
    current_out_ref[...] = current_ref[...]


def finish_kernel(table_ref, earlier_ref, *refs):
    members = (len(refs) - 2) // 2
    pieces, rows, (parity_ref, out_ref) = refs[:members], refs[members:-2], refs[-2:]
    parity_into(parity_ref, table_ref, [r[...] for r in rows])
    last = table_ref.shape[0] - 1
    lost = table_ref[last : last + 1, :] > 0.5
    for c, piece in zip(behind(members, shifts_of(members)[0]), pieces):
        out_ref[c] = jnp.where(lost, piece[...], earlier_ref[c])


def call(kernel, specs, outs, args, flops, **options):
    total = sum(x.size for x in args) + sum(o.size for o in jax.tree.leaves(outs))
    return pl.pallas_call(
        kernel,
        in_specs=specs,
        out_specs=jax.tree.map(lambda _: IN_VMEM, outs),
        out_shape=outs,
        compiler_params=pltpu.CompilerParams(vmem_limit_bytes=KERNEL_VMEM),
        cost_estimate=pl.CostEstimate(flops=flops, bytes_accessed=4 * total, transcendentals=0),
        **options,
    )(*args)


def floats(*shape):
    return jax.ShapeDtypeStruct(shape, jnp.float32)


def permute(pieces, targets):
    return [lax.ppermute(p, "code", list(enumerate(t))) for p, t in zip(pieces, targets)]


def pass_on(pieces, shifts, members):
    return permute(pieces, [[(d + s) % members for d in range(members)] for s in shifts])


def trade(pieces, rounds, members):
    return permute(pieces, [[d ^ r for d in range(members)] for r in rounds])


def cut(blocks, order):
    return [lax.dynamic_index_in_dim(blocks, c, 0, keepdims=False) for c in order]


def local(state_slab, previous_slab, previous_parity, generator, failed_ids):
    position = lax.axis_index("code")
    members = lax.axis_size("code")
    slab_rows, width = state_slab.shape[2:]
    spans = generator.shape[0]
    own_rows = slab_rows // members
    blocks = (members, own_rows, width)
    earlier = previous_slab.reshape(blocks)
    current = state_slab.reshape(blocks)
    direct = 4 <= members <= DIRECT_MEMBERS and members & (members - 1) == 0

    base, table = call(
        functools.partial(plan_kernel, direct),
        [IN_SMEM, IN_SMEM, IN_VMEM],
        (floats(2, own_rows, width), floats((3 + spans) * members + 1, width)),
        (failed_ids, generator, previous_parity[0]),
        4 * spans * own_rows * width,
    )
    parity_shape = floats(own_rows, spans * width)
    rebuild_cost = 4 * slab_rows * width
    parity_cost = 2 * spans * slab_rows * width
    if direct:
        rebuilt_shifts, current_shifts = shifts_of(members)
        block = floats(own_rows, width)
        own_earlier, *cut_earlier = cut(earlier, met(members))
        earlier_rows = trade(cut_earlier, partners_of(members), members)
        own_current, *cut_current = cut(current, ahead(members, current_shifts))
        *outgoing, last_current = call(
            rebuild_paired_kernel,
            [IN_VMEM] * (members + 3),
            [block] * (members + 1),
            (base, table, cut_current[-1], own_earlier, *earlier_rows),
            rebuild_cost,
        )
        incoming = pass_on(outgoing[1:], rebuilt_shifts[1:], members)
        cut_current[-1] = last_current
        current_rows = [own_current, *pass_on(cut_current, current_shifts[1:], members)]
        new_parity, restored_state = call(
            finish_kernel,
            [IN_VMEM] * (2 + 2 * members),
            (parity_shape, floats(*blocks)),
            (table, earlier, outgoing[0], *incoming, *current_rows),
            parity_cost,
        )
    else:
        earlier_rows = lax.all_to_all(earlier, "code", 0, 0, tiled=True)
        current_rows = lax.all_to_all(current, "code", 0, 0, tiled=True)
        outgoing = call(
            rebuild_whole_kernel,
            [IN_VMEM] * 3,
            floats(*blocks),
            (base, table, earlier_rows),
            rebuild_cost,
        )
        incoming = lax.all_to_all(outgoing, "code", 0, 0, tiled=True)
        lost = (position == failed_ids[0, 0]) | (position == failed_ids[0, 1])
        restored_state = jnp.where(lost, incoming, earlier)
        new_parity = call(
            parity_whole_kernel,
            [IN_VMEM] * 2,
            parity_shape,
            (table, current_rows),
            parity_cost,
        )
    return (new_parity[None], restored_state.reshape(state_slab.shape))


def solution(mesh):
    placed = (
        P(("grp", "rep"), "code", None, None),
        P(("grp", "rep"), "code", None, None),
        P(("grp", "rep"), "code", None),
        P(),
        P(("grp", "rep"), None),
    )
    return jax.shard_map(
        local,
        mesh=mesh,
        in_specs=placed,
        out_specs=(P(("grp", "rep"), "code", None), P(("grp", "rep"), "code", None, None)),
        check_vma=False,
    )
```

```python
import functools

import jax
import jax.numpy as jnp
from jax import lax
from jax.experimental import pallas as pl
from jax.experimental.pallas import tpu as pltpu
from jax.sharding import PartitionSpec as P

IN_VMEM = pl.BlockSpec(memory_space=pltpu.VMEM)
IN_SMEM = pl.BlockSpec(memory_space=pltpu.SMEM)
ANYWHERE = pl.BlockSpec(memory_space=pl.ANY)

DIRECT_MEMBERS = 8
KERNEL_VMEM = 8 * 2**20


def rounds_of(members):
    return range(members - 1, 0, -1)


def order_of(members, direct):
    if not direct:
        return list(range(members))
    me = lax.axis_index("code")
    return [me ^ r for r in (0, *rounds_of(members))]


def targets_of(members, direct):
    if not direct:
        return list(range(members))
    me = lax.axis_index("code")
    return [lax.rem(me + s, members) for s in range(members)]


def sources_of(members, direct):
    if not direct:
        return list(range(members))
    me = lax.axis_index("code")
    return [lax.rem(me + members - s, members) for s in range(members)]


def plan_kernel(direct, ids_ref, generator_ref, parity_ref, base_ref, table_ref):
    spans, members = generator_ref.shape
    width = base_ref.shape[2]
    first, second = ids_ref[0, 0], ids_ref[0, 1]
    col_first = [generator_ref[j, first] for j in range(spans)]
    col_second = [generator_ref[j, second] for j in range(spans)]
    gram_first = sum(x * x for x in col_first)
    gram_cross = sum(x * y for x, y in zip(col_first, col_second))
    gram_second = sum(y * y for y in col_second)
    determinant = gram_first * gram_second - gram_cross * gram_cross

    def spread(value):
        return jnp.full((1, width), value, jnp.float32)

    def put(row, value):
        table_ref[row : row + 1, :] = value

    over = spread(determinant)
    weights = [
        [spread(gram_second * x - gram_cross * y) / over for x, y in zip(col_first, col_second)],
        [spread(gram_first * y - gram_cross * x) / over for x, y in zip(col_first, col_second)],
    ]
    for k in range(2):
        base_ref[k] = sum(
            weights[k][j] * parity_ref[:, j * width : (j + 1) * width] for j in range(spans)
        )
    for i, c in enumerate(order_of(members, direct)):
        column = [generator_ref[j, c] for j in range(spans)]
        alive = jnp.logical_and(first != c, second != c)
        for k in range(2):
            put(
                k * members + i,
                sum(weights[k][j] * jnp.where(alive, column[j], 0.0) for j in range(spans)),
            )
    for i, c in enumerate(sources_of(members, direct)):
        for j in range(spans):
            put((2 + j) * members + i, spread(generator_ref[j, c]))
    for i, c in enumerate(targets_of(members, direct)):
        put((2 + spans) * members + i, spread(jnp.where(first == c, 1.0, 0.0)))
    me = lax.axis_index("code")
    lost = jnp.logical_or(first == me, second == me)
    put((3 + spans) * members, spread(jnp.where(lost, 1.0, 0.0)))


def weigh(table_ref, start, rows):
    total = None
    for i, block in enumerate(rows):
        term = table_ref[start + i : start + i + 1, :] * block
        total = term if total is None else total + term
    return total


def rebuilt_for(base_ref, table_ref, rows):
    members = len(rows)
    rebuilt = [base_ref[k] - weigh(table_ref, k * members, rows) for k in range(2)]
    picks = table_ref.shape[0] - 1 - members
    return [
        jnp.where(table_ref[picks + i : picks + i + 1, :] > 0.5, *rebuilt) for i in range(members)
    ]


def rebuild_whole_kernel(base_ref, table_ref, rows_ref, out_ref):
    rows = [rows_ref[c] for c in range(rows_ref.shape[0])]
    for c, block in enumerate(rebuilt_for(base_ref, table_ref, rows)):
        out_ref[c] = block


def parity_whole_kernel(table_ref, rows_ref, out_ref):
    parity_into(out_ref, table_ref, [rows_ref[c] for c in range(rows_ref.shape[0])])


def parity_into(out_ref, table_ref, rows):
    members, width = len(rows), table_ref.shape[1]
    for j in range(out_ref.shape[1] // width):
        out_ref[:, j * width : (j + 1) * width] = weigh(table_ref, (2 + j) * members, rows)


def rebuild_paired_kernel(base_ref, table_ref, *refs):
    rows, outs = refs[: len(refs) // 2], refs[len(refs) // 2 :]
    for out_ref, block in zip(outs, rebuilt_for(base_ref, table_ref, [r[...] for r in rows])):
        out_ref[...] = block


def parity_paired_kernel(table_ref, *refs):
    rows, out_ref, done_ref = refs[:-2], refs[-2], refs[-1]
    parity_into(out_ref, table_ref, [r[...] for r in rows])
    done_ref[...] = jnp.zeros(done_ref.shape, done_ref.dtype)


def restore_kernel(table_ref, earlier_ref, held_back_by, *refs):
    pieces, out_ref = refs[:-1], refs[-1]
    members = len(pieces)
    last = table_ref.shape[0] - 1
    lost = table_ref[last : last + 1, :] > 0.5
    for c, piece in zip(sources_of(members, True), pieces):
        out_ref[c] = jnp.where(lost, piece[...], earlier_ref[c])


def call(kernel, specs, outs, args, flops, **options):
    total = sum(x.size for x in args) + sum(o.size for o in jax.tree.leaves(outs))
    return pl.pallas_call(
        kernel,
        in_specs=specs,
        out_specs=jax.tree.map(lambda _: IN_VMEM, outs),
        out_shape=outs,
        compiler_params=pltpu.CompilerParams(vmem_limit_bytes=KERNEL_VMEM),
        cost_estimate=pl.CostEstimate(flops=flops, bytes_accessed=4 * total, transcendentals=0),
        **options,
    )(*args)


def floats(*shape):
    return jax.ShapeDtypeStruct(shape, jnp.float32)


def pass_on(pieces, members):
    return [
        lax.ppermute(piece, "code", [(d, (d + s) % members) for d in range(members)])
        for s, piece in enumerate(pieces, 1)
    ]


def trade(pieces, rounds, members):
    return [
        lax.ppermute(piece, "code", [(d, d ^ r) for d in range(members)])
        for r, piece in zip(rounds, pieces)
    ]


def cut(blocks, order):
    return [lax.dynamic_index_in_dim(blocks, c, 0, keepdims=False) for c in order]


def local(state_slab, previous_slab, previous_parity, generator, failed_ids):
    position = lax.axis_index("code")
    members = lax.axis_size("code")
    slab_rows, width = state_slab.shape[2:]
    spans = generator.shape[0]
    own_rows = slab_rows // members
    blocks = (members, own_rows, width)
    earlier = previous_slab.reshape(blocks)
    current = state_slab.reshape(blocks)
    direct = 4 <= members <= DIRECT_MEMBERS and members & (members - 1) == 0

    base, table = call(
        functools.partial(plan_kernel, direct),
        [IN_SMEM, IN_SMEM, IN_VMEM],
        (floats(2, own_rows, width), floats((3 + spans) * members + 1, width)),
        (failed_ids, generator, previous_parity[0]),
        4 * spans * own_rows * width,
    )
    parity_shape = floats(own_rows, spans * width)
    rebuild_cost = 4 * slab_rows * width
    parity_cost = 2 * spans * slab_rows * width
    if direct:
        rounds = list(rounds_of(members))
        block = floats(own_rows, width)
        own_earlier, *cut_earlier = cut(earlier, order_of(members, True))
        earlier_rows = trade(cut_earlier, rounds, members)
        current, table = lax.optimization_barrier((current, table))
        own_current, *cut_current = cut(current, targets_of(members, True))
        outgoing = call(
            rebuild_paired_kernel,
            [IN_VMEM] * (members + 2),
            [block] * members,
            (base, table, own_earlier, *earlier_rows),
            rebuild_cost,
        )
        incoming = pass_on(outgoing[1:], members)
        current_rows = [own_current, *pass_on(cut_current, members)]
        new_parity, parity_done = call(
            parity_paired_kernel,
            [IN_VMEM] * (members + 1),
            (parity_shape, floats(8, 128)),
            (table, *current_rows),
            parity_cost,
        )
        restored_state = call(
            restore_kernel,
            [IN_VMEM, IN_VMEM, ANYWHERE] + [IN_VMEM] * members,
            floats(*blocks),
            (table, earlier, parity_done, outgoing[0], *incoming),
            0,
        )
    else:
        earlier_rows = lax.all_to_all(earlier, "code", 0, 0, tiled=True)
        current_rows = lax.all_to_all(current, "code", 0, 0, tiled=True)
        outgoing = call(
            rebuild_whole_kernel,
            [IN_VMEM] * 3,
            floats(*blocks),
            (base, table, earlier_rows),
            rebuild_cost,
        )
        incoming = lax.all_to_all(outgoing, "code", 0, 0, tiled=True)
        lost = (position == failed_ids[0, 0]) | (position == failed_ids[0, 1])
        restored_state = jnp.where(lost, incoming, earlier)
        new_parity = call(
            parity_whole_kernel,
            [IN_VMEM] * 2,
            parity_shape,
            (table, current_rows),
            parity_cost,
        )
    return (new_parity[None], restored_state.reshape(state_slab.shape))


def solution(mesh):
    placed = (
        P(("grp", "rep"), "code", None, None),
        P(("grp", "rep"), "code", None, None),
        P(("grp", "rep"), "code", None),
        P(),
        P(("grp", "rep"), None),
    )
    return jax.shard_map(
        local,
        mesh=mesh,
        in_specs=placed,
        out_specs=(P(("grp", "rep"), "code", None), P(("grp", "rep"), "code", None, None)),
        check_vma=False,
    )
```

```python
import functools

import jax
import jax.numpy as jnp
from jax import lax
from jax.experimental import pallas as pl
from jax.experimental.pallas import tpu as pltpu
from jax.sharding import PartitionSpec as P

IN_VMEM = pl.BlockSpec(memory_space=pltpu.VMEM)
IN_SMEM = pl.BlockSpec(memory_space=pltpu.SMEM)
ANYWHERE = pl.BlockSpec(memory_space=pl.ANY)

KERNEL_VMEM = 8 * 2**20

PAIRED_MEMBERS = 4
PARTNERS = (0, 1, 2, 3)


def partners():
    me = lax.axis_index("code")
    return [me ^ r for r in PARTNERS]


def plan_kernel(paired, ids_ref, generator_ref, parity_ref, base_ref, table_ref):
    spans, members = generator_ref.shape
    width = base_ref.shape[2]
    first, second = ids_ref[0, 0], ids_ref[0, 1]
    col_first = [generator_ref[j, first] for j in range(spans)]
    col_second = [generator_ref[j, second] for j in range(spans)]
    gram_first = sum(x * x for x in col_first)
    gram_cross = sum(x * y for x, y in zip(col_first, col_second))
    gram_second = sum(y * y for y in col_second)
    determinant = gram_first * gram_second - gram_cross * gram_cross

    def spread(value):
        return jnp.full((1, width), value, jnp.float32)

    def put(row, value):
        table_ref[row : row + 1, :] = value

    over = spread(determinant)
    weights = [
        [spread(gram_second * x - gram_cross * y) / over for x, y in zip(col_first, col_second)],
        [spread(gram_first * y - gram_cross * x) / over for x, y in zip(col_first, col_second)],
    ]
    for k in range(2):
        base_ref[k] = sum(
            weights[k][j] * parity_ref[:, j * width : (j + 1) * width] for j in range(spans)
        )
    for i, c in enumerate(partners() if paired else range(members)):
        column = [generator_ref[j, c] for j in range(spans)]
        alive = jnp.logical_and(first != c, second != c)
        for k in range(2):
            put(
                k * members + i,
                sum(weights[k][j] * jnp.where(alive, column[j], 0.0) for j in range(spans)),
            )
        for j in range(spans):
            put((2 + j) * members + i, spread(column[j]))
        put((2 + spans) * members + i, spread(jnp.where(first == c, 1.0, 0.0)))
    me = lax.axis_index("code")
    lost = jnp.logical_or(first == me, second == me)
    put((3 + spans) * members, spread(jnp.where(lost, 1.0, 0.0)))


def weigh(table_ref, start, rows):
    total = None
    for i, block in enumerate(rows):
        term = table_ref[start + i : start + i + 1, :] * block
        total = term if total is None else total + term
    return total


def rebuilt_for(base_ref, table_ref, rows):
    members = len(rows)
    rebuilt = [base_ref[k] - weigh(table_ref, k * members, rows) for k in range(2)]
    picks = table_ref.shape[0] - 1 - members
    return [
        jnp.where(table_ref[picks + i : picks + i + 1, :] > 0.5, *rebuilt) for i in range(members)
    ]


def rebuild_whole_kernel(base_ref, table_ref, rows_ref, out_ref):
    rows = [rows_ref[c] for c in range(rows_ref.shape[0])]
    for c, block in enumerate(rebuilt_for(base_ref, table_ref, rows)):
        out_ref[c] = block


def parity_whole_kernel(table_ref, rows_ref, out_ref):
    parity_into(out_ref, table_ref, [rows_ref[c] for c in range(rows_ref.shape[0])])


def parity_into(out_ref, table_ref, rows):
    members, width = len(rows), table_ref.shape[1]
    for j in range(out_ref.shape[1] // width):
        out_ref[:, j * width : (j + 1) * width] = weigh(table_ref, (2 + j) * members, rows)


def rebuild_paired_kernel(base_ref, table_ref, *refs):
    rows, current_ref, outs = refs[:4], refs[4], refs[5:]
    rebuilt = rebuilt_for(base_ref, table_ref, [r[...] for r in rows])
    for out_ref, block in zip(outs, rebuilt + rebuilt[2:]):
        out_ref[...] = block
    outs[6][...] = current_ref[...]


def finish_kernel(table_ref, earlier_ref, *refs):
    (
        rebuilt_3_outer,
        rebuilt_2_even,
        rebuilt_1,
        rebuilt_3_inner,
        rebuilt_2_odd,
        current_2_odd,
        rebuilt_own,
        current_own,
        current_1,
        current_2_even,
        current_3,
        parity_ref,
        out_ref,
    ) = refs
    current = [
        current_own[...],
        current_1[...],
        current_2_even[...] + current_2_odd[...],
        current_3[...],
    ]
    rebuilt = [
        rebuilt_own[...],
        rebuilt_1[...],
        rebuilt_2_even[...] + rebuilt_2_odd[...],
        rebuilt_3_outer[...] + rebuilt_3_inner[...],
    ]
    parity_into(parity_ref, table_ref, current)
    last = table_ref.shape[0] - 1
    lost = table_ref[last : last + 1, :] > 0.5
    for c, block in zip(partners(), rebuilt):
        out_ref[c] = jnp.where(lost, block, earlier_ref[c])


def call(kernel, specs, outs, args, flops, **options):
    total = sum(x.size for x in args) + sum(o.size for o in jax.tree.leaves(outs))
    return pl.pallas_call(
        kernel,
        in_specs=specs,
        out_specs=jax.tree.map(lambda _: IN_VMEM, outs),
        out_shape=outs,
        compiler_params=pltpu.CompilerParams(vmem_limit_bytes=KERNEL_VMEM),
        cost_estimate=pl.CostEstimate(flops=flops, bytes_accessed=4 * total, transcendentals=0),
        **options,
    )(*args)


def floats(*shape):
    return jax.ShapeDtypeStruct(shape, jnp.float32)


def swap(piece, *pairs):
    both_ways = [way for a, b in pairs for way in ((a, b), (b, a))]
    return lax.ppermute(piece, "code", both_ways)


def cut(blocks, order):
    return [lax.dynamic_index_in_dim(blocks, c, 0, keepdims=False) for c in order]


def local(state_slab, previous_slab, previous_parity, generator, failed_ids):
    position = lax.axis_index("code")
    members = lax.axis_size("code")
    slab_rows, width = state_slab.shape[2:]
    spans = generator.shape[0]
    own_rows = slab_rows // members
    blocks = (members, own_rows, width)
    earlier = previous_slab.reshape(blocks)
    current = state_slab.reshape(blocks)
    paired = members == PAIRED_MEMBERS

    base, table = call(
        functools.partial(plan_kernel, paired),
        [IN_SMEM, IN_SMEM, IN_VMEM],
        (floats(2, own_rows, width), floats((3 + spans) * members + 1, width)),
        (failed_ids, generator, previous_parity[0]),
        4 * spans * own_rows * width,
    )
    parity_shape = floats(own_rows, spans * width)
    rebuild_cost = 4 * slab_rows * width
    parity_cost = 2 * spans * slab_rows * width
    if paired:
        block, stack = floats(own_rows, width), floats(2, own_rows, width)
        own_earlier, earlier_1, earlier_2, earlier_3 = cut(earlier, partners())
        earlier_rows = [
            own_earlier,
            swap(earlier_1, (0, 1), (2, 3)),
            swap(earlier_2, (0, 2), (1, 3)),
            swap(earlier_3, (0, 3), (1, 2)),
        ]
        own_current, current_1, current_2, current_3 = cut(current, partners())
        current_3 = swap(current_3, (0, 3), (1, 2))
        current_2_even = swap(current_2, (0, 2))
        current_1 = swap(current_1, (0, 1), (2, 3))
        (
            rebuilt_own,
            rebuilt_1,
            rebuilt_2_even,
            rebuilt_3_outer,
            rebuilt_2_odd,
            rebuilt_3_inner,
            current_2_odd,
        ) = call(
            rebuild_paired_kernel,
            [IN_VMEM] * 7,
            [block] * 7,
            (base, table, *earlier_rows, current_2),
            rebuild_cost,
        )
        new_parity, restored_state = call(
            finish_kernel,
            [IN_VMEM] * 13,
            (parity_shape, floats(*blocks)),
            (
                table,
                earlier,
                swap(rebuilt_3_outer, (0, 3)),
                swap(rebuilt_2_even, (0, 2)),
                swap(rebuilt_1, (0, 1), (2, 3)),
                swap(rebuilt_3_inner, (1, 2)),
                swap(rebuilt_2_odd, (1, 3)),
                swap(current_2_odd, (1, 3)),
                rebuilt_own,
                own_current,
                current_1,
                current_2_even,
                current_3,
            ),
            parity_cost,
        )
    else:
        earlier_rows = lax.all_to_all(earlier, "code", 0, 0, tiled=True)
        current_rows = lax.all_to_all(current, "code", 0, 0, tiled=True)
        outgoing = call(
            rebuild_whole_kernel,
            [IN_VMEM] * 3,
            floats(*blocks),
            (base, table, earlier_rows),
            rebuild_cost,
        )
        incoming = lax.all_to_all(outgoing, "code", 0, 0, tiled=True)
        lost = (position == failed_ids[0, 0]) | (position == failed_ids[0, 1])
        restored_state = jnp.where(lost, incoming, earlier)
        new_parity = call(
            parity_whole_kernel,
            [IN_VMEM] * 2,
            parity_shape,
            (table, current_rows),
            parity_cost,
        )
    return (new_parity[None], restored_state.reshape(state_slab.shape))


def solution(mesh):
    placed = (
        P(("grp", "rep"), "code", None, None),
        P(("grp", "rep"), "code", None, None),
        P(("grp", "rep"), "code", None),
        P(),
        P(("grp", "rep"), None),
    )
    return jax.shard_map(
        local,
        mesh=mesh,
        in_specs=placed,
        out_specs=(P(("grp", "rep"), "code", None), P(("grp", "rep"), "code", None, None)),
        check_vma=False,
    )
```

```python
import functools

import jax
import jax.numpy as jnp
from jax import lax
from jax.experimental import pallas as pl
from jax.experimental.pallas import tpu as pltpu
from jax.sharding import PartitionSpec as P

IN_VMEM = pl.BlockSpec(memory_space=pltpu.VMEM)
IN_SMEM = pl.BlockSpec(memory_space=pltpu.SMEM)
ANYWHERE = pl.BlockSpec(memory_space=pl.ANY)

PAIRED_MEMBERS = 4
SHIFTS = (0, 1, 2, 3)
KERNEL_VMEM = 8 * 2**20


def rounds_of(members):
    return range(1, members)


def order_of(members, direct):
    if not direct:
        return list(range(members))
    me = lax.axis_index("code")
    return [me ^ r for r in (0, *rounds_of(members))]


def targets_of(members, direct):
    if not direct:
        return list(range(members))
    me = lax.axis_index("code")
    return [lax.rem(me + s, members) for s in SHIFTS]


def sources_of(members, direct):
    if not direct:
        return list(range(members))
    me = lax.axis_index("code")
    return [lax.rem(me + members - s, members) for s in SHIFTS]


NEXT = (1, 0, 3, 2)
IN_ONE_HALF = ((3, 2, 1, 0), (2, 3, 0, 1), NEXT)
DELIVERIES = {
    (0, 1): IN_ONE_HALF,
    (2, 3): IN_ONE_HALF,
    (0, 2): ((1, 2, 3, 0), (2, 1, 0, 3), NEXT),
    (1, 3): ((3, 0, 1, 2), (0, 3, 2, 1), NEXT),
    (0, 3): ((3, 1, 2, 0), (1, 3, 0, 2), NEXT),
    (1, 2): ((0, 2, 1, 3), (2, 0, 3, 1), NEXT),
}
WAYS = sorted(set(DELIVERIES.values()))


def way_codes():
    members = range(PAIRED_MEMBERS)
    codes = [
        WAYS.index(DELIVERIES[min(a, b), max(a, b)]) if a != b else 0
        for a in members
        for b in members
    ]
    for way in WAYS:
        for me in members:
            codes += [targets[me] for targets in way]
            codes += [targets.index(me) for targets in way]
    return codes


def plan_kernel(direct, ids_ref, generator_ref, codes_ref, parity_ref, *outs):
    base_ref, table_ref = outs[:2]
    spans, members = generator_ref.shape
    width = base_ref.shape[2]
    first, second = ids_ref[0, 0], ids_ref[0, 1]
    col_first = [generator_ref[j, first] for j in range(spans)]
    col_second = [generator_ref[j, second] for j in range(spans)]
    gram_first = sum(x * x for x in col_first)
    gram_cross = sum(x * y for x, y in zip(col_first, col_second))
    gram_second = sum(y * y for y in col_second)
    determinant = gram_first * gram_second - gram_cross * gram_cross

    def spread(value):
        return jnp.full((1, width), value, jnp.float32)

    def put(row, value):
        table_ref[row : row + 1, :] = value

    over = spread(determinant)
    weights = [
        [spread(gram_second * x - gram_cross * y) / over for x, y in zip(col_first, col_second)],
        [spread(gram_first * y - gram_cross * x) / over for x, y in zip(col_first, col_second)],
    ]
    for k in range(2):
        base_ref[k] = sum(
            weights[k][j] * parity_ref[:, j * width : (j + 1) * width] for j in range(spans)
        )
    for i, c in enumerate(order_of(members, direct)):
        column = [generator_ref[j, c] for j in range(spans)]
        alive = jnp.logical_and(first != c, second != c)
        for k in range(2):
            put(
                k * members + i,
                sum(weights[k][j] * jnp.where(alive, column[j], 0.0) for j in range(spans)),
            )
    for i, c in enumerate(sources_of(members, direct)):
        for j in range(spans):
            put((2 + j) * members + i, spread(generator_ref[j, c]))
    me = lax.axis_index("code")
    targets = range(members)
    if direct:
        way = codes_ref[first * members + second]
        outs[2][0] = way
        rounds = members - 1
        start = members * members + (way * members + me) * 2 * rounds
        targets = [me] + [codes_ref[start + r] for r in range(rounds)]
        for r in range(rounds):
            source = codes_ref[start + rounds + r]
            for c in range(members):
                put((3 + spans + r) * members + c, spread(jnp.where(source == c, 1.0, 0.0)))
    for i, c in enumerate(targets):
        put((2 + spans) * members + i, spread(jnp.where(first == c, 1.0, 0.0)))
    lost = jnp.logical_or(first == me, second == me)
    put(table_ref.shape[0] - 1, spread(jnp.where(lost, 1.0, 0.0)))


def weigh(table_ref, start, rows):
    total = None
    for i, block in enumerate(rows):
        term = table_ref[start + i : start + i + 1, :] * block
        total = term if total is None else total + term
    return total


def rebuilt_for(spans, base_ref, table_ref, rows):
    members = len(rows)
    rebuilt = [base_ref[k] - weigh(table_ref, k * members, rows) for k in range(2)]
    picks = (2 + spans) * members
    return [
        jnp.where(table_ref[picks + i : picks + i + 1, :] > 0.5, *rebuilt) for i in range(members)
    ]


def rebuild_whole_kernel(spans, base_ref, table_ref, rows_ref, out_ref):
    rows = [rows_ref[c] for c in range(rows_ref.shape[0])]
    for c, block in enumerate(rebuilt_for(spans, base_ref, table_ref, rows)):
        out_ref[c] = block


def parity_whole_kernel(table_ref, rows_ref, out_ref):
    parity_into(out_ref, table_ref, [rows_ref[c] for c in range(rows_ref.shape[0])])


def parity_into(out_ref, table_ref, rows):
    members, width = len(rows), table_ref.shape[1]
    for j in range(out_ref.shape[1] // width):
        out_ref[:, j * width : (j + 1) * width] = weigh(table_ref, (2 + j) * members, rows)


def rebuild_paired_kernel(spans, held_back_by, base_ref, table_ref, *refs):
    rows, outs = refs[: len(refs) // 2], refs[len(refs) // 2 :]
    for out_ref, block in zip(outs, rebuilt_for(spans, base_ref, table_ref, [r[...] for r in rows])):
        out_ref[...] = block


def finish_kernel(table_ref, earlier_ref, *refs):
    members = (len(refs) - 2) // 2
    rows, pieces, (parity_ref, out_ref) = refs[:members], refs[members:-2], refs[-2:]
    parity_into(parity_ref, table_ref, [r[...] for r in rows])
    last = table_ref.shape[0] - 1
    lost = table_ref[last : last + 1, :] > 0.5
    arrivals = last - (members - 1) * members
    for c in range(members):
        block = pieces[0][...]
        for r, piece in enumerate(pieces[1:]):
            i = arrivals + r * members + c
            block = jnp.where(table_ref[i : i + 1, :] > 0.5, piece[...], block)
        out_ref[c] = jnp.where(lost, block, earlier_ref[c])


def call(kernel, specs, outs, args, flops, **options):
    total = sum(x.size for x in args) + sum(o.size for o in jax.tree.leaves(outs))
    options.setdefault("out_specs", jax.tree.map(lambda _: IN_VMEM, outs))
    return pl.pallas_call(
        kernel,
        in_specs=specs,
        out_shape=outs,
        compiler_params=pltpu.CompilerParams(vmem_limit_bytes=KERNEL_VMEM),
        cost_estimate=pl.CostEstimate(flops=flops, bytes_accessed=4 * total, transcendentals=0),
        **options,
    )(*args)


def floats(*shape):
    return jax.ShapeDtypeStruct(shape, jnp.float32)


def pass_on(pieces, members):
    return [
        lax.ppermute(piece, "code", [(d, (d + s) % members) for d in range(members)])
        for s, piece in zip(SHIFTS[1:], pieces)
    ]


def trade(pieces, rounds, members):
    return [
        lax.ppermute(piece, "code", [(d, d ^ r) for d in range(members)])
        for r, piece in zip(rounds, pieces)
    ]


def deliver(way, *pieces):
    return tuple(lax.ppermute(p, "code", list(enumerate(t))) for p, t in zip(pieces, way))


def cut(blocks, order):
    return [lax.dynamic_index_in_dim(blocks, c, 0, keepdims=False) for c in order]


def local(state_slab, previous_slab, previous_parity, generator, failed_ids):
    position = lax.axis_index("code")
    members = lax.axis_size("code")
    slab_rows, width = state_slab.shape[2:]
    spans = generator.shape[0]
    own_rows = slab_rows // members
    blocks = (members, own_rows, width)
    earlier = previous_slab.reshape(blocks)
    current = state_slab.reshape(blocks)
    direct = members == PAIRED_MEMBERS

    codes = jnp.array(way_codes() if direct else [0], jnp.int32)
    arrivals = members * (members - 1) if direct else 0
    plan_outs = [
        floats(2, own_rows, width),
        floats((3 + spans) * members + arrivals + 1, width),
        jax.ShapeDtypeStruct((1,), jnp.int32),
    ]
    base, table, way = call(
        functools.partial(plan_kernel, direct),
        [IN_SMEM, IN_SMEM, IN_SMEM, IN_VMEM],
        plan_outs,
        (failed_ids, generator, codes, previous_parity[0]),
        4 * spans * own_rows * width,
        out_specs=[IN_VMEM, IN_VMEM, IN_SMEM],
    )
    parity_shape = floats(own_rows, spans * width)
    rebuild_cost = 4 * slab_rows * width
    parity_cost = 2 * spans * slab_rows * width
    if direct:
        rounds = list(rounds_of(members))
        block = floats(own_rows, width)
        own_earlier, *cut_earlier = cut(earlier, order_of(members, True))
        earlier_rows = trade(cut_earlier, rounds, members)
        current, earlier_rows[-1] = lax.optimization_barrier((current, earlier_rows[-1]))
        own_current, *cut_current = cut(current, targets_of(members, True))
        current_rows = [own_current, *pass_on(cut_current, members)]
        outgoing = call(
            functools.partial(rebuild_paired_kernel, spans),
            [ANYWHERE] + [IN_VMEM] * (members + 2),
            [block] * members,
            (current_rows[1], base, table, own_earlier, *earlier_rows),
            rebuild_cost,
        )
        deliveries = [functools.partial(deliver, w) for w in WAYS]
        incoming = lax.switch(way[0], deliveries, *outgoing[1:])
        new_parity, restored_state = call(
            finish_kernel,
            [IN_VMEM] * (2 + 2 * members),
            (parity_shape, floats(*blocks)),
            (table, earlier, *current_rows, outgoing[0], *incoming),
            parity_cost,
        )
    else:
        earlier_rows = lax.all_to_all(earlier, "code", 0, 0, tiled=True)
        current_rows = lax.all_to_all(current, "code", 0, 0, tiled=True)
        outgoing = call(
            functools.partial(rebuild_whole_kernel, spans),
            [IN_VMEM] * 3,
            floats(*blocks),
            (base, table, earlier_rows),
            rebuild_cost,
        )
        incoming = lax.all_to_all(outgoing, "code", 0, 0, tiled=True)
        lost = (position == failed_ids[0, 0]) | (position == failed_ids[0, 1])
        restored_state = jnp.where(lost, incoming, earlier)
        new_parity = call(
            parity_whole_kernel,
            [IN_VMEM] * 2,
            parity_shape,
            (table, current_rows),
            parity_cost,
        )
    return (new_parity[None], restored_state.reshape(state_slab.shape))


def solution(mesh):
    placed = (
        P(("grp", "rep"), "code", None, None),
        P(("grp", "rep"), "code", None, None),
        P(("grp", "rep"), "code", None),
        P(),
        P(("grp", "rep"), None),
    )
    return jax.shard_map(
        local,
        mesh=mesh,
        in_specs=placed,
        out_specs=(P(("grp", "rep"), "code", None), P(("grp", "rep"), "code", None, None)),
        check_vma=False,
    )
```

```python
import functools

import jax
import jax.numpy as jnp
from jax import lax
from jax.experimental import pallas as pl
from jax.experimental.pallas import tpu as pltpu
from jax.sharding import PartitionSpec as P

IN_VMEM = pl.BlockSpec(memory_space=pltpu.VMEM)
IN_SMEM = pl.BlockSpec(memory_space=pltpu.SMEM)
ANYWHERE = pl.BlockSpec(memory_space=pl.ANY)

PAIRED_MEMBERS = 4
KERNEL_VMEM = 8 * 2**20


def rounds_of(members):
    return range(1, members)


def order_of(members, direct):
    if not direct:
        return list(range(members))
    me = lax.axis_index("code")
    return [me ^ r for r in (0, *rounds_of(members))]


NEXT = (1, 0, 3, 2)
IN_ONE_HALF = ((3, 2, 1, 0), (2, 3, 0, 1), NEXT)
DELIVERIES = {
    (0, 1): IN_ONE_HALF,
    (2, 3): IN_ONE_HALF,
    (0, 2): ((1, 2, 3, 0), (2, 1, 0, 3), NEXT),
    (1, 3): ((3, 0, 1, 2), (0, 3, 2, 1), NEXT),
    (0, 3): ((3, 1, 2, 0), (1, 3, 0, 2), NEXT),
    (1, 2): ((0, 2, 1, 3), (2, 0, 3, 1), NEXT),
}
WAYS = sorted(set(DELIVERIES.values()))


def way_codes():
    members = range(PAIRED_MEMBERS)
    codes = [
        WAYS.index(DELIVERIES[min(a, b), max(a, b)]) if a != b else 0
        for a in members
        for b in members
    ]
    for way in WAYS:
        for me in members:
            codes += [targets[me] for targets in way]
            codes += [targets.index(me) for targets in way]
    return codes


def plan_kernel(direct, ids_ref, generator_ref, codes_ref, parity_ref, *outs):
    base_ref, table_ref = outs[:2]
    spans, members = generator_ref.shape
    width = base_ref.shape[2]
    first, second = ids_ref[0, 0], ids_ref[0, 1]
    col_first = [generator_ref[j, first] for j in range(spans)]
    col_second = [generator_ref[j, second] for j in range(spans)]
    gram_first = sum(x * x for x in col_first)
    gram_cross = sum(x * y for x, y in zip(col_first, col_second))
    gram_second = sum(y * y for y in col_second)
    determinant = gram_first * gram_second - gram_cross * gram_cross

    def spread(value):
        return jnp.full((1, width), value, jnp.float32)

    def put(row, value):
        table_ref[row : row + 1, :] = value

    over = spread(determinant)
    weights = [
        [spread(gram_second * x - gram_cross * y) / over for x, y in zip(col_first, col_second)],
        [spread(gram_first * y - gram_cross * x) / over for x, y in zip(col_first, col_second)],
    ]
    for k in range(2):
        base_ref[k] = sum(
            weights[k][j] * parity_ref[:, j * width : (j + 1) * width] for j in range(spans)
        )
    for i, c in enumerate(order_of(members, direct)):
        column = [generator_ref[j, c] for j in range(spans)]
        alive = jnp.logical_and(first != c, second != c)
        for k in range(2):
            put(
                k * members + i,
                sum(weights[k][j] * jnp.where(alive, column[j], 0.0) for j in range(spans)),
            )
        for j in range(spans):
            put((2 + j) * members + i, spread(column[j]))
    me = lax.axis_index("code")
    targets = range(members)
    if direct:
        way = codes_ref[first * members + second]
        outs[2][0] = way
        rounds = members - 1
        start = members * members + (way * members + me) * 2 * rounds
        targets = [me] + [codes_ref[start + r] for r in range(rounds)]
        for r in range(rounds):
            source = codes_ref[start + rounds + r]
            for c in range(members):
                put((3 + spans + r) * members + c, spread(jnp.where(source == c, 1.0, 0.0)))
    for i, c in enumerate(targets):
        put((2 + spans) * members + i, spread(jnp.where(first == c, 1.0, 0.0)))
    lost = jnp.logical_or(first == me, second == me)
    put(table_ref.shape[0] - 1, spread(jnp.where(lost, 1.0, 0.0)))


def weigh(table_ref, start, rows):
    total = None
    for i, block in enumerate(rows):
        term = table_ref[start + i : start + i + 1, :] * block
        total = term if total is None else total + term
    return total


def rebuilt_for(spans, base_ref, table_ref, rows):
    members = len(rows)
    rebuilt = [base_ref[k] - weigh(table_ref, k * members, rows) for k in range(2)]
    picks = (2 + spans) * members
    return [
        jnp.where(table_ref[picks + i : picks + i + 1, :] > 0.5, *rebuilt) for i in range(members)
    ]


def rebuild_whole_kernel(spans, base_ref, table_ref, rows_ref, out_ref):
    rows = [rows_ref[c] for c in range(rows_ref.shape[0])]
    for c, block in enumerate(rebuilt_for(spans, base_ref, table_ref, rows)):
        out_ref[c] = block


def parity_whole_kernel(table_ref, rows_ref, out_ref):
    parity_into(out_ref, table_ref, [rows_ref[c] for c in range(rows_ref.shape[0])])


def parity_into(out_ref, table_ref, rows):
    members, width = len(rows), table_ref.shape[1]
    for j in range(out_ref.shape[1] // width):
        out_ref[:, j * width : (j + 1) * width] = weigh(table_ref, (2 + j) * members, rows)


def rebuild_paired_kernel(spans, base_ref, table_ref, current_ref, *refs):
    rows, outs = refs[: len(refs) // 2], refs[len(refs) // 2 :]
    blocks = rebuilt_for(spans, base_ref, table_ref, [r[...] for r in rows])
    for out_ref, block in zip(outs[:-1], blocks):
        out_ref[...] = block
    outs[-1][0] = blocks[-1]
    outs[-1][1] = current_ref[...]


def finish_kernel(table_ref, earlier_ref, *refs):
    *inputs, parity_ref, out_ref = refs
    members = len(inputs) // 2 + 1
    rows, pieces, both_ref = inputs[: members - 1], inputs[members - 1 : -1], inputs[-1]
    rows = [rows[0][...], both_ref[1], *(r[...] for r in rows[1:])]
    pieces = [*(p[...] for p in pieces), both_ref[0]]
    parity_into(parity_ref, table_ref, rows)
    last = table_ref.shape[0] - 1
    lost = table_ref[last : last + 1, :] > 0.5
    arrivals = last - (members - 1) * members
    for c in range(members):
        block = pieces[0]
        for r, piece in enumerate(pieces[1:]):
            i = arrivals + r * members + c
            block = jnp.where(table_ref[i : i + 1, :] > 0.5, piece, block)
        out_ref[c] = jnp.where(lost, block, earlier_ref[c])


def call(kernel, specs, outs, args, flops, **options):
    total = sum(x.size for x in args) + sum(o.size for o in jax.tree.leaves(outs))
    options.setdefault("out_specs", jax.tree.map(lambda _: IN_VMEM, outs))
    return pl.pallas_call(
        kernel,
        in_specs=specs,
        out_shape=outs,
        compiler_params=pltpu.CompilerParams(vmem_limit_bytes=KERNEL_VMEM),
        cost_estimate=pl.CostEstimate(flops=flops, bytes_accessed=4 * total, transcendentals=0),
        **options,
    )(*args)


def floats(*shape):
    return jax.ShapeDtypeStruct(shape, jnp.float32)


def trade(pieces, rounds, members):
    return [
        lax.ppermute(piece, "code", [(d, d ^ r) for d in range(members)])
        for r, piece in zip(rounds, pieces)
    ]


def deliver(way, *pieces):
    return tuple(lax.ppermute(p, "code", list(enumerate(t))) for p, t in zip(pieces, way))


def cut(blocks, order):
    return [lax.dynamic_index_in_dim(blocks, c, 0, keepdims=False) for c in order]


def local(state_slab, previous_slab, previous_parity, generator, failed_ids):
    position = lax.axis_index("code")
    members = lax.axis_size("code")
    slab_rows, width = state_slab.shape[2:]
    spans = generator.shape[0]
    own_rows = slab_rows // members
    blocks = (members, own_rows, width)
    earlier = previous_slab.reshape(blocks)
    current = state_slab.reshape(blocks)
    direct = members == PAIRED_MEMBERS

    codes = jnp.array(way_codes() if direct else [0], jnp.int32)
    arrivals = members * (members - 1) if direct else 0
    plan_outs = [
        floats(2, own_rows, width),
        floats((3 + spans) * members + arrivals + 1, width),
        jax.ShapeDtypeStruct((1,), jnp.int32),
    ]
    base, table, way = call(
        functools.partial(plan_kernel, direct),
        [IN_SMEM, IN_SMEM, IN_SMEM, IN_VMEM],
        plan_outs,
        (failed_ids, generator, codes, previous_parity[0]),
        4 * spans * own_rows * width,
        out_specs=[IN_VMEM, IN_VMEM, IN_SMEM],
    )
    parity_shape = floats(own_rows, spans * width)
    rebuild_cost = 4 * slab_rows * width
    parity_cost = 2 * spans * slab_rows * width
    if direct:
        rounds = list(rounds_of(members))
        block = floats(own_rows, width)
        own_earlier, *cut_earlier = cut(earlier, order_of(members, True))
        earlier_rows = trade(cut_earlier, rounds, members)
        current, table = lax.optimization_barrier((current, table))
        own_current, next_current, *cut_current = cut(current, order_of(members, True))
        current_rows = [own_current, *trade(cut_current, rounds[1:], members)]
        outgoing = call(
            functools.partial(rebuild_paired_kernel, spans),
            [IN_VMEM] * (members + 3),
            [block] * (members - 1) + [floats(2, own_rows, width)],
            (base, table, next_current, own_earlier, *earlier_rows),
            rebuild_cost,
        )
        deliveries = [functools.partial(deliver, w) for w in WAYS]
        incoming = lax.switch(way[0], deliveries, *outgoing[1:])
        new_parity, restored_state = call(
            finish_kernel,
            [IN_VMEM] * (2 * members + 1),
            (parity_shape, floats(*blocks)),
            (table, earlier, *current_rows, outgoing[0], *incoming),
            parity_cost,
        )
    else:
        earlier_rows = lax.all_to_all(earlier, "code", 0, 0, tiled=True)
        current_rows = lax.all_to_all(current, "code", 0, 0, tiled=True)
        outgoing = call(
            functools.partial(rebuild_whole_kernel, spans),
            [IN_VMEM] * 3,
            floats(*blocks),
            (base, table, earlier_rows),
            rebuild_cost,
        )
        incoming = lax.all_to_all(outgoing, "code", 0, 0, tiled=True)
        lost = (position == failed_ids[0, 0]) | (position == failed_ids[0, 1])
        restored_state = jnp.where(lost, incoming, earlier)
        new_parity = call(
            parity_whole_kernel,
            [IN_VMEM] * 2,
            parity_shape,
            (table, current_rows),
            parity_cost,
        )
    return (new_parity[None], restored_state.reshape(state_slab.shape))


def solution(mesh):
    placed = (
        P(("grp", "rep"), "code", None, None),
        P(("grp", "rep"), "code", None, None),
        P(("grp", "rep"), "code", None),
        P(),
        P(("grp", "rep"), None),
    )
    return jax.shard_map(
        local,
        mesh=mesh,
        in_specs=placed,
        out_specs=(P(("grp", "rep"), "code", None), P(("grp", "rep"), "code", None, None)),
        check_vma=False,
    )
```

```python
import functools

import jax
import jax.numpy as jnp
from jax import lax
from jax.experimental import pallas as pl
from jax.experimental.pallas import tpu as pltpu
from jax.sharding import PartitionSpec as P

IN_VMEM = pl.BlockSpec(memory_space=pltpu.VMEM)
IN_SMEM = pl.BlockSpec(memory_space=pltpu.SMEM)
ANYWHERE = pl.BlockSpec(memory_space=pl.ANY)

PAIRED_MEMBERS = 4
KERNEL_VMEM = 8 * 2**20


PARTNERS = ((3, 2, 1), (1, 3, 2))
CURRENT_SHIFTS = ((1, 2, 3), (1, 3, 2))
REBUILT_SHIFTS = ((1, 2, 3), (1, 3, 2))


def chosen(choices):
    odd = lax.rem(lax.axis_index("rep"), 2)
    return [jnp.where(odd == 1, b, a) if a != b else a for a, b in zip(*choices)]


def partners():
    me = lax.axis_index("code")
    return [me] + [me ^ r for r in chosen(PARTNERS)]


def ahead(shifts):
    me, members = lax.axis_index("code"), lax.axis_size("code")
    return [me] + [lax.rem(me + s, members) for s in chosen(shifts)]


def behind(shifts):
    me, members = lax.axis_index("code"), lax.axis_size("code")
    return [me] + [lax.rem(me + members - s, members) for s in chosen(shifts)]


def plan_kernel(paired, ids_ref, generator_ref, parity_ref, base_ref, table_ref):
    spans, members = generator_ref.shape
    width = base_ref.shape[2]
    first, second = ids_ref[0, 0], ids_ref[0, 1]
    col_first = [generator_ref[j, first] for j in range(spans)]
    col_second = [generator_ref[j, second] for j in range(spans)]
    gram_first = sum(x * x for x in col_first)
    gram_cross = sum(x * y for x, y in zip(col_first, col_second))
    gram_second = sum(y * y for y in col_second)
    determinant = gram_first * gram_second - gram_cross * gram_cross

    def spread(value):
        return jnp.full((1, width), value, jnp.float32)

    def put(row, value):
        table_ref[row : row + 1, :] = value

    over = spread(determinant)
    weights = [
        [spread(gram_second * x - gram_cross * y) / over for x, y in zip(col_first, col_second)],
        [spread(gram_first * y - gram_cross * x) / over for x, y in zip(col_first, col_second)],
    ]
    for k in range(2):
        base_ref[k] = sum(
            weights[k][j] * parity_ref[:, j * width : (j + 1) * width] for j in range(spans)
        )
    from_earlier = from_current = to_rebuilt = range(members)
    if paired:
        from_earlier, from_current = partners(), behind(CURRENT_SHIFTS)
        to_rebuilt = ahead(REBUILT_SHIFTS)
    for i, c in enumerate(from_earlier):
        column = [generator_ref[j, c] for j in range(spans)]
        alive = jnp.logical_and(first != c, second != c)
        for k in range(2):
            put(
                k * members + i,
                sum(weights[k][j] * jnp.where(alive, column[j], 0.0) for j in range(spans)),
            )
    for i, c in enumerate(from_current):
        for j in range(spans):
            put((2 + j) * members + i, spread(generator_ref[j, c]))
    for i, c in enumerate(to_rebuilt):
        put((2 + spans) * members + i, spread(jnp.where(first == c, 1.0, 0.0)))
    me = lax.axis_index("code")
    lost = jnp.logical_or(first == me, second == me)
    put((3 + spans) * members, spread(jnp.where(lost, 1.0, 0.0)))


def weigh(table_ref, start, rows):
    total = None
    for i, block in enumerate(rows):
        term = table_ref[start + i : start + i + 1, :] * block
        total = term if total is None else total + term
    return total


def rebuilt_for(base_ref, table_ref, rows):
    members = len(rows)
    rebuilt = [base_ref[k] - weigh(table_ref, k * members, rows) for k in range(2)]
    picks = table_ref.shape[0] - 1 - members
    return [
        jnp.where(table_ref[picks + i : picks + i + 1, :] > 0.5, *rebuilt) for i in range(members)
    ]


def rebuild_whole_kernel(base_ref, table_ref, rows_ref, out_ref):
    rows = [rows_ref[c] for c in range(rows_ref.shape[0])]
    for c, block in enumerate(rebuilt_for(base_ref, table_ref, rows)):
        out_ref[c] = block


def parity_whole_kernel(table_ref, rows_ref, out_ref):
    parity_into(out_ref, table_ref, [rows_ref[c] for c in range(rows_ref.shape[0])])


def parity_into(out_ref, table_ref, rows):
    members, width = len(rows), table_ref.shape[1]
    for j in range(out_ref.shape[1] // width):
        out_ref[:, j * width : (j + 1) * width] = weigh(table_ref, (2 + j) * members, rows)


def rebuild_paired_kernel(base_ref, table_ref, *refs):
    rows, outs = refs[: len(refs) // 2], refs[len(refs) // 2 :]
    for out_ref, block in zip(outs, rebuilt_for(base_ref, table_ref, [r[...] for r in rows])):
        out_ref[...] = block


def parity_paired_kernel(table_ref, *refs):
    rows, out_ref, done_ref = refs[:-2], refs[-2], refs[-1]
    parity_into(out_ref, table_ref, [r[...] for r in rows])
    done_ref[...] = jnp.zeros(done_ref.shape, done_ref.dtype)


def restore_kernel(table_ref, earlier_ref, held_back_by, *refs):
    pieces, out_ref = refs[:-1], refs[-1]
    members = len(pieces)
    last = table_ref.shape[0] - 1
    lost = table_ref[last : last + 1, :] > 0.5
    for c, piece in zip(behind(REBUILT_SHIFTS), pieces):
        out_ref[c] = jnp.where(lost, piece[...], earlier_ref[c])


def call(kernel, specs, outs, args, flops, **options):
    total = sum(x.size for x in args) + sum(o.size for o in jax.tree.leaves(outs))
    return pl.pallas_call(
        kernel,
        in_specs=specs,
        out_specs=jax.tree.map(lambda _: IN_VMEM, outs),
        out_shape=outs,
        compiler_params=pltpu.CompilerParams(vmem_limit_bytes=KERNEL_VMEM),
        cost_estimate=pl.CostEstimate(flops=flops, bytes_accessed=4 * total, transcendentals=0),
        **options,
    )(*args)


def floats(*shape):
    return jax.ShapeDtypeStruct(shape, jnp.float32)


def permute(pieces, moves, target):
    members, reps = lax.axis_size("code"), lax.axis_size("rep")
    return [
        lax.ppermute(
            piece,
            ("code", "rep"),
            [
                (d * reps + rep, target(d, moves[rep % 2][i]) * reps + rep)
                for d in range(members)
                for rep in range(reps)
            ],
        )
        for i, piece in enumerate(pieces)
    ]


def trade(pieces):
    return permute(pieces, PARTNERS, lambda d, r: d ^ r)


def pass_on(pieces, shifts):
    return permute(pieces, shifts, lambda d, s: (d + s) % PAIRED_MEMBERS)


def cut(blocks, order):
    return [lax.dynamic_index_in_dim(blocks, c, 0, keepdims=False) for c in order]


def local(state_slab, previous_slab, previous_parity, generator, failed_ids):
    position = lax.axis_index("code")
    members = lax.axis_size("code")
    slab_rows, width = state_slab.shape[2:]
    spans = generator.shape[0]
    own_rows = slab_rows // members
    blocks = (members, own_rows, width)
    earlier = previous_slab.reshape(blocks)
    current = state_slab.reshape(blocks)
    paired = members == PAIRED_MEMBERS

    base, table = call(
        functools.partial(plan_kernel, paired),
        [IN_SMEM, IN_SMEM, IN_VMEM],
        (floats(2, own_rows, width), floats((3 + spans) * members + 1, width)),
        (failed_ids, generator, previous_parity[0]),
        4 * spans * own_rows * width,
    )
    parity_shape = floats(own_rows, spans * width)
    rebuild_cost = 4 * slab_rows * width
    parity_cost = 2 * spans * slab_rows * width
    if paired:
        block = floats(own_rows, width)
        own_earlier, *cut_earlier = cut(earlier, partners())
        earlier_rows = trade(cut_earlier)
        own_current, *cut_current = cut(current, ahead(CURRENT_SHIFTS))
        outgoing = call(
            rebuild_paired_kernel,
            [IN_VMEM] * (members + 2),
            [block] * members,
            (base, table, own_earlier, *earlier_rows),
            rebuild_cost,
        )
        incoming = pass_on(outgoing[1:], REBUILT_SHIFTS)
        current_rows = [own_current, *pass_on(cut_current, CURRENT_SHIFTS)]
        new_parity, parity_done = call(
            parity_paired_kernel,
            [IN_VMEM] * (members + 1),
            (parity_shape, floats(8, 128)),
            (table, *current_rows),
            parity_cost,
        )
        restored_state = call(
            restore_kernel,
            [IN_VMEM, IN_VMEM, ANYWHERE] + [IN_VMEM] * members,
            floats(*blocks),
            (table, earlier, parity_done, outgoing[0], *incoming),
            0,
        )
    else:
        earlier_rows = lax.all_to_all(earlier, "code", 0, 0, tiled=True)
        current_rows = lax.all_to_all(current, "code", 0, 0, tiled=True)
        outgoing = call(
            rebuild_whole_kernel,
            [IN_VMEM] * 3,
            floats(*blocks),
            (base, table, earlier_rows),
            rebuild_cost,
        )
        incoming = lax.all_to_all(outgoing, "code", 0, 0, tiled=True)
        lost = (position == failed_ids[0, 0]) | (position == failed_ids[0, 1])
        restored_state = jnp.where(lost, incoming, earlier)
        new_parity = call(
            parity_whole_kernel,
            [IN_VMEM] * 2,
            parity_shape,
            (table, current_rows),
            parity_cost,
        )
    return (new_parity[None], restored_state.reshape(state_slab.shape))


def solution(mesh):
    placed = (
        P(("grp", "rep"), "code", None, None),
        P(("grp", "rep"), "code", None, None),
        P(("grp", "rep"), "code", None),
        P(),
        P(("grp", "rep"), None),
    )
    return jax.shard_map(
        local,
        mesh=mesh,
        in_specs=placed,
        out_specs=(P(("grp", "rep"), "code", None), P(("grp", "rep"), "code", None, None)),
        check_vma=False,
    )
```

```python
import functools

import jax
import jax.numpy as jnp
from jax import lax
from jax.experimental import pallas as pl
from jax.experimental.pallas import tpu as pltpu
from jax.sharding import PartitionSpec as P

IN_VMEM = pl.BlockSpec(memory_space=pltpu.VMEM)
IN_SMEM = pl.BlockSpec(memory_space=pltpu.SMEM)
ANYWHERE = pl.BlockSpec(memory_space=pl.ANY)

DIRECT_MEMBERS = 8
KERNEL_VMEM = 8 * 2**20


def rounds_of(members):
    half = members // 2
    return [half] + [r for r in range(members - 1, 0, -1) if r != half]


def order_of(members, direct):
    if not direct:
        return list(range(members))
    me = lax.axis_index("code")
    return [me ^ r for r in (0, *rounds_of(members))]


def targets_of(members, direct):
    if not direct:
        return list(range(members))
    me = lax.axis_index("code")
    return [lax.rem(me + s, members) for s in range(members)]


def sources_of(members, direct):
    if not direct:
        return list(range(members))
    me = lax.axis_index("code")
    return [lax.rem(me + members - s, members) for s in range(members)]


def plan_kernel(direct, ids_ref, generator_ref, parity_ref, base_ref, table_ref):
    spans, members = generator_ref.shape
    width = base_ref.shape[2]
    first, second = ids_ref[0, 0], ids_ref[0, 1]
    col_first = [generator_ref[j, first] for j in range(spans)]
    col_second = [generator_ref[j, second] for j in range(spans)]
    gram_first = sum(x * x for x in col_first)
    gram_cross = sum(x * y for x, y in zip(col_first, col_second))
    gram_second = sum(y * y for y in col_second)
    determinant = gram_first * gram_second - gram_cross * gram_cross

    def spread(value):
        return jnp.full((1, width), value, jnp.float32)

    def put(row, value):
        table_ref[row : row + 1, :] = value

    over = spread(determinant)
    weights = [
        [spread(gram_second * x - gram_cross * y) / over for x, y in zip(col_first, col_second)],
        [spread(gram_first * y - gram_cross * x) / over for x, y in zip(col_first, col_second)],
    ]
    for k in range(2):
        base_ref[k] = sum(
            weights[k][j] * parity_ref[:, j * width : (j + 1) * width] for j in range(spans)
        )
    for i, c in enumerate(order_of(members, direct)):
        column = [generator_ref[j, c] for j in range(spans)]
        alive = jnp.logical_and(first != c, second != c)
        for k in range(2):
            put(
                k * members + i,
                sum(weights[k][j] * jnp.where(alive, column[j], 0.0) for j in range(spans)),
            )
    for i, c in enumerate(sources_of(members, direct)):
        for j in range(spans):
            put((2 + j) * members + i, spread(generator_ref[j, c]))
    for i, c in enumerate(targets_of(members, direct)):
        put((2 + spans) * members + i, spread(jnp.where(first == c, 1.0, 0.0)))
    me = lax.axis_index("code")
    lost = jnp.logical_or(first == me, second == me)
    put((3 + spans) * members, spread(jnp.where(lost, 1.0, 0.0)))


def weigh(table_ref, start, rows):
    total = None
    for i, block in enumerate(rows):
        term = table_ref[start + i : start + i + 1, :] * block
        total = term if total is None else total + term
    return total


def rebuilt_for(base_ref, table_ref, rows):
    members = len(rows)
    rebuilt = [base_ref[k] - weigh(table_ref, k * members, rows) for k in range(2)]
    picks = table_ref.shape[0] - 1 - members
    return [
        jnp.where(table_ref[picks + i : picks + i + 1, :] > 0.5, *rebuilt) for i in range(members)
    ]


def rebuild_whole_kernel(base_ref, table_ref, rows_ref, out_ref):
    rows = [rows_ref[c] for c in range(rows_ref.shape[0])]
    for c, block in enumerate(rebuilt_for(base_ref, table_ref, rows)):
        out_ref[c] = block


def parity_whole_kernel(table_ref, rows_ref, out_ref):
    parity_into(out_ref, table_ref, [rows_ref[c] for c in range(rows_ref.shape[0])])


def parity_into(out_ref, table_ref, rows):
    members, width = len(rows), table_ref.shape[1]
    for j in range(out_ref.shape[1] // width):
        out_ref[:, j * width : (j + 1) * width] = weigh(table_ref, (2 + j) * members, rows)


def rebuild_paired_kernel(base_ref, table_ref, *refs):
    rows, outs = refs[: len(refs) // 2], refs[len(refs) // 2 :]
    for out_ref, block in zip(outs, rebuilt_for(base_ref, table_ref, [r[...] for r in rows])):
        out_ref[...] = block


def parity_paired_kernel(table_ref, *refs):
    rows, out_ref, done_ref = refs[:-2], refs[-2], refs[-1]
    parity_into(out_ref, table_ref, [r[...] for r in rows])
    done_ref[...] = jnp.zeros(done_ref.shape, done_ref.dtype)


def restore_kernel(table_ref, earlier_ref, held_back_by, *refs):
    pieces, out_ref = refs[:-1], refs[-1]
    members = len(pieces)
    last = table_ref.shape[0] - 1
    lost = table_ref[last : last + 1, :] > 0.5
    for c, piece in zip(sources_of(members, True), pieces):
        out_ref[c] = jnp.where(lost, piece[...], earlier_ref[c])


def call(kernel, specs, outs, args, flops, **options):
    total = sum(x.size for x in args) + sum(o.size for o in jax.tree.leaves(outs))
    return pl.pallas_call(
        kernel,
        in_specs=specs,
        out_specs=jax.tree.map(lambda _: IN_VMEM, outs),
        out_shape=outs,
        compiler_params=pltpu.CompilerParams(vmem_limit_bytes=KERNEL_VMEM),
        cost_estimate=pl.CostEstimate(flops=flops, bytes_accessed=4 * total, transcendentals=0),
        **options,
    )(*args)


def floats(*shape):
    return jax.ShapeDtypeStruct(shape, jnp.float32)


def pass_on(pieces, members):
    return [
        lax.ppermute(piece, "code", [(d, (d + s) % members) for d in range(members)])
        for s, piece in enumerate(pieces, 1)
    ]


def trade(pieces, rounds, members):
    return [
        lax.ppermute(piece, "code", [(d, d ^ r) for d in range(members)])
        for r, piece in zip(rounds, pieces)
    ]


def cut(blocks, order):
    return [lax.dynamic_index_in_dim(blocks, c, 0, keepdims=False) for c in order]


def local(state_slab, previous_slab, previous_parity, generator, failed_ids):
    position = lax.axis_index("code")
    members = lax.axis_size("code")
    slab_rows, width = state_slab.shape[2:]
    spans = generator.shape[0]
    own_rows = slab_rows // members
    blocks = (members, own_rows, width)
    earlier = previous_slab.reshape(blocks)
    current = state_slab.reshape(blocks)
    direct = 4 <= members <= DIRECT_MEMBERS and members & (members - 1) == 0

    base, table = call(
        functools.partial(plan_kernel, direct),
        [IN_SMEM, IN_SMEM, IN_VMEM],
        (floats(2, own_rows, width), floats((3 + spans) * members + 1, width)),
        (failed_ids, generator, previous_parity[0]),
        4 * spans * own_rows * width,
    )
    parity_shape = floats(own_rows, spans * width)
    rebuild_cost = 4 * slab_rows * width
    parity_cost = 2 * spans * slab_rows * width
    if direct:
        rounds = list(rounds_of(members))
        block = floats(own_rows, width)
        own_earlier, *cut_earlier = cut(earlier, order_of(members, True))
        earlier_rows = trade(cut_earlier, rounds, members)
        own_current, *cut_current = cut(current, targets_of(members, True))
        outgoing = call(
            rebuild_paired_kernel,
            [IN_VMEM] * (members + 2),
            [block] * members,
            (base, table, own_earlier, *earlier_rows),
            rebuild_cost,
        )
        incoming = pass_on(outgoing[1:], members)
        current_rows = [own_current, *pass_on(cut_current, members)]
        new_parity, parity_done = call(
            parity_paired_kernel,
            [IN_VMEM] * (members + 1),
            (parity_shape, floats(8, 128)),
            (table, *current_rows),
            parity_cost,
        )
        restored_state = call(
            restore_kernel,
            [IN_VMEM, IN_VMEM, ANYWHERE] + [IN_VMEM] * members,
            floats(*blocks),
            (table, earlier, parity_done, outgoing[0], *incoming),
            0,
        )
    else:
        earlier_rows = lax.all_to_all(earlier, "code", 0, 0, tiled=True)
        current_rows = lax.all_to_all(current, "code", 0, 0, tiled=True)
        outgoing = call(
            rebuild_whole_kernel,
            [IN_VMEM] * 3,
            floats(*blocks),
            (base, table, earlier_rows),
            rebuild_cost,
        )
        incoming = lax.all_to_all(outgoing, "code", 0, 0, tiled=True)
        lost = (position == failed_ids[0, 0]) | (position == failed_ids[0, 1])
        restored_state = jnp.where(lost, incoming, earlier)
        new_parity = call(
            parity_whole_kernel,
            [IN_VMEM] * 2,
            parity_shape,
            (table, current_rows),
            parity_cost,
        )
    return (new_parity[None], restored_state.reshape(state_slab.shape))


def solution(mesh):
    placed = (
        P(("grp", "rep"), "code", None, None),
        P(("grp", "rep"), "code", None, None),
        P(("grp", "rep"), "code", None),
        P(),
        P(("grp", "rep"), None),
    )
    return jax.shard_map(
        local,
        mesh=mesh,
        in_specs=placed,
        out_specs=(P(("grp", "rep"), "code", None), P(("grp", "rep"), "code", None, None)),
        check_vma=False,
    )
```

```python
import functools

import jax
import jax.numpy as jnp
from jax import lax
from jax.experimental import pallas as pl
from jax.experimental.pallas import tpu as pltpu
from jax.sharding import PartitionSpec as P

IN_VMEM = pl.BlockSpec(memory_space=pltpu.VMEM)
IN_SMEM = pl.BlockSpec(memory_space=pltpu.SMEM)
ANYWHERE = pl.BlockSpec(memory_space=pl.ANY)

DIRECT_MEMBERS = 8
KERNEL_VMEM = 8 * 2**20


def rounds_of(members):
    half = members // 2
    return [half] + [r for r in range(1, members) if r != half]


def order_of(members, direct):
    if not direct:
        return list(range(members))
    me = lax.axis_index("code")
    return [me ^ r for r in (0, *rounds_of(members))]


def shifts_of(members, rebuilt):
    others = list(range(1, members))
    return [0] + (others if rebuilt else others[::-1])


def targets_of(members, direct, rebuilt):
    if not direct:
        return list(range(members))
    me = lax.axis_index("code")
    return [lax.rem(me + s, members) for s in shifts_of(members, rebuilt)]


def sources_of(members, direct, rebuilt):
    if not direct:
        return list(range(members))
    me = lax.axis_index("code")
    return [lax.rem(me + members - s, members) for s in shifts_of(members, rebuilt)]


def plan_kernel(direct, ids_ref, generator_ref, parity_ref, base_ref, table_ref):
    spans, members = generator_ref.shape
    width = base_ref.shape[2]
    first, second = ids_ref[0, 0], ids_ref[0, 1]
    col_first = [generator_ref[j, first] for j in range(spans)]
    col_second = [generator_ref[j, second] for j in range(spans)]
    gram_first = sum(x * x for x in col_first)
    gram_cross = sum(x * y for x, y in zip(col_first, col_second))
    gram_second = sum(y * y for y in col_second)
    determinant = gram_first * gram_second - gram_cross * gram_cross

    def spread(value):
        return jnp.full((1, width), value, jnp.float32)

    def put(row, value):
        table_ref[row : row + 1, :] = value

    over = spread(determinant)
    weights = [
        [spread(gram_second * x - gram_cross * y) / over for x, y in zip(col_first, col_second)],
        [spread(gram_first * y - gram_cross * x) / over for x, y in zip(col_first, col_second)],
    ]
    for k in range(2):
        base_ref[k] = sum(
            weights[k][j] * parity_ref[:, j * width : (j + 1) * width] for j in range(spans)
        )
    for i, c in enumerate(order_of(members, direct)):
        column = [generator_ref[j, c] for j in range(spans)]
        alive = jnp.logical_and(first != c, second != c)
        for k in range(2):
            put(
                k * members + i,
                sum(weights[k][j] * jnp.where(alive, column[j], 0.0) for j in range(spans)),
            )
    for i, c in enumerate(sources_of(members, direct, False)):
        for j in range(spans):
            put((2 + j) * members + i, spread(generator_ref[j, c]))
    for i, c in enumerate(targets_of(members, direct, True)):
        put((2 + spans) * members + i, spread(jnp.where(first == c, 1.0, 0.0)))
    me = lax.axis_index("code")
    lost = jnp.logical_or(first == me, second == me)
    put((3 + spans) * members, spread(jnp.where(lost, 1.0, 0.0)))


def weigh(table_ref, start, rows):
    total = None
    for i, block in enumerate(rows):
        term = table_ref[start + i : start + i + 1, :] * block
        total = term if total is None else total + term
    return total


def rebuilt_for(base_ref, table_ref, rows):
    members = len(rows)
    rebuilt = [base_ref[k] - weigh(table_ref, k * members, rows) for k in range(2)]
    picks = table_ref.shape[0] - 1 - members
    return [
        jnp.where(table_ref[picks + i : picks + i + 1, :] > 0.5, *rebuilt) for i in range(members)
    ]


def rebuild_whole_kernel(base_ref, table_ref, rows_ref, out_ref):
    rows = [rows_ref[c] for c in range(rows_ref.shape[0])]
    for c, block in enumerate(rebuilt_for(base_ref, table_ref, rows)):
        out_ref[c] = block


def parity_whole_kernel(table_ref, rows_ref, out_ref):
    parity_into(out_ref, table_ref, [rows_ref[c] for c in range(rows_ref.shape[0])])


def parity_into(out_ref, table_ref, rows):
    members, width = len(rows), table_ref.shape[1]
    for j in range(out_ref.shape[1] // width):
        out_ref[:, j * width : (j + 1) * width] = weigh(table_ref, (2 + j) * members, rows)


def rebuild_paired_kernel(base_ref, table_ref, *refs):
    rows, outs = refs[: len(refs) // 2], refs[len(refs) // 2 :]
    for out_ref, block in zip(outs, rebuilt_for(base_ref, table_ref, [r[...] for r in rows])):
        out_ref[...] = block


def parity_paired_kernel(table_ref, *refs):
    rows, out_ref, done_ref = refs[:-2], refs[-2], refs[-1]
    parity_into(out_ref, table_ref, [r[...] for r in rows])
    done_ref[...] = jnp.zeros(done_ref.shape, done_ref.dtype)


def restore_kernel(table_ref, earlier_ref, held_back_by, *refs):
    pieces, out_ref = refs[:-1], refs[-1]
    members = len(pieces)
    last = table_ref.shape[0] - 1
    lost = table_ref[last : last + 1, :] > 0.5
    for c, piece in zip(sources_of(members, True, True), pieces):
        out_ref[c] = jnp.where(lost, piece[...], earlier_ref[c])


def call(kernel, specs, outs, args, flops, **options):
    total = sum(x.size for x in args) + sum(o.size for o in jax.tree.leaves(outs))
    return pl.pallas_call(
        kernel,
        in_specs=specs,
        out_specs=jax.tree.map(lambda _: IN_VMEM, outs),
        out_shape=outs,
        compiler_params=pltpu.CompilerParams(vmem_limit_bytes=KERNEL_VMEM),
        cost_estimate=pl.CostEstimate(flops=flops, bytes_accessed=4 * total, transcendentals=0),
        **options,
    )(*args)


def floats(*shape):
    return jax.ShapeDtypeStruct(shape, jnp.float32)


def pass_on(pieces, members, rebuilt):
    return [
        lax.ppermute(piece, "code", [(d, (d + s) % members) for d in range(members)])
        for s, piece in zip(shifts_of(members, rebuilt)[1:], pieces)
    ]


def trade(pieces, rounds, members):
    return [
        lax.ppermute(piece, "code", [(d, d ^ r) for d in range(members)])
        for r, piece in zip(rounds, pieces)
    ]


def cut(blocks, order):
    return [lax.dynamic_index_in_dim(blocks, c, 0, keepdims=False) for c in order]


def local(state_slab, previous_slab, previous_parity, generator, failed_ids):
    position = lax.axis_index("code")
    members = lax.axis_size("code")
    slab_rows, width = state_slab.shape[2:]
    spans = generator.shape[0]
    own_rows = slab_rows // members
    blocks = (members, own_rows, width)
    earlier = previous_slab.reshape(blocks)
    current = state_slab.reshape(blocks)
    direct = 4 <= members <= DIRECT_MEMBERS and members & (members - 1) == 0

    base, table = call(
        functools.partial(plan_kernel, direct),
        [IN_SMEM, IN_SMEM, IN_VMEM],
        (floats(2, own_rows, width), floats((3 + spans) * members + 1, width)),
        (failed_ids, generator, previous_parity[0]),
        4 * spans * own_rows * width,
    )
    parity_shape = floats(own_rows, spans * width)
    rebuild_cost = 4 * slab_rows * width
    parity_cost = 2 * spans * slab_rows * width
    if direct:
        rounds = list(rounds_of(members))
        block = floats(own_rows, width)
        own, lead, *rest = order_of(members, True)
        (lead_block,) = cut(earlier, [lead])
        later, lead_block = lax.optimization_barrier((earlier, lead_block))
        own_earlier, *cut_earlier = cut(later, [own] + rest)
        cut_earlier = [lead_block, *cut_earlier]
        earlier_rows = trade(cut_earlier, rounds, members)
        own_current, *cut_current = cut(current, targets_of(members, True, False))
        outgoing = call(
            rebuild_paired_kernel,
            [IN_VMEM] * (members + 2),
            [block] * members,
            (base, table, own_earlier, *earlier_rows),
            rebuild_cost,
        )
        incoming = pass_on(outgoing[1:], members, True)
        current_rows = [own_current, *pass_on(cut_current, members, False)]
        new_parity, parity_done = call(
            parity_paired_kernel,
            [IN_VMEM] * (members + 1),
            (parity_shape, floats(8, 128)),
            (table, *current_rows),
            parity_cost,
        )
        restored_state = call(
            restore_kernel,
            [IN_VMEM, IN_VMEM, ANYWHERE] + [IN_VMEM] * members,
            floats(*blocks),
            (table, earlier, parity_done, outgoing[0], *incoming),
            0,
        )
    else:
        earlier_rows = lax.all_to_all(earlier, "code", 0, 0, tiled=True)
        current_rows = lax.all_to_all(current, "code", 0, 0, tiled=True)
        outgoing = call(
            rebuild_whole_kernel,
            [IN_VMEM] * 3,
            floats(*blocks),
            (base, table, earlier_rows),
            rebuild_cost,
        )
        incoming = lax.all_to_all(outgoing, "code", 0, 0, tiled=True)
        lost = (position == failed_ids[0, 0]) | (position == failed_ids[0, 1])
        restored_state = jnp.where(lost, incoming, earlier)
        new_parity = call(
            parity_whole_kernel,
            [IN_VMEM] * 2,
            parity_shape,
            (table, current_rows),
            parity_cost,
        )
    return (new_parity[None], restored_state.reshape(state_slab.shape))


def solution(mesh):
    placed = (
        P(("grp", "rep"), "code", None, None),
        P(("grp", "rep"), "code", None, None),
        P(("grp", "rep"), "code", None),
        P(),
        P(("grp", "rep"), None),
    )
    return jax.shard_map(
        local,
        mesh=mesh,
        in_specs=placed,
        out_specs=(P(("grp", "rep"), "code", None), P(("grp", "rep"), "code", None, None)),
        check_vma=False,
    )
```

```python
import functools

import jax
import jax.numpy as jnp
from jax import lax
from jax.experimental import pallas as pl
from jax.experimental.pallas import tpu as pltpu
from jax.sharding import PartitionSpec as P

IN_VMEM = pl.BlockSpec(memory_space=pltpu.VMEM)
IN_SMEM = pl.BlockSpec(memory_space=pltpu.SMEM)
ANYWHERE = pl.BlockSpec(memory_space=pl.ANY)

PAIRED_MEMBERS = 4
KERNEL_VMEM = 8 * 2**20

EARLIER_ROUNDS = (("xor", 2), ("xor", 1), ("xor", 3))
CURRENT_ROUNDS = (("xor", 1), ("xor", 3), ("xor", 2))
REBUILT_ROUNDS = (("on", 3), ("on", 2), ("on", 1))


def target(d, way, n, members):
    return d ^ n if way == "xor" else (d + n) % members


def source(d, way, n, members):
    return d ^ n if way == "xor" else (d + members - n) % members


def targets_of(rounds, members):
    me = lax.axis_index("code")
    return [me] + [target(me, *way, members) for way in rounds]


def sources_of(rounds, members):
    me = lax.axis_index("code")
    return [me] + [source(me, *way, members) for way in rounds]


def plan_kernel(paired, ids_ref, generator_ref, parity_ref, base_ref, table_ref):
    spans, members = generator_ref.shape
    width = base_ref.shape[2]
    first, second = ids_ref[0, 0], ids_ref[0, 1]
    col_first = [generator_ref[j, first] for j in range(spans)]
    col_second = [generator_ref[j, second] for j in range(spans)]
    gram_first = sum(x * x for x in col_first)
    gram_cross = sum(x * y for x, y in zip(col_first, col_second))
    gram_second = sum(y * y for y in col_second)
    determinant = gram_first * gram_second - gram_cross * gram_cross

    def spread(value):
        return jnp.full((1, width), value, jnp.float32)

    def put(row, value):
        table_ref[row : row + 1, :] = value

    over = spread(determinant)
    weights = [
        [spread(gram_second * x - gram_cross * y) / over for x, y in zip(col_first, col_second)],
        [spread(gram_first * y - gram_cross * x) / over for x, y in zip(col_first, col_second)],
    ]
    for k in range(2):
        base_ref[k] = sum(
            weights[k][j] * parity_ref[:, j * width : (j + 1) * width] for j in range(spans)
        )
    from_earlier = from_current = to_rebuilt = range(members)
    if paired:
        from_earlier = sources_of(EARLIER_ROUNDS, members)
        from_current = sources_of(CURRENT_ROUNDS, members)
        to_rebuilt = targets_of(REBUILT_ROUNDS, members)
    for i, c in enumerate(from_earlier):
        column = [generator_ref[j, c] for j in range(spans)]
        alive = jnp.logical_and(first != c, second != c)
        for k in range(2):
            put(
                k * members + i,
                sum(weights[k][j] * jnp.where(alive, column[j], 0.0) for j in range(spans)),
            )
    for i, c in enumerate(from_current):
        for j in range(spans):
            put((2 + j) * members + i, spread(generator_ref[j, c]))
    for i, c in enumerate(to_rebuilt):
        put((2 + spans) * members + i, spread(jnp.where(first == c, 1.0, 0.0)))
    me = lax.axis_index("code")
    lost = jnp.logical_or(first == me, second == me)
    put((3 + spans) * members, spread(jnp.where(lost, 1.0, 0.0)))


def weigh(table_ref, start, rows):
    total = None
    for i, block in enumerate(rows):
        term = table_ref[start + i : start + i + 1, :] * block
        total = term if total is None else total + term
    return total


def rebuilt_for(base_ref, table_ref, rows):
    members = len(rows)
    rebuilt = [base_ref[k] - weigh(table_ref, k * members, rows) for k in range(2)]
    picks = table_ref.shape[0] - 1 - members
    return [
        jnp.where(table_ref[picks + i : picks + i + 1, :] > 0.5, *rebuilt) for i in range(members)
    ]


def rebuild_whole_kernel(base_ref, table_ref, rows_ref, out_ref):
    rows = [rows_ref[c] for c in range(rows_ref.shape[0])]
    for c, block in enumerate(rebuilt_for(base_ref, table_ref, rows)):
        out_ref[c] = block


def parity_whole_kernel(table_ref, rows_ref, out_ref):
    parity_into(out_ref, table_ref, [rows_ref[c] for c in range(rows_ref.shape[0])])


def parity_into(out_ref, table_ref, rows):
    members, width = len(rows), table_ref.shape[1]
    for j in range(out_ref.shape[1] // width):
        out_ref[:, j * width : (j + 1) * width] = weigh(table_ref, (2 + j) * members, rows)


def rebuild_paired_kernel(base_ref, table_ref, *refs):
    rows, outs = refs[: len(refs) // 2], refs[len(refs) // 2 :]
    for out_ref, block in zip(outs, rebuilt_for(base_ref, table_ref, [r[...] for r in rows])):
        out_ref[...] = block


def parity_paired_kernel(table_ref, *refs):
    rows, out_ref, done_ref = refs[:-2], refs[-2], refs[-1]
    parity_into(out_ref, table_ref, [r[...] for r in rows])
    done_ref[...] = jnp.zeros(done_ref.shape, done_ref.dtype)


def restore_kernel(table_ref, earlier_ref, held_back_by, *refs):
    pieces, out_ref = refs[:-1], refs[-1]
    members = len(pieces)
    last = table_ref.shape[0] - 1
    lost = table_ref[last : last + 1, :] > 0.5
    for c, piece in zip(sources_of(REBUILT_ROUNDS, members), pieces):
        out_ref[c] = jnp.where(lost, piece[...], earlier_ref[c])


def call(kernel, specs, outs, args, flops, **options):
    total = sum(x.size for x in args) + sum(o.size for o in jax.tree.leaves(outs))
    return pl.pallas_call(
        kernel,
        in_specs=specs,
        out_specs=jax.tree.map(lambda _: IN_VMEM, outs),
        out_shape=outs,
        compiler_params=pltpu.CompilerParams(vmem_limit_bytes=KERNEL_VMEM),
        cost_estimate=pl.CostEstimate(flops=flops, bytes_accessed=4 * total, transcendentals=0),
        **options,
    )(*args)


def floats(*shape):
    return jax.ShapeDtypeStruct(shape, jnp.float32)


def pass_on(pieces, rounds, members):
    return [
        lax.ppermute(
            piece, "code", [(d, target(d, *way, members)) for d in range(members)]
        )
        for way, piece in zip(rounds, pieces)
    ]


def cut(blocks, order):
    return [lax.dynamic_index_in_dim(blocks, c, 0, keepdims=False) for c in order]


def local(state_slab, previous_slab, previous_parity, generator, failed_ids):
    position = lax.axis_index("code")
    members = lax.axis_size("code")
    slab_rows, width = state_slab.shape[2:]
    spans = generator.shape[0]
    own_rows = slab_rows // members
    blocks = (members, own_rows, width)
    earlier = previous_slab.reshape(blocks)
    current = state_slab.reshape(blocks)
    paired = members == PAIRED_MEMBERS

    base, table = call(
        functools.partial(plan_kernel, paired),
        [IN_SMEM, IN_SMEM, IN_VMEM],
        (floats(2, own_rows, width), floats((3 + spans) * members + 1, width)),
        (failed_ids, generator, previous_parity[0]),
        4 * spans * own_rows * width,
    )
    parity_shape = floats(own_rows, spans * width)
    rebuild_cost = 4 * slab_rows * width
    parity_cost = 2 * spans * slab_rows * width
    if paired:
        block = floats(own_rows, width)
        own_earlier, *cut_earlier = cut(earlier, targets_of(EARLIER_ROUNDS, members))
        earlier_rows = pass_on(cut_earlier, EARLIER_ROUNDS, members)
        own_current, *cut_current = cut(current, targets_of(CURRENT_ROUNDS, members))
        outgoing = call(
            rebuild_paired_kernel,
            [IN_VMEM] * (members + 2),
            [block] * members,
            (base, table, own_earlier, *earlier_rows),
            rebuild_cost,
        )
        incoming = pass_on(outgoing[1:], REBUILT_ROUNDS, members)
        current_rows = [own_current, *pass_on(cut_current, CURRENT_ROUNDS, members)]
        new_parity, parity_done = call(
            parity_paired_kernel,
            [IN_VMEM] * (members + 1),
            (parity_shape, floats(8, 128)),
            (table, *current_rows),
            parity_cost,
        )
        restored_state = call(
            restore_kernel,
            [IN_VMEM, IN_VMEM, ANYWHERE] + [IN_VMEM] * members,
            floats(*blocks),
            (table, earlier, parity_done, outgoing[0], *incoming),
            0,
        )
    else:
        earlier_rows = lax.all_to_all(earlier, "code", 0, 0, tiled=True)
        current_rows = lax.all_to_all(current, "code", 0, 0, tiled=True)
        outgoing = call(
            rebuild_whole_kernel,
            [IN_VMEM] * 3,
            floats(*blocks),
            (base, table, earlier_rows),
            rebuild_cost,
        )
        incoming = lax.all_to_all(outgoing, "code", 0, 0, tiled=True)
        lost = (position == failed_ids[0, 0]) | (position == failed_ids[0, 1])
        restored_state = jnp.where(lost, incoming, earlier)
        new_parity = call(
            parity_whole_kernel,
            [IN_VMEM] * 2,
            parity_shape,
            (table, current_rows),
            parity_cost,
        )
    return (new_parity[None], restored_state.reshape(state_slab.shape))


def solution(mesh):
    placed = (
        P(("grp", "rep"), "code", None, None),
        P(("grp", "rep"), "code", None, None),
        P(("grp", "rep"), "code", None),
        P(),
        P(("grp", "rep"), None),
    )
    return jax.shard_map(
        local,
        mesh=mesh,
        in_specs=placed,
        out_specs=(P(("grp", "rep"), "code", None), P(("grp", "rep"), "code", None, None)),
        check_vma=False,
    )
```

```python
import functools

import jax
import jax.numpy as jnp
from jax import lax
from jax.experimental import pallas as pl
from jax.experimental.pallas import tpu as pltpu
from jax.sharding import PartitionSpec as P

IN_VMEM = pl.BlockSpec(memory_space=pltpu.VMEM)
IN_SMEM = pl.BlockSpec(memory_space=pltpu.SMEM)
ANYWHERE = pl.BlockSpec(memory_space=pl.ANY)

PAIRED_MEMBERS = 4
KERNEL_VMEM = 8 * 2**20

EARLIER_ROUNDS = (("xor", 2), ("xor", 3), ("xor", 1))
CURRENT_ROUNDS = (("on", 1), ("on", 2), ("on", 3))
REBUILT_ROUNDS = (("on", 2), ("on", 1), ("on", 3))


def target(d, way, n, members):
    return d ^ n if way == "xor" else (d + n) % members


def source(d, way, n, members):
    return d ^ n if way == "xor" else (d + members - n) % members


def targets_of(rounds, members):
    me = lax.axis_index("code")
    return [me] + [target(me, *way, members) for way in rounds]


def sources_of(rounds, members):
    me = lax.axis_index("code")
    return [me] + [source(me, *way, members) for way in rounds]


def plan_kernel(paired, ids_ref, generator_ref, parity_ref, base_ref, table_ref):
    spans, members = generator_ref.shape
    width = base_ref.shape[2]
    first, second = ids_ref[0, 0], ids_ref[0, 1]
    col_first = [generator_ref[j, first] for j in range(spans)]
    col_second = [generator_ref[j, second] for j in range(spans)]
    gram_first = sum(x * x for x in col_first)
    gram_cross = sum(x * y for x, y in zip(col_first, col_second))
    gram_second = sum(y * y for y in col_second)
    determinant = gram_first * gram_second - gram_cross * gram_cross

    def spread(value):
        return jnp.full((1, width), value, jnp.float32)

    def put(row, value):
        table_ref[row : row + 1, :] = value

    over = spread(determinant)
    weights = [
        [spread(gram_second * x - gram_cross * y) / over for x, y in zip(col_first, col_second)],
        [spread(gram_first * y - gram_cross * x) / over for x, y in zip(col_first, col_second)],
    ]
    for k in range(2):
        base_ref[k] = sum(
            weights[k][j] * parity_ref[:, j * width : (j + 1) * width] for j in range(spans)
        )
    from_earlier = from_current = to_rebuilt = range(members)
    if paired:
        from_earlier = sources_of(EARLIER_ROUNDS, members)
        from_current = sources_of(CURRENT_ROUNDS, members)
        to_rebuilt = targets_of(REBUILT_ROUNDS, members)
    for i, c in enumerate(from_earlier):
        column = [generator_ref[j, c] for j in range(spans)]
        alive = jnp.logical_and(first != c, second != c)
        for k in range(2):
            put(
                k * members + i,
                sum(weights[k][j] * jnp.where(alive, column[j], 0.0) for j in range(spans)),
            )
    for i, c in enumerate(from_current):
        for j in range(spans):
            put((2 + j) * members + i, spread(generator_ref[j, c]))
    for i, c in enumerate(to_rebuilt):
        put((2 + spans) * members + i, spread(jnp.where(first == c, 1.0, 0.0)))
    me = lax.axis_index("code")
    lost = jnp.logical_or(first == me, second == me)
    put((3 + spans) * members, spread(jnp.where(lost, 1.0, 0.0)))


def weigh(table_ref, start, rows):
    total = None
    for i, block in enumerate(rows):
        term = table_ref[start + i : start + i + 1, :] * block
        total = term if total is None else total + term
    return total


def rebuilt_for(base_ref, table_ref, rows):
    members = len(rows)
    rebuilt = [base_ref[k] - weigh(table_ref, k * members, rows) for k in range(2)]
    picks = table_ref.shape[0] - 1 - members
    return [
        jnp.where(table_ref[picks + i : picks + i + 1, :] > 0.5, *rebuilt) for i in range(members)
    ]


def rebuild_whole_kernel(base_ref, table_ref, rows_ref, out_ref):
    rows = [rows_ref[c] for c in range(rows_ref.shape[0])]
    for c, block in enumerate(rebuilt_for(base_ref, table_ref, rows)):
        out_ref[c] = block


def parity_whole_kernel(table_ref, rows_ref, out_ref):
    parity_into(out_ref, table_ref, [rows_ref[c] for c in range(rows_ref.shape[0])])


def parity_into(out_ref, table_ref, rows):
    members, width = len(rows), table_ref.shape[1]
    for j in range(out_ref.shape[1] // width):
        out_ref[:, j * width : (j + 1) * width] = weigh(table_ref, (2 + j) * members, rows)


def rebuild_paired_kernel(base_ref, table_ref, *refs):
    rows, outs = refs[: len(refs) // 2], refs[len(refs) // 2 :]
    for out_ref, block in zip(outs, rebuilt_for(base_ref, table_ref, [r[...] for r in rows])):
        out_ref[...] = block


def parity_paired_kernel(table_ref, *refs):
    rows, out_ref, done_ref = refs[:-2], refs[-2], refs[-1]
    parity_into(out_ref, table_ref, [r[...] for r in rows])
    done_ref[...] = jnp.zeros(done_ref.shape, done_ref.dtype)


def restore_kernel(table_ref, earlier_ref, held_back_by, *refs):
    pieces, out_ref = refs[:-1], refs[-1]
    members = len(pieces)
    last = table_ref.shape[0] - 1
    lost = table_ref[last : last + 1, :] > 0.5
    for c, piece in zip(sources_of(REBUILT_ROUNDS, members), pieces):
        out_ref[c] = jnp.where(lost, piece[...], earlier_ref[c])


def call(kernel, specs, outs, args, flops, **options):
    total = sum(x.size for x in args) + sum(o.size for o in jax.tree.leaves(outs))
    return pl.pallas_call(
        kernel,
        in_specs=specs,
        out_specs=jax.tree.map(lambda _: IN_VMEM, outs),
        out_shape=outs,
        compiler_params=pltpu.CompilerParams(vmem_limit_bytes=KERNEL_VMEM),
        cost_estimate=pl.CostEstimate(flops=flops, bytes_accessed=4 * total, transcendentals=0),
        **options,
    )(*args)


def floats(*shape):
    return jax.ShapeDtypeStruct(shape, jnp.float32)


def pass_on(pieces, rounds, members):
    return [
        lax.ppermute(
            piece, "code", [(d, target(d, *way, members)) for d in range(members)]
        )
        for way, piece in zip(rounds, pieces)
    ]


def cut(blocks, order):
    return [lax.dynamic_index_in_dim(blocks, c, 0, keepdims=False) for c in order]


def local(state_slab, previous_slab, previous_parity, generator, failed_ids):
    position = lax.axis_index("code")
    members = lax.axis_size("code")
    slab_rows, width = state_slab.shape[2:]
    spans = generator.shape[0]
    own_rows = slab_rows // members
    blocks = (members, own_rows, width)
    earlier = previous_slab.reshape(blocks)
    current = state_slab.reshape(blocks)
    paired = members == PAIRED_MEMBERS

    base, table = call(
        functools.partial(plan_kernel, paired),
        [IN_SMEM, IN_SMEM, IN_VMEM],
        (floats(2, own_rows, width), floats((3 + spans) * members + 1, width)),
        (failed_ids, generator, previous_parity[0]),
        4 * spans * own_rows * width,
    )
    parity_shape = floats(own_rows, spans * width)
    rebuild_cost = 4 * slab_rows * width
    parity_cost = 2 * spans * slab_rows * width
    if paired:
        block = floats(own_rows, width)
        own_earlier, *cut_earlier = cut(earlier, targets_of(EARLIER_ROUNDS, members))
        earlier_rows = pass_on(cut_earlier, EARLIER_ROUNDS, members)
        own_current, *cut_current = cut(current, targets_of(CURRENT_ROUNDS, members))
        outgoing = call(
            rebuild_paired_kernel,
            [IN_VMEM] * (members + 2),
            [block] * members,
            (base, table, own_earlier, *earlier_rows),
            rebuild_cost,
        )
        incoming = pass_on(outgoing[1:], REBUILT_ROUNDS, members)
        current_rows = [own_current, *pass_on(cut_current, CURRENT_ROUNDS, members)]
        new_parity, parity_done = call(
            parity_paired_kernel,
            [IN_VMEM] * (members + 1),
            (parity_shape, floats(8, 128)),
            (table, *current_rows),
            parity_cost,
        )
        restored_state = call(
            restore_kernel,
            [IN_VMEM, IN_VMEM, ANYWHERE] + [IN_VMEM] * members,
            floats(*blocks),
            (table, earlier, parity_done, outgoing[0], *incoming),
            0,
        )
    else:
        earlier_rows = lax.all_to_all(earlier, "code", 0, 0, tiled=True)
        current_rows = lax.all_to_all(current, "code", 0, 0, tiled=True)
        outgoing = call(
            rebuild_whole_kernel,
            [IN_VMEM] * 3,
            floats(*blocks),
            (base, table, earlier_rows),
            rebuild_cost,
        )
        incoming = lax.all_to_all(outgoing, "code", 0, 0, tiled=True)
        lost = (position == failed_ids[0, 0]) | (position == failed_ids[0, 1])
        restored_state = jnp.where(lost, incoming, earlier)
        new_parity = call(
            parity_whole_kernel,
            [IN_VMEM] * 2,
            parity_shape,
            (table, current_rows),
            parity_cost,
        )
    return (new_parity[None], restored_state.reshape(state_slab.shape))


def solution(mesh):
    placed = (
        P(("grp", "rep"), "code", None, None),
        P(("grp", "rep"), "code", None, None),
        P(("grp", "rep"), "code", None),
        P(),
        P(("grp", "rep"), None),
    )
    return jax.shard_map(
        local,
        mesh=mesh,
        in_specs=placed,
        out_specs=(P(("grp", "rep"), "code", None), P(("grp", "rep"), "code", None, None)),
        check_vma=False,
    )
```

```python
import functools

import jax
import jax.numpy as jnp
from jax import lax
from jax.experimental import pallas as pl
from jax.experimental.pallas import tpu as pltpu
from jax.sharding import PartitionSpec as P

IN_VMEM = pl.BlockSpec(memory_space=pltpu.VMEM)
IN_SMEM = pl.BlockSpec(memory_space=pltpu.SMEM)
ANYWHERE = pl.BlockSpec(memory_space=pl.ANY)

PAIRED_MEMBERS = 4
KERNEL_VMEM = 8 * 2**20

EARLIER_ROUNDS = (("xor", 1), ("xor", 3), ("xor", 2))
REBUILT_ROUNDS = (("on", 1), ("on", 2), ("on", 3))


def target(d, way, n, members):
    return d ^ n if way == "xor" else (d + n) % members


def source(d, way, n, members):
    return d ^ n if way == "xor" else (d + members - n) % members


def targets_of(rounds, members):
    me = lax.axis_index("code")
    return [me] + [target(me, *way, members) for way in rounds]


def sources_of(rounds, members):
    me = lax.axis_index("code")
    return [me] + [source(me, *way, members) for way in rounds]


def plan_kernel(paired, ids_ref, generator_ref, parity_ref, base_ref, table_ref):
    spans, members = generator_ref.shape
    width = base_ref.shape[2]
    first, second = ids_ref[0, 0], ids_ref[0, 1]
    col_first = [generator_ref[j, first] for j in range(spans)]
    col_second = [generator_ref[j, second] for j in range(spans)]
    gram_first = sum(x * x for x in col_first)
    gram_cross = sum(x * y for x, y in zip(col_first, col_second))
    gram_second = sum(y * y for y in col_second)
    determinant = gram_first * gram_second - gram_cross * gram_cross

    def spread(value):
        return jnp.full((1, width), value, jnp.float32)

    def put(row, value):
        table_ref[row : row + 1, :] = value

    over = spread(determinant)
    weights = [
        [spread(gram_second * x - gram_cross * y) / over for x, y in zip(col_first, col_second)],
        [spread(gram_first * y - gram_cross * x) / over for x, y in zip(col_first, col_second)],
    ]
    for k in range(2):
        base_ref[k] = sum(
            weights[k][j] * parity_ref[:, j * width : (j + 1) * width] for j in range(spans)
        )
    from_earlier = from_current = to_rebuilt = range(members)
    if paired:
        from_earlier = sources_of(EARLIER_ROUNDS, members)
        to_rebuilt = targets_of(REBUILT_ROUNDS, members)
    for i, c in enumerate(from_earlier):
        column = [generator_ref[j, c] for j in range(spans)]
        alive = jnp.logical_and(first != c, second != c)
        for k in range(2):
            put(
                k * members + i,
                sum(weights[k][j] * jnp.where(alive, column[j], 0.0) for j in range(spans)),
            )
    for i, c in enumerate(from_current):
        for j in range(spans):
            put((2 + j) * members + i, spread(generator_ref[j, c]))
    for i, c in enumerate(to_rebuilt):
        put((2 + spans) * members + i, spread(jnp.where(first == c, 1.0, 0.0)))
    me = lax.axis_index("code")
    lost = jnp.logical_or(first == me, second == me)
    put((3 + spans) * members, spread(jnp.where(lost, 1.0, 0.0)))


def weigh(table_ref, start, rows):
    total = None
    for i, block in enumerate(rows):
        term = table_ref[start + i : start + i + 1, :] * block
        total = term if total is None else total + term
    return total


def rebuilt_for(base_ref, table_ref, rows):
    members = len(rows)
    rebuilt = [base_ref[k] - weigh(table_ref, k * members, rows) for k in range(2)]
    picks = table_ref.shape[0] - 1 - members
    return [
        jnp.where(table_ref[picks + i : picks + i + 1, :] > 0.5, *rebuilt) for i in range(members)
    ]


def rebuild_whole_kernel(base_ref, table_ref, rows_ref, out_ref):
    rows = [rows_ref[c] for c in range(rows_ref.shape[0])]
    for c, block in enumerate(rebuilt_for(base_ref, table_ref, rows)):
        out_ref[c] = block


def parity_whole_kernel(table_ref, rows_ref, out_ref):
    parity_into(out_ref, table_ref, [rows_ref[c] for c in range(rows_ref.shape[0])])


def parity_into(out_ref, table_ref, rows):
    members, width = len(rows), table_ref.shape[1]
    for j in range(out_ref.shape[1] // width):
        out_ref[:, j * width : (j + 1) * width] = weigh(table_ref, (2 + j) * members, rows)


def rebuild_paired_kernel(base_ref, table_ref, *refs):
    rows, outs = refs[: len(refs) // 2], refs[len(refs) // 2 :]
    for out_ref, block in zip(outs, rebuilt_for(base_ref, table_ref, [r[...] for r in rows])):
        out_ref[...] = block


def parity_paired_kernel(table_ref, rows_ref, out_ref, done_ref):
    parity_whole_kernel(table_ref, rows_ref, out_ref)
    done_ref[...] = jnp.zeros(done_ref.shape, done_ref.dtype)


def restore_kernel(table_ref, earlier_ref, held_back_by, *refs):
    pieces, out_ref = refs[:-1], refs[-1]
    members = len(pieces)
    last = table_ref.shape[0] - 1
    lost = table_ref[last : last + 1, :] > 0.5
    for c, piece in zip(sources_of(REBUILT_ROUNDS, members), pieces):
        out_ref[c] = jnp.where(lost, piece[...], earlier_ref[c])


def call(kernel, specs, outs, args, flops, **options):
    total = sum(x.size for x in args) + sum(o.size for o in jax.tree.leaves(outs))
    return pl.pallas_call(
        kernel,
        in_specs=specs,
        out_specs=jax.tree.map(lambda _: IN_VMEM, outs),
        out_shape=outs,
        compiler_params=pltpu.CompilerParams(vmem_limit_bytes=KERNEL_VMEM),
        cost_estimate=pl.CostEstimate(flops=flops, bytes_accessed=4 * total, transcendentals=0),
        **options,
    )(*args)


def floats(*shape):
    return jax.ShapeDtypeStruct(shape, jnp.float32)


def pass_on(pieces, rounds, members):
    return [
        lax.ppermute(
            piece, "code", [(d, target(d, *way, members)) for d in range(members)]
        )
        for way, piece in zip(rounds, pieces)
    ]


def cut(blocks, order):
    return [lax.dynamic_index_in_dim(blocks, c, 0, keepdims=False) for c in order]


def local(state_slab, previous_slab, previous_parity, generator, failed_ids):
    position = lax.axis_index("code")
    members = lax.axis_size("code")
    slab_rows, width = state_slab.shape[2:]
    spans = generator.shape[0]
    own_rows = slab_rows // members
    blocks = (members, own_rows, width)
    earlier = previous_slab.reshape(blocks)
    current = state_slab.reshape(blocks)
    paired = members == PAIRED_MEMBERS

    base, table = call(
        functools.partial(plan_kernel, paired),
        [IN_SMEM, IN_SMEM, IN_VMEM],
        (floats(2, own_rows, width), floats((3 + spans) * members + 1, width)),
        (failed_ids, generator, previous_parity[0]),
        4 * spans * own_rows * width,
    )
    parity_shape = floats(own_rows, spans * width)
    rebuild_cost = 4 * slab_rows * width
    parity_cost = 2 * spans * slab_rows * width
    if paired:
        block = floats(own_rows, width)
        own_earlier, *cut_earlier = cut(earlier, targets_of(EARLIER_ROUNDS, members))
        earlier_rows = pass_on(cut_earlier, EARLIER_ROUNDS, members)
        current, own_earlier = lax.optimization_barrier((current, own_earlier))
        current_rows = lax.all_to_all(current, "code", 0, 0, tiled=True)
        outgoing = call(
            rebuild_paired_kernel,
            [IN_VMEM] * (members + 2),
            [block] * members,
            (base, table, own_earlier, *earlier_rows),
            rebuild_cost,
        )
        incoming = pass_on(outgoing[1:], REBUILT_ROUNDS, members)
        new_parity, parity_done = call(
            parity_paired_kernel,
            [IN_VMEM] * 2,
            (parity_shape, floats(8, 128)),
            (table, current_rows),
            parity_cost,
        )
        restored_state = call(
            restore_kernel,
            [IN_VMEM, IN_VMEM, ANYWHERE] + [IN_VMEM] * members,
            floats(*blocks),
            (table, earlier, parity_done, outgoing[0], *incoming),
            0,
        )
    else:
        earlier_rows = lax.all_to_all(earlier, "code", 0, 0, tiled=True)
        current_rows = lax.all_to_all(current, "code", 0, 0, tiled=True)
        outgoing = call(
            rebuild_whole_kernel,
            [IN_VMEM] * 3,
            floats(*blocks),
            (base, table, earlier_rows),
            rebuild_cost,
        )
        incoming = lax.all_to_all(outgoing, "code", 0, 0, tiled=True)
        lost = (position == failed_ids[0, 0]) | (position == failed_ids[0, 1])
        restored_state = jnp.where(lost, incoming, earlier)
        new_parity = call(
            parity_whole_kernel,
            [IN_VMEM] * 2,
            parity_shape,
            (table, current_rows),
            parity_cost,
        )
    return (new_parity[None], restored_state.reshape(state_slab.shape))


def solution(mesh):
    placed = (
        P(("grp", "rep"), "code", None, None),
        P(("grp", "rep"), "code", None, None),
        P(("grp", "rep"), "code", None),
        P(),
        P(("grp", "rep"), None),
    )
    return jax.shard_map(
        local,
        mesh=mesh,
        in_specs=placed,
        out_specs=(P(("grp", "rep"), "code", None), P(("grp", "rep"), "code", None, None)),
        check_vma=False,
    )
```

```python
import functools

import jax
import jax.numpy as jnp
from jax import lax
from jax.experimental import pallas as pl
from jax.experimental.pallas import tpu as pltpu
from jax.sharding import PartitionSpec as P

IN_VMEM = pl.BlockSpec(memory_space=pltpu.VMEM)
IN_SMEM = pl.BlockSpec(memory_space=pltpu.SMEM)
ANYWHERE = pl.BlockSpec(memory_space=pl.ANY)

PAIRED_MEMBERS = 4
KERNEL_VMEM = 8 * 2**20

EARLIER_ROUNDS = (("xor", 2), ("xor", 3), ("xor", 1))
CURRENT_ROUNDS = (("on", 1), ("on", 3), ("on", 2))
REBUILT_ROUNDS = (("on", 1), ("on", 2), ("on", 3))


def target(d, way, n, members):
    return d ^ n if way == "xor" else (d + n) % members


def source(d, way, n, members):
    return d ^ n if way == "xor" else (d + members - n) % members


def targets_of(rounds, members):
    me = lax.axis_index("code")
    return [me] + [target(me, *way, members) for way in rounds]


def sources_of(rounds, members):
    me = lax.axis_index("code")
    return [me] + [source(me, *way, members) for way in rounds]


def plan_kernel(paired, ids_ref, generator_ref, parity_ref, base_ref, table_ref):
    spans, members = generator_ref.shape
    width = base_ref.shape[2]
    first, second = ids_ref[0, 0], ids_ref[0, 1]
    col_first = [generator_ref[j, first] for j in range(spans)]
    col_second = [generator_ref[j, second] for j in range(spans)]
    gram_first = sum(x * x for x in col_first)
    gram_cross = sum(x * y for x, y in zip(col_first, col_second))
    gram_second = sum(y * y for y in col_second)
    determinant = gram_first * gram_second - gram_cross * gram_cross

    def spread(value):
        return jnp.full((1, width), value, jnp.float32)

    def put(row, value):
        table_ref[row : row + 1, :] = value

    over = spread(determinant)
    weights = [
        [spread(gram_second * x - gram_cross * y) / over for x, y in zip(col_first, col_second)],
        [spread(gram_first * y - gram_cross * x) / over for x, y in zip(col_first, col_second)],
    ]
    for k in range(2):
        base_ref[k] = sum(
            weights[k][j] * parity_ref[:, j * width : (j + 1) * width] for j in range(spans)
        )
    from_earlier = from_current = to_rebuilt = range(members)
    if paired:
        from_earlier = sources_of(EARLIER_ROUNDS, members)
        from_current = sources_of(CURRENT_ROUNDS, members)
        to_rebuilt = targets_of(REBUILT_ROUNDS, members)
    for i, c in enumerate(from_earlier):
        column = [generator_ref[j, c] for j in range(spans)]
        alive = jnp.logical_and(first != c, second != c)
        for k in range(2):
            put(
                k * members + i,
                sum(weights[k][j] * jnp.where(alive, column[j], 0.0) for j in range(spans)),
            )
    for i, c in enumerate(from_current):
        for j in range(spans):
            put((2 + j) * members + i, spread(generator_ref[j, c]))
    for i, c in enumerate(to_rebuilt):
        put((2 + spans) * members + i, spread(jnp.where(first == c, 1.0, 0.0)))
    me = lax.axis_index("code")
    lost = jnp.logical_or(first == me, second == me)
    put((3 + spans) * members, spread(jnp.where(lost, 1.0, 0.0)))


def weigh(table_ref, start, rows):
    total = None
    for i, block in enumerate(rows):
        term = table_ref[start + i : start + i + 1, :] * block
        total = term if total is None else total + term
    return total


def rebuilt_for(base_ref, table_ref, rows):
    members = len(rows)
    rebuilt = [base_ref[k] - weigh(table_ref, k * members, rows) for k in range(2)]
    picks = table_ref.shape[0] - 1 - members
    return [
        jnp.where(table_ref[picks + i : picks + i + 1, :] > 0.5, *rebuilt) for i in range(members)
    ]


def rebuild_whole_kernel(base_ref, table_ref, rows_ref, out_ref):
    rows = [rows_ref[c] for c in range(rows_ref.shape[0])]
    for c, block in enumerate(rebuilt_for(base_ref, table_ref, rows)):
        out_ref[c] = block


def parity_whole_kernel(table_ref, rows_ref, out_ref):
    parity_into(out_ref, table_ref, [rows_ref[c] for c in range(rows_ref.shape[0])])


def parity_into(out_ref, table_ref, rows):
    members, width = len(rows), table_ref.shape[1]
    for j in range(out_ref.shape[1] // width):
        out_ref[:, j * width : (j + 1) * width] = weigh(table_ref, (2 + j) * members, rows)


def rebuild_paired_kernel(base_ref, table_ref, *refs):
    rows, outs = refs[: len(refs) // 2], refs[len(refs) // 2 :]
    for out_ref, block in zip(outs, rebuilt_for(base_ref, table_ref, [r[...] for r in rows])):
        out_ref[...] = block


def parity_paired_kernel(table_ref, *refs):
    rows, out_ref, done_ref = refs[:-2], refs[-2], refs[-1]
    parity_into(out_ref, table_ref, [r[...] for r in rows])
    done_ref[...] = jnp.zeros(done_ref.shape, done_ref.dtype)


def restore_kernel(table_ref, earlier_ref, held_back_by, *refs):
    pieces, out_ref = refs[:-1], refs[-1]
    members = len(pieces)
    last = table_ref.shape[0] - 1
    lost = table_ref[last : last + 1, :] > 0.5
    for c, piece in zip(sources_of(REBUILT_ROUNDS, members), pieces):
        out_ref[c] = jnp.where(lost, piece[...], earlier_ref[c])


def call(kernel, specs, outs, args, flops, **options):
    total = sum(x.size for x in args) + sum(o.size for o in jax.tree.leaves(outs))
    return pl.pallas_call(
        kernel,
        in_specs=specs,
        out_specs=jax.tree.map(lambda _: IN_VMEM, outs),
        out_shape=outs,
        compiler_params=pltpu.CompilerParams(vmem_limit_bytes=KERNEL_VMEM),
        cost_estimate=pl.CostEstimate(flops=flops, bytes_accessed=4 * total, transcendentals=0),
        **options,
    )(*args)


def floats(*shape):
    return jax.ShapeDtypeStruct(shape, jnp.float32)


def pass_on(pieces, rounds, members):
    return [
        lax.ppermute(
            piece, "code", [(d, target(d, *way, members)) for d in range(members)]
        )
        for way, piece in zip(rounds, pieces)
    ]


def cut(blocks, order):
    return [lax.dynamic_index_in_dim(blocks, c, 0, keepdims=False) for c in order]


def local(state_slab, previous_slab, previous_parity, generator, failed_ids):
    position = lax.axis_index("code")
    members = lax.axis_size("code")
    slab_rows, width = state_slab.shape[2:]
    spans = generator.shape[0]
    own_rows = slab_rows // members
    blocks = (members, own_rows, width)
    earlier = previous_slab.reshape(blocks)
    current = state_slab.reshape(blocks)
    paired = members == PAIRED_MEMBERS

    base, table = call(
        functools.partial(plan_kernel, paired),
        [IN_SMEM, IN_SMEM, IN_VMEM],
        (floats(2, own_rows, width), floats((3 + spans) * members + 1, width)),
        (failed_ids, generator, previous_parity[0]),
        4 * spans * own_rows * width,
    )
    parity_shape = floats(own_rows, spans * width)
    rebuild_cost = 4 * slab_rows * width
    parity_cost = 2 * spans * slab_rows * width
    if paired:
        block = floats(own_rows, width)
        own_earlier, *cut_earlier = cut(earlier, targets_of(EARLIER_ROUNDS, members))
        earlier_rows = pass_on(cut_earlier, EARLIER_ROUNDS, members)
        own_current, *cut_current = cut(current, targets_of(CURRENT_ROUNDS, members))
        outgoing = call(
            rebuild_paired_kernel,
            [IN_VMEM] * (members + 2),
            [block] * members,
            (base, table, own_earlier, *earlier_rows),
            rebuild_cost,
        )
        incoming = pass_on(outgoing[1:], REBUILT_ROUNDS, members)
        current_rows = [own_current, *pass_on(cut_current, CURRENT_ROUNDS, members)]
        new_parity, parity_done = call(
            parity_paired_kernel,
            [IN_VMEM] * (members + 1),
            (parity_shape, floats(8, 128)),
            (table, *current_rows),
            parity_cost,
        )
        restored_state = call(
            restore_kernel,
            [IN_VMEM, IN_VMEM, ANYWHERE] + [IN_VMEM] * members,
            floats(*blocks),
            (table, earlier, parity_done, outgoing[0], *incoming),
            0,
        )
    else:
        earlier_rows = lax.all_to_all(earlier, "code", 0, 0, tiled=True)
        current_rows = lax.all_to_all(current, "code", 0, 0, tiled=True)
        outgoing = call(
            rebuild_whole_kernel,
            [IN_VMEM] * 3,
            floats(*blocks),
            (base, table, earlier_rows),
            rebuild_cost,
        )
        incoming = lax.all_to_all(outgoing, "code", 0, 0, tiled=True)
        lost = (position == failed_ids[0, 0]) | (position == failed_ids[0, 1])
        restored_state = jnp.where(lost, incoming, earlier)
        new_parity = call(
            parity_whole_kernel,
            [IN_VMEM] * 2,
            parity_shape,
            (table, current_rows),
            parity_cost,
        )
    return (new_parity[None], restored_state.reshape(state_slab.shape))


def solution(mesh):
    placed = (
        P(("grp", "rep"), "code", None, None),
        P(("grp", "rep"), "code", None, None),
        P(("grp", "rep"), "code", None),
        P(),
        P(("grp", "rep"), None),
    )
    return jax.shard_map(
        local,
        mesh=mesh,
        in_specs=placed,
        out_specs=(P(("grp", "rep"), "code", None), P(("grp", "rep"), "code", None, None)),
        check_vma=False,
    )
```

```python
import functools

import jax
import jax.numpy as jnp
from jax import lax
from jax.experimental import pallas as pl
from jax.experimental.pallas import tpu as pltpu
from jax.sharding import PartitionSpec as P

IN_VMEM = pl.BlockSpec(memory_space=pltpu.VMEM)
IN_SMEM = pl.BlockSpec(memory_space=pltpu.SMEM)
ANYWHERE = pl.BlockSpec(memory_space=pl.ANY)

PAIRED_MEMBERS = 4
KERNEL_VMEM = 8 * 2**20

EARLIER_ROUNDS = (("xor", 2), ("xor", 3), ("xor", 1))
CURRENT_ROUNDS = (("xor", 3), ("xor", 2), ("xor", 1))
REBUILT_ROUNDS = (("on", 1), ("on", 2), ("on", 3))


def target(d, way, n, members):
    return d ^ n if way == "xor" else (d + n) % members


def source(d, way, n, members):
    return d ^ n if way == "xor" else (d + members - n) % members


def targets_of(rounds, members):
    me = lax.axis_index("code")
    return [me] + [target(me, *way, members) for way in rounds]


def sources_of(rounds, members):
    me = lax.axis_index("code")
    return [me] + [source(me, *way, members) for way in rounds]


def plan_kernel(paired, ids_ref, generator_ref, parity_ref, base_ref, table_ref):
    spans, members = generator_ref.shape
    width = base_ref.shape[2]
    first, second = ids_ref[0, 0], ids_ref[0, 1]
    col_first = [generator_ref[j, first] for j in range(spans)]
    col_second = [generator_ref[j, second] for j in range(spans)]
    gram_first = sum(x * x for x in col_first)
    gram_cross = sum(x * y for x, y in zip(col_first, col_second))
    gram_second = sum(y * y for y in col_second)
    determinant = gram_first * gram_second - gram_cross * gram_cross

    def spread(value):
        return jnp.full((1, width), value, jnp.float32)

    def put(row, value):
        table_ref[row : row + 1, :] = value

    over = spread(determinant)
    weights = [
        [spread(gram_second * x - gram_cross * y) / over for x, y in zip(col_first, col_second)],
        [spread(gram_first * y - gram_cross * x) / over for x, y in zip(col_first, col_second)],
    ]
    for k in range(2):
        base_ref[k] = sum(
            weights[k][j] * parity_ref[:, j * width : (j + 1) * width] for j in range(spans)
        )
    from_earlier = from_current = to_rebuilt = range(members)
    if paired:
        from_earlier = sources_of(EARLIER_ROUNDS, members)
        from_current = sources_of(CURRENT_ROUNDS, members)
        to_rebuilt = targets_of(REBUILT_ROUNDS, members)
    for i, c in enumerate(from_earlier):
        column = [generator_ref[j, c] for j in range(spans)]
        alive = jnp.logical_and(first != c, second != c)
        for k in range(2):
            put(
                k * members + i,
                sum(weights[k][j] * jnp.where(alive, column[j], 0.0) for j in range(spans)),
            )
    for i, c in enumerate(from_current):
        for j in range(spans):
            put((2 + j) * members + i, spread(generator_ref[j, c]))
    for i, c in enumerate(to_rebuilt):
        put((2 + spans) * members + i, spread(jnp.where(first == c, 1.0, 0.0)))
    me = lax.axis_index("code")
    lost = jnp.logical_or(first == me, second == me)
    put((3 + spans) * members, spread(jnp.where(lost, 1.0, 0.0)))


def weigh(table_ref, start, rows):
    total = None
    for i, block in enumerate(rows):
        term = table_ref[start + i : start + i + 1, :] * block
        total = term if total is None else total + term
    return total


def rebuilt_for(base_ref, table_ref, rows):
    members = len(rows)
    rebuilt = [base_ref[k] - weigh(table_ref, k * members, rows) for k in range(2)]
    picks = table_ref.shape[0] - 1 - members
    return [
        jnp.where(table_ref[picks + i : picks + i + 1, :] > 0.5, *rebuilt) for i in range(members)
    ]


def rebuild_whole_kernel(base_ref, table_ref, rows_ref, out_ref):
    rows = [rows_ref[c] for c in range(rows_ref.shape[0])]
    for c, block in enumerate(rebuilt_for(base_ref, table_ref, rows)):
        out_ref[c] = block


def parity_whole_kernel(table_ref, rows_ref, out_ref):
    parity_into(out_ref, table_ref, [rows_ref[c] for c in range(rows_ref.shape[0])])


def parity_into(out_ref, table_ref, rows):
    members, width = len(rows), table_ref.shape[1]
    for j in range(out_ref.shape[1] // width):
        out_ref[:, j * width : (j + 1) * width] = weigh(table_ref, (2 + j) * members, rows)


def rebuild_paired_kernel(base_ref, table_ref, *refs):
    rows, outs = refs[: len(refs) // 2], refs[len(refs) // 2 :]
    for out_ref, block in zip(outs, rebuilt_for(base_ref, table_ref, [r[...] for r in rows])):
        out_ref[...] = block


def parity_paired_kernel(table_ref, *refs):
    rows, out_ref, done_ref = refs[:-2], refs[-2], refs[-1]
    parity_into(out_ref, table_ref, [r[...] for r in rows])
    done_ref[...] = jnp.zeros(done_ref.shape, done_ref.dtype)


def restore_kernel(table_ref, earlier_ref, held_back_by, *refs):
    pieces, out_ref = refs[:-1], refs[-1]
    members = len(pieces)
    last = table_ref.shape[0] - 1
    lost = table_ref[last : last + 1, :] > 0.5
    for c, piece in zip(sources_of(REBUILT_ROUNDS, members), pieces):
        out_ref[c] = jnp.where(lost, piece[...], earlier_ref[c])


def call(kernel, specs, outs, args, flops, **options):
    total = sum(x.size for x in args) + sum(o.size for o in jax.tree.leaves(outs))
    return pl.pallas_call(
        kernel,
        in_specs=specs,
        out_specs=jax.tree.map(lambda _: IN_VMEM, outs),
        out_shape=outs,
        compiler_params=pltpu.CompilerParams(vmem_limit_bytes=KERNEL_VMEM),
        cost_estimate=pl.CostEstimate(flops=flops, bytes_accessed=4 * total, transcendentals=0),
        **options,
    )(*args)


def floats(*shape):
    return jax.ShapeDtypeStruct(shape, jnp.float32)


def pass_on(pieces, rounds, members):
    return [
        lax.ppermute(
            piece, "code", [(d, target(d, *way, members)) for d in range(members)]
        )
        for way, piece in zip(rounds, pieces)
    ]


def cut(blocks, order):
    return [lax.dynamic_index_in_dim(blocks, c, 0, keepdims=False) for c in order]


def local(state_slab, previous_slab, previous_parity, generator, failed_ids):
    position = lax.axis_index("code")
    members = lax.axis_size("code")
    slab_rows, width = state_slab.shape[2:]
    spans = generator.shape[0]
    own_rows = slab_rows // members
    blocks = (members, own_rows, width)
    earlier = previous_slab.reshape(blocks)
    current = state_slab.reshape(blocks)
    paired = members == PAIRED_MEMBERS

    base, table = call(
        functools.partial(plan_kernel, paired),
        [IN_SMEM, IN_SMEM, IN_VMEM],
        (floats(2, own_rows, width), floats((3 + spans) * members + 1, width)),
        (failed_ids, generator, previous_parity[0]),
        4 * spans * own_rows * width,
    )
    parity_shape = floats(own_rows, spans * width)
    rebuild_cost = 4 * slab_rows * width
    parity_cost = 2 * spans * slab_rows * width
    if paired:
        block = floats(own_rows, width)
        own_earlier, *cut_earlier = cut(earlier, targets_of(EARLIER_ROUNDS, members))
        earlier_rows = pass_on(cut_earlier, EARLIER_ROUNDS, members)
        own_current, *cut_current = cut(current, targets_of(CURRENT_ROUNDS, members))
        outgoing = call(
            rebuild_paired_kernel,
            [IN_VMEM] * (members + 2),
            [block] * members,
            (base, table, own_earlier, *earlier_rows),
            rebuild_cost,
        )
        incoming = pass_on(outgoing[1:], REBUILT_ROUNDS, members)
        current_rows = [own_current, *pass_on(cut_current, CURRENT_ROUNDS, members)]
        new_parity, parity_done = call(
            parity_paired_kernel,
            [IN_VMEM] * (members + 1),
            (parity_shape, floats(8, 128)),
            (table, *current_rows),
            parity_cost,
        )
        restored_state = call(
            restore_kernel,
            [IN_VMEM, IN_VMEM, ANYWHERE] + [IN_VMEM] * members,
            floats(*blocks),
            (table, earlier, parity_done, outgoing[0], *incoming),
            0,
        )
    else:
        earlier_rows = lax.all_to_all(earlier, "code", 0, 0, tiled=True)
        current_rows = lax.all_to_all(current, "code", 0, 0, tiled=True)
        outgoing = call(
            rebuild_whole_kernel,
            [IN_VMEM] * 3,
            floats(*blocks),
            (base, table, earlier_rows),
            rebuild_cost,
        )
        incoming = lax.all_to_all(outgoing, "code", 0, 0, tiled=True)
        lost = (position == failed_ids[0, 0]) | (position == failed_ids[0, 1])
        restored_state = jnp.where(lost, incoming, earlier)
        new_parity = call(
            parity_whole_kernel,
            [IN_VMEM] * 2,
            parity_shape,
            (table, current_rows),
            parity_cost,
        )
    return (new_parity[None], restored_state.reshape(state_slab.shape))


def solution(mesh):
    placed = (
        P(("grp", "rep"), "code", None, None),
        P(("grp", "rep"), "code", None, None),
        P(("grp", "rep"), "code", None),
        P(),
        P(("grp", "rep"), None),
    )
    return jax.shard_map(
        local,
        mesh=mesh,
        in_specs=placed,
        out_specs=(P(("grp", "rep"), "code", None), P(("grp", "rep"), "code", None, None)),
        check_vma=False,
    )
```

```python
import functools

import jax
import jax.numpy as jnp
from jax import lax
from jax.experimental import pallas as pl
from jax.experimental.pallas import tpu as pltpu
from jax.sharding import PartitionSpec as P

IN_VMEM = pl.BlockSpec(memory_space=pltpu.VMEM)
IN_SMEM = pl.BlockSpec(memory_space=pltpu.SMEM)
ANYWHERE = pl.BlockSpec(memory_space=pl.ANY)

PAIRED_MEMBERS = 4
KERNEL_VMEM = 8 * 2**20

EARLIER_ROUNDS = (("xor", 1), ("xor", 3), ("xor", 2))
CURRENT_ROUNDS = (("on", 3), ("on", 2), ("on", 1))
REBUILT_ROUNDS = (("on", 1), ("on", 2), ("on", 3))


def target(d, way, n, members):
    return d ^ n if way == "xor" else (d + n) % members


def source(d, way, n, members):
    return d ^ n if way == "xor" else (d + members - n) % members


def targets_of(rounds, members):
    me = lax.axis_index("code")
    return [me] + [target(me, *way, members) for way in rounds]


def sources_of(rounds, members):
    me = lax.axis_index("code")
    return [me] + [source(me, *way, members) for way in rounds]


def plan_kernel(paired, ids_ref, generator_ref, parity_ref, base_ref, table_ref):
    spans, members = generator_ref.shape
    width = base_ref.shape[2]
    first, second = ids_ref[0, 0], ids_ref[0, 1]
    col_first = [generator_ref[j, first] for j in range(spans)]
    col_second = [generator_ref[j, second] for j in range(spans)]
    gram_first = sum(x * x for x in col_first)
    gram_cross = sum(x * y for x, y in zip(col_first, col_second))
    gram_second = sum(y * y for y in col_second)
    determinant = gram_first * gram_second - gram_cross * gram_cross

    def spread(value):
        return jnp.full((1, width), value, jnp.float32)

    def put(row, value):
        table_ref[row : row + 1, :] = value

    over = spread(determinant)
    weights = [
        [spread(gram_second * x - gram_cross * y) / over for x, y in zip(col_first, col_second)],
        [spread(gram_first * y - gram_cross * x) / over for x, y in zip(col_first, col_second)],
    ]
    for k in range(2):
        base_ref[k] = sum(
            weights[k][j] * parity_ref[:, j * width : (j + 1) * width] for j in range(spans)
        )
    from_earlier = from_current = to_rebuilt = range(members)
    if paired:
        from_earlier = sources_of(EARLIER_ROUNDS, members)
        from_current = sources_of(CURRENT_ROUNDS, members)
        to_rebuilt = targets_of(REBUILT_ROUNDS, members)
    for i, c in enumerate(from_earlier):
        column = [generator_ref[j, c] for j in range(spans)]
        alive = jnp.logical_and(first != c, second != c)
        for k in range(2):
            put(
                k * members + i,
                sum(weights[k][j] * jnp.where(alive, column[j], 0.0) for j in range(spans)),
            )
    for i, c in enumerate(from_current):
        for j in range(spans):
            put((2 + j) * members + i, spread(generator_ref[j, c]))
    for i, c in enumerate(to_rebuilt):
        put((2 + spans) * members + i, spread(jnp.where(first == c, 1.0, 0.0)))
    me = lax.axis_index("code")
    lost = jnp.logical_or(first == me, second == me)
    put((3 + spans) * members, spread(jnp.where(lost, 1.0, 0.0)))


def weigh(table_ref, start, rows):
    total = None
    for i, block in enumerate(rows):
        term = table_ref[start + i : start + i + 1, :] * block
        total = term if total is None else total + term
    return total


def rebuilt_for(base_ref, table_ref, rows):
    members = len(rows)
    rebuilt = [base_ref[k] - weigh(table_ref, k * members, rows) for k in range(2)]
    picks = table_ref.shape[0] - 1 - members
    return [
        jnp.where(table_ref[picks + i : picks + i + 1, :] > 0.5, *rebuilt) for i in range(members)
    ]


def rebuild_whole_kernel(base_ref, table_ref, rows_ref, out_ref):
    rows = [rows_ref[c] for c in range(rows_ref.shape[0])]
    for c, block in enumerate(rebuilt_for(base_ref, table_ref, rows)):
        out_ref[c] = block


def parity_whole_kernel(table_ref, rows_ref, out_ref):
    parity_into(out_ref, table_ref, [rows_ref[c] for c in range(rows_ref.shape[0])])


def parity_into(out_ref, table_ref, rows):
    members, width = len(rows), table_ref.shape[1]
    for j in range(out_ref.shape[1] // width):
        out_ref[:, j * width : (j + 1) * width] = weigh(table_ref, (2 + j) * members, rows)


def rebuild_paired_kernel(base_ref, table_ref, *refs):
    rows, outs = refs[: len(refs) // 2], refs[len(refs) // 2 :]
    for out_ref, block in zip(outs, rebuilt_for(base_ref, table_ref, [r[...] for r in rows])):
        out_ref[...] = block


def parity_paired_kernel(table_ref, *refs):
    rows, out_ref, done_ref = refs[:-2], refs[-2], refs[-1]
    parity_into(out_ref, table_ref, [r[...] for r in rows])
    done_ref[...] = jnp.zeros(done_ref.shape, done_ref.dtype)


def settle_kernel(earlier_ref, out_ref):
    out_ref[...] = earlier_ref[...]


def restore_kernel(table_ref, held_back_by, settled_ref, *refs):
    pieces, (out_ref, sems) = refs[:-2], refs[-2:]
    members = len(pieces)
    last = table_ref.shape[0] - 1

    @pl.when(table_ref[last, 0] > 0.5)
    def _():
        copies = [
            pltpu.make_async_copy(piece, out_ref.at[c], sems.at[i])
            for i, (c, piece) in enumerate(zip(sources_of(REBUILT_ROUNDS, members), pieces))
        ]
        for copy in copies:
            copy.start()
        for copy in copies:
            copy.wait()


def call(kernel, specs, outs, args, flops, **options):
    total = sum(x.size for x in args) + sum(o.size for o in jax.tree.leaves(outs))
    options.setdefault("out_specs", jax.tree.map(lambda _: IN_VMEM, outs))
    return pl.pallas_call(
        kernel,
        in_specs=specs,
        out_shape=outs,
        compiler_params=pltpu.CompilerParams(vmem_limit_bytes=KERNEL_VMEM),
        cost_estimate=pl.CostEstimate(flops=flops, bytes_accessed=4 * total, transcendentals=0),
        **options,
    )(*args)


def floats(*shape):
    return jax.ShapeDtypeStruct(shape, jnp.float32)


def pass_on(pieces, rounds, members):
    return [
        lax.ppermute(
            piece, "code", [(d, target(d, *way, members)) for d in range(members)]
        )
        for way, piece in zip(rounds, pieces)
    ]


def cut(blocks, order):
    return [lax.dynamic_index_in_dim(blocks, c, 0, keepdims=False) for c in order]


def local(state_slab, previous_slab, previous_parity, generator, failed_ids):
    position = lax.axis_index("code")
    members = lax.axis_size("code")
    slab_rows, width = state_slab.shape[2:]
    spans = generator.shape[0]
    own_rows = slab_rows // members
    blocks = (members, own_rows, width)
    earlier = previous_slab.reshape(blocks)
    current = state_slab.reshape(blocks)
    paired = members == PAIRED_MEMBERS

    base, table = call(
        functools.partial(plan_kernel, paired),
        [IN_SMEM, IN_SMEM, IN_VMEM],
        (floats(2, own_rows, width), floats((3 + spans) * members + 1, width)),
        (failed_ids, generator, previous_parity[0]),
        4 * spans * own_rows * width,
    )
    parity_shape = floats(own_rows, spans * width)
    rebuild_cost = 4 * slab_rows * width
    parity_cost = 2 * spans * slab_rows * width
    if paired:
        block = floats(own_rows, width)
        own_earlier, *cut_earlier = cut(earlier, targets_of(EARLIER_ROUNDS, members))
        earlier_rows = pass_on(cut_earlier, EARLIER_ROUNDS, members)
        own_current, *cut_current = cut(current, targets_of(CURRENT_ROUNDS, members))
        outgoing = call(
            rebuild_paired_kernel,
            [IN_VMEM] * (members + 2),
            [block] * members,
            (base, table, own_earlier, *earlier_rows),
            rebuild_cost,
        )
        incoming = pass_on(outgoing[1:], REBUILT_ROUNDS, members)
        current_rows = [own_current, *pass_on(cut_current, CURRENT_ROUNDS, members)]
        new_parity, parity_done = call(
            parity_paired_kernel,
            [IN_VMEM] * (members + 1),
            (parity_shape, floats(8, 128)),
            (table, *current_rows),
            parity_cost,
        )
        settled = call(settle_kernel, [IN_VMEM], floats(*blocks), (earlier,), 0)
        restored_state = call(
            restore_kernel,
            [IN_VMEM, ANYWHERE, ANYWHERE] + [IN_VMEM] * members,
            floats(*blocks),
            (table, parity_done, settled, outgoing[0], *incoming),
            0,
            out_specs=ANYWHERE,
            input_output_aliases={2: 0},
            scratch_shapes=[pltpu.SemaphoreType.DMA((members,))],
        )
    else:
        earlier_rows = lax.all_to_all(earlier, "code", 0, 0, tiled=True)
        current_rows = lax.all_to_all(current, "code", 0, 0, tiled=True)
        outgoing = call(
            rebuild_whole_kernel,
            [IN_VMEM] * 3,
            floats(*blocks),
            (base, table, earlier_rows),
            rebuild_cost,
        )
        incoming = lax.all_to_all(outgoing, "code", 0, 0, tiled=True)
        lost = (position == failed_ids[0, 0]) | (position == failed_ids[0, 1])
        restored_state = jnp.where(lost, incoming, earlier)
        new_parity = call(
            parity_whole_kernel,
            [IN_VMEM] * 2,
            parity_shape,
            (table, current_rows),
            parity_cost,
        )
    return (new_parity[None], restored_state.reshape(state_slab.shape))


def solution(mesh):
    placed = (
        P(("grp", "rep"), "code", None, None),
        P(("grp", "rep"), "code", None, None),
        P(("grp", "rep"), "code", None),
        P(),
        P(("grp", "rep"), None),
    )
    return jax.shard_map(
        local,
        mesh=mesh,
        in_specs=placed,
        out_specs=(P(("grp", "rep"), "code", None), P(("grp", "rep"), "code", None, None)),
        check_vma=False,
    )
```

```python
import functools

import jax
import jax.numpy as jnp
from jax import lax
from jax.experimental import pallas as pl
from jax.experimental.pallas import tpu as pltpu
from jax.sharding import PartitionSpec as P

IN_VMEM = pl.BlockSpec(memory_space=pltpu.VMEM)
IN_SMEM = pl.BlockSpec(memory_space=pltpu.SMEM)
ANYWHERE = pl.BlockSpec(memory_space=pl.ANY)

PAIRED_MEMBERS = 4
KERNEL_VMEM = 8 * 2**20

EARLIER_ROUNDS = (("xor", 1), ("xor", 2), ("xor", 3))
CURRENT_ROUNDS = (("on", 3), ("on", 2), ("on", 1))
REBUILT_ROUNDS = (("on", 1), ("on", 2), ("on", 3))


def target(d, way, n, members):
    return d ^ n if way == "xor" else (d + n) % members


def source(d, way, n, members):
    return d ^ n if way == "xor" else (d + members - n) % members


def targets_of(rounds, members):
    me = lax.axis_index("code")
    return [me] + [target(me, *way, members) for way in rounds]


def sources_of(rounds, members):
    me = lax.axis_index("code")
    return [me] + [source(me, *way, members) for way in rounds]


def plan_kernel(paired, ids_ref, generator_ref, parity_ref, base_ref, table_ref):
    spans, members = generator_ref.shape
    width = base_ref.shape[2]
    first, second = ids_ref[0, 0], ids_ref[0, 1]
    col_first = [generator_ref[j, first] for j in range(spans)]
    col_second = [generator_ref[j, second] for j in range(spans)]
    gram_first = sum(x * x for x in col_first)
    gram_cross = sum(x * y for x, y in zip(col_first, col_second))
    gram_second = sum(y * y for y in col_second)
    determinant = gram_first * gram_second - gram_cross * gram_cross

    def spread(value):
        return jnp.full((1, width), value, jnp.float32)

    def put(row, value):
        table_ref[row : row + 1, :] = value

    over = spread(determinant)
    weights = [
        [spread(gram_second * x - gram_cross * y) / over for x, y in zip(col_first, col_second)],
        [spread(gram_first * y - gram_cross * x) / over for x, y in zip(col_first, col_second)],
    ]
    for k in range(2):
        base_ref[k] = sum(
            weights[k][j] * parity_ref[:, j * width : (j + 1) * width] for j in range(spans)
        )
    from_earlier = from_current = to_rebuilt = range(members)
    if paired:
        from_earlier = sources_of(EARLIER_ROUNDS, members)
        from_current = sources_of(CURRENT_ROUNDS, members)
        to_rebuilt = targets_of(REBUILT_ROUNDS, members)
    for i, c in enumerate(from_earlier):
        column = [generator_ref[j, c] for j in range(spans)]
        alive = jnp.logical_and(first != c, second != c)
        for k in range(2):
            put(
                k * members + i,
                sum(weights[k][j] * jnp.where(alive, column[j], 0.0) for j in range(spans)),
            )
    for i, c in enumerate(from_current):
        for j in range(spans):
            put((2 + j) * members + i, spread(generator_ref[j, c]))
    for i, c in enumerate(to_rebuilt):
        put((2 + spans) * members + i, spread(jnp.where(first == c, 1.0, 0.0)))
    me = lax.axis_index("code")
    lost = jnp.logical_or(first == me, second == me)
    put((3 + spans) * members, spread(jnp.where(lost, 1.0, 0.0)))


def weigh(table_ref, start, rows):
    total = None
    for i, block in enumerate(rows):
        term = table_ref[start + i : start + i + 1, :] * block
        total = term if total is None else total + term
    return total


def rebuilt_for(base_ref, table_ref, rows):
    members = len(rows)
    rebuilt = [base_ref[k] - weigh(table_ref, k * members, rows) for k in range(2)]
    picks = table_ref.shape[0] - 1 - members
    return [
        jnp.where(table_ref[picks + i : picks + i + 1, :] > 0.5, *rebuilt) for i in range(members)
    ]


def rebuild_whole_kernel(base_ref, table_ref, rows_ref, out_ref):
    rows = [rows_ref[c] for c in range(rows_ref.shape[0])]
    for c, block in enumerate(rebuilt_for(base_ref, table_ref, rows)):
        out_ref[c] = block


def parity_whole_kernel(table_ref, rows_ref, out_ref):
    parity_into(out_ref, table_ref, [rows_ref[c] for c in range(rows_ref.shape[0])])


def parity_into(out_ref, table_ref, rows):
    members, width = len(rows), table_ref.shape[1]
    for j in range(out_ref.shape[1] // width):
        out_ref[:, j * width : (j + 1) * width] = weigh(table_ref, (2 + j) * members, rows)


def rebuild_paired_kernel(base_ref, table_ref, *refs):
    rows, outs = refs[: len(refs) // 2], refs[len(refs) // 2 :]
    for out_ref, block in zip(outs, rebuilt_for(base_ref, table_ref, [r[...] for r in rows])):
        out_ref[...] = block


def parity_paired_kernel(table_ref, *refs):
    rows, out_ref, done_ref = refs[:-2], refs[-2], refs[-1]
    parity_into(out_ref, table_ref, [r[...] for r in rows])
    done_ref[...] = jnp.zeros(done_ref.shape, done_ref.dtype)


def settle_kernel(earlier_ref, out_ref):
    out_ref[...] = earlier_ref[...]


def restore_kernel(table_ref, held_back_by, settled_ref, *refs):
    pieces, (out_ref, sems) = refs[:-2], refs[-2:]
    members = len(pieces)
    last = table_ref.shape[0] - 1

    @pl.when(table_ref[last, 0] > 0.5)
    def _():
        copies = [
            pltpu.make_async_copy(piece, out_ref.at[c], sems.at[i])
            for i, (c, piece) in enumerate(zip(sources_of(REBUILT_ROUNDS, members), pieces))
        ]
        for copy in copies:
            copy.start()
        for copy in copies:
            copy.wait()


def call(kernel, specs, outs, args, flops, **options):
    total = sum(x.size for x in args) + sum(o.size for o in jax.tree.leaves(outs))
    options.setdefault("out_specs", jax.tree.map(lambda _: IN_VMEM, outs))
    return pl.pallas_call(
        kernel,
        in_specs=specs,
        out_shape=outs,
        compiler_params=pltpu.CompilerParams(vmem_limit_bytes=KERNEL_VMEM),
        cost_estimate=pl.CostEstimate(flops=flops, bytes_accessed=4 * total, transcendentals=0),
        **options,
    )(*args)


def floats(*shape):
    return jax.ShapeDtypeStruct(shape, jnp.float32)


def pass_on(pieces, rounds, members):
    return [
        lax.ppermute(
            piece, "code", [(d, target(d, *way, members)) for d in range(members)]
        )
        for way, piece in zip(rounds, pieces)
    ]


def cut(blocks, order):
    return [lax.dynamic_index_in_dim(blocks, c, 0, keepdims=False) for c in order]


def local(state_slab, previous_slab, previous_parity, generator, failed_ids):
    position = lax.axis_index("code")
    members = lax.axis_size("code")
    slab_rows, width = state_slab.shape[2:]
    spans = generator.shape[0]
    own_rows = slab_rows // members
    blocks = (members, own_rows, width)
    earlier = previous_slab.reshape(blocks)
    current = state_slab.reshape(blocks)
    paired = members == PAIRED_MEMBERS

    base, table = call(
        functools.partial(plan_kernel, paired),
        [IN_SMEM, IN_SMEM, IN_VMEM],
        (floats(2, own_rows, width), floats((3 + spans) * members + 1, width)),
        (failed_ids, generator, previous_parity[0]),
        4 * spans * own_rows * width,
    )
    parity_shape = floats(own_rows, spans * width)
    rebuild_cost = 4 * slab_rows * width
    parity_cost = 2 * spans * slab_rows * width
    if paired:
        block = floats(own_rows, width)
        own, *others = targets_of(EARLIER_ROUNDS, members)
        far = cut(earlier, [others[1], others[2]])
        later, far[0] = lax.optimization_barrier((earlier, far[0]))
        own_earlier, next_earlier = cut(later, [own, others[0]])
        cut_earlier = far[:0] + [next_earlier] + far[0:]
        earlier_rows = pass_on(cut_earlier, EARLIER_ROUNDS, members)
        own_current, *cut_current = cut(current, targets_of(CURRENT_ROUNDS, members))
        outgoing = call(
            rebuild_paired_kernel,
            [IN_VMEM] * (members + 2),
            [block] * members,
            (base, table, own_earlier, *earlier_rows),
            rebuild_cost,
        )
        incoming = pass_on(outgoing[1:], REBUILT_ROUNDS, members)
        current_rows = [own_current, *pass_on(cut_current, CURRENT_ROUNDS, members)]
        new_parity, parity_done = call(
            parity_paired_kernel,
            [IN_VMEM] * (members + 1),
            (parity_shape, floats(8, 128)),
            (table, *current_rows),
            parity_cost,
        )
        settled = call(settle_kernel, [IN_VMEM], floats(*blocks), (earlier,), 0)
        restored_state = call(
            restore_kernel,
            [IN_VMEM, ANYWHERE, ANYWHERE] + [IN_VMEM] * members,
            floats(*blocks),
            (table, parity_done, settled, outgoing[0], *incoming),
            0,
            out_specs=ANYWHERE,
            input_output_aliases={2: 0},
            scratch_shapes=[pltpu.SemaphoreType.DMA((members,))],
        )
    else:
        earlier_rows = lax.all_to_all(earlier, "code", 0, 0, tiled=True)
        current_rows = lax.all_to_all(current, "code", 0, 0, tiled=True)
        outgoing = call(
            rebuild_whole_kernel,
            [IN_VMEM] * 3,
            floats(*blocks),
            (base, table, earlier_rows),
            rebuild_cost,
        )
        incoming = lax.all_to_all(outgoing, "code", 0, 0, tiled=True)
        lost = (position == failed_ids[0, 0]) | (position == failed_ids[0, 1])
        restored_state = jnp.where(lost, incoming, earlier)
        new_parity = call(
            parity_whole_kernel,
            [IN_VMEM] * 2,
            parity_shape,
            (table, current_rows),
            parity_cost,
        )
    return (new_parity[None], restored_state.reshape(state_slab.shape))


def solution(mesh):
    placed = (
        P(("grp", "rep"), "code", None, None),
        P(("grp", "rep"), "code", None, None),
        P(("grp", "rep"), "code", None),
        P(),
        P(("grp", "rep"), None),
    )
    return jax.shard_map(
        local,
        mesh=mesh,
        in_specs=placed,
        out_specs=(P(("grp", "rep"), "code", None), P(("grp", "rep"), "code", None, None)),
        check_vma=False,
    )
```

```python
import functools

import jax
import jax.numpy as jnp
from jax import lax
from jax.experimental import pallas as pl
from jax.experimental.pallas import tpu as pltpu
from jax.sharding import PartitionSpec as P

IN_VMEM = pl.BlockSpec(memory_space=pltpu.VMEM)
IN_SMEM = pl.BlockSpec(memory_space=pltpu.SMEM)
ANYWHERE = pl.BlockSpec(memory_space=pl.ANY)

PAIRED_MEMBERS = 4
KERNEL_VMEM = 8 * 2**20

EARLIER_ROUNDS = (("xor", 1), ("xor", 3), ("xor", 2))
CURRENT_ROUNDS = (("on", 3), ("on", 2), ("on", 1))
REBUILT_ROUNDS = (("on", 1), ("on", 2), ("on", 3))


def target(d, way, n, members):
    return d ^ n if way == "xor" else (d + n) % members


def source(d, way, n, members):
    return d ^ n if way == "xor" else (d + members - n) % members


def targets_of(rounds, members):
    me = lax.axis_index("code")
    return [me] + [target(me, *way, members) for way in rounds]


def sources_of(rounds, members):
    me = lax.axis_index("code")
    return [me] + [source(me, *way, members) for way in rounds]


def plan_kernel(paired, ids_ref, generator_ref, parity_ref, base_ref, table_ref):
    spans, members = generator_ref.shape
    width = base_ref.shape[2]
    first, second = ids_ref[0, 0], ids_ref[0, 1]
    col_first = [generator_ref[j, first] for j in range(spans)]
    col_second = [generator_ref[j, second] for j in range(spans)]
    gram_first = sum(x * x for x in col_first)
    gram_cross = sum(x * y for x, y in zip(col_first, col_second))
    gram_second = sum(y * y for y in col_second)
    determinant = gram_first * gram_second - gram_cross * gram_cross

    def spread(value):
        return jnp.full((1, width), value, jnp.float32)

    def put(row, value):
        table_ref[row : row + 1, :] = value

    over = spread(determinant)
    weights = [
        [spread(gram_second * x - gram_cross * y) / over for x, y in zip(col_first, col_second)],
        [spread(gram_first * y - gram_cross * x) / over for x, y in zip(col_first, col_second)],
    ]
    for k in range(2):
        base_ref[k] = sum(
            weights[k][j] * parity_ref[:, j * width : (j + 1) * width] for j in range(spans)
        )
    from_earlier = from_current = to_rebuilt = range(members)
    if paired:
        from_earlier = sources_of(EARLIER_ROUNDS, members)
        from_current = sources_of(CURRENT_ROUNDS, members)
        to_rebuilt = targets_of(REBUILT_ROUNDS, members)
    for i, c in enumerate(from_earlier):
        column = [generator_ref[j, c] for j in range(spans)]
        alive = jnp.logical_and(first != c, second != c)
        for k in range(2):
            put(
                k * members + i,
                sum(weights[k][j] * jnp.where(alive, column[j], 0.0) for j in range(spans)),
            )
    for i, c in enumerate(from_current):
        for j in range(spans):
            put((2 + j) * members + i, spread(generator_ref[j, c]))
    for i, c in enumerate(to_rebuilt):
        put((2 + spans) * members + i, spread(jnp.where(first == c, 1.0, 0.0)))
    me = lax.axis_index("code")
    lost = jnp.logical_or(first == me, second == me)
    put((3 + spans) * members, spread(jnp.where(lost, 1.0, 0.0)))


def weigh(table_ref, start, rows):
    total = None
    for i, block in enumerate(rows):
        term = table_ref[start + i : start + i + 1, :] * block
        total = term if total is None else total + term
    return total


def rebuilt_for(base_ref, table_ref, rows):
    members = len(rows)
    rebuilt = [base_ref[k] - weigh(table_ref, k * members, rows) for k in range(2)]
    picks = table_ref.shape[0] - 1 - members
    return [
        jnp.where(table_ref[picks + i : picks + i + 1, :] > 0.5, *rebuilt) for i in range(members)
    ]


def rebuild_whole_kernel(base_ref, table_ref, rows_ref, out_ref):
    rows = [rows_ref[c] for c in range(rows_ref.shape[0])]
    for c, block in enumerate(rebuilt_for(base_ref, table_ref, rows)):
        out_ref[c] = block


def parity_whole_kernel(table_ref, rows_ref, out_ref):
    parity_into(out_ref, table_ref, [rows_ref[c] for c in range(rows_ref.shape[0])])


def parity_into(out_ref, table_ref, rows):
    members, width = len(rows), table_ref.shape[1]
    for j in range(out_ref.shape[1] // width):
        out_ref[:, j * width : (j + 1) * width] = weigh(table_ref, (2 + j) * members, rows)


def rebuild_paired_kernel(base_ref, table_ref, *refs):
    rows, outs = refs[: len(refs) // 2], refs[len(refs) // 2 :]
    for out_ref, block in zip(outs, rebuilt_for(base_ref, table_ref, [r[...] for r in rows])):
        out_ref[...] = block


def parity_paired_kernel(table_ref, *refs):
    rows, out_ref, done_ref = refs[:-2], refs[-2], refs[-1]
    parity_into(out_ref, table_ref, [r[...] for r in rows])
    done_ref[...] = jnp.zeros(done_ref.shape, done_ref.dtype)


def settle_kernel(earlier_ref, out_ref):
    out_ref[...] = earlier_ref[...]


def restore_kernel(table_ref, held_back_by, settled_ref, *refs):
    pieces, (out_ref, sems) = refs[:-2], refs[-2:]
    members = len(pieces)
    last = table_ref.shape[0] - 1

    @pl.when(table_ref[last, 0] > 0.5)
    def _():
        copies = [
            pltpu.make_async_copy(piece, out_ref.at[c], sems.at[i])
            for i, (c, piece) in enumerate(zip(sources_of(REBUILT_ROUNDS, members), pieces))
        ]
        for copy in copies:
            copy.start()
        for copy in copies:
            copy.wait()


def call(kernel, specs, outs, args, flops, **options):
    total = sum(x.size for x in args) + sum(o.size for o in jax.tree.leaves(outs))
    options.setdefault("out_specs", jax.tree.map(lambda _: IN_VMEM, outs))
    return pl.pallas_call(
        kernel,
        in_specs=specs,
        out_shape=outs,
        compiler_params=pltpu.CompilerParams(vmem_limit_bytes=KERNEL_VMEM),
        cost_estimate=pl.CostEstimate(flops=flops, bytes_accessed=4 * total, transcendentals=0),
        **options,
    )(*args)


def floats(*shape):
    return jax.ShapeDtypeStruct(shape, jnp.float32)


def pass_on(pieces, rounds, members):
    return [
        lax.ppermute(
            piece, "code", [(d, target(d, *way, members)) for d in range(members)]
        )
        for way, piece in zip(rounds, pieces)
    ]


def cut(blocks, order):
    return [lax.dynamic_index_in_dim(blocks, c, 0, keepdims=False) for c in order]


def local(state_slab, previous_slab, previous_parity, generator, failed_ids):
    position = lax.axis_index("code")
    members = lax.axis_size("code")
    slab_rows, width = state_slab.shape[2:]
    spans = generator.shape[0]
    own_rows = slab_rows // members
    blocks = (members, own_rows, width)
    earlier = previous_slab.reshape(blocks)
    current = state_slab.reshape(blocks)
    paired = members == PAIRED_MEMBERS

    base, table = call(
        functools.partial(plan_kernel, paired),
        [IN_SMEM, IN_SMEM, IN_VMEM],
        (floats(2, own_rows, width), floats((3 + spans) * members + 1, width)),
        (failed_ids, generator, previous_parity[0]),
        4 * spans * own_rows * width,
    )
    parity_shape = floats(own_rows, spans * width)
    rebuild_cost = 4 * slab_rows * width
    parity_cost = 2 * spans * slab_rows * width
    if paired:
        block = floats(own_rows, width)
        own, *others = targets_of(EARLIER_ROUNDS, members)
        far = cut(earlier, [others[1], others[2]])
        later, far[0] = lax.optimization_barrier((earlier, far[0]))
        own_earlier, next_earlier = cut(later, [own, others[0]])
        cut_earlier = far[:0] + [next_earlier] + far[0:]
        earlier_rows = pass_on(cut_earlier, EARLIER_ROUNDS, members)
        own_current, *cut_current = cut(current, targets_of(CURRENT_ROUNDS, members))
        outgoing = call(
            rebuild_paired_kernel,
            [IN_VMEM] * (members + 2),
            [block] * members,
            (base, table, own_earlier, *earlier_rows),
            rebuild_cost,
        )
        incoming = pass_on(outgoing[1:], REBUILT_ROUNDS, members)
        current_rows = [own_current, *pass_on(cut_current, CURRENT_ROUNDS, members)]
        new_parity, parity_done = call(
            parity_paired_kernel,
            [IN_VMEM] * (members + 1),
            (parity_shape, floats(8, 128)),
            (table, *current_rows),
            parity_cost,
        )
        settled = call(settle_kernel, [IN_VMEM], floats(*blocks), (earlier,), 0)
        restored_state = call(
            restore_kernel,
            [IN_VMEM, ANYWHERE, ANYWHERE] + [IN_VMEM] * members,
            floats(*blocks),
            (table, parity_done, settled, outgoing[0], *incoming),
            0,
            out_specs=ANYWHERE,
            input_output_aliases={2: 0},
            scratch_shapes=[pltpu.SemaphoreType.DMA((members,))],
        )
    else:
        earlier_rows = lax.all_to_all(earlier, "code", 0, 0, tiled=True)
        current_rows = lax.all_to_all(current, "code", 0, 0, tiled=True)
        outgoing = call(
            rebuild_whole_kernel,
            [IN_VMEM] * 3,
            floats(*blocks),
            (base, table, earlier_rows),
            rebuild_cost,
        )
        incoming = lax.all_to_all(outgoing, "code", 0, 0, tiled=True)
        lost = (position == failed_ids[0, 0]) | (position == failed_ids[0, 1])
        restored_state = jnp.where(lost, incoming, earlier)
        new_parity = call(
            parity_whole_kernel,
            [IN_VMEM] * 2,
            parity_shape,
            (table, current_rows),
            parity_cost,
        )
    return (new_parity[None], restored_state.reshape(state_slab.shape))


def solution(mesh):
    placed = (
        P(("grp", "rep"), "code", None, None),
        P(("grp", "rep"), "code", None, None),
        P(("grp", "rep"), "code", None),
        P(),
        P(("grp", "rep"), None),
    )
    return jax.shard_map(
        local,
        mesh=mesh,
        in_specs=placed,
        out_specs=(P(("grp", "rep"), "code", None), P(("grp", "rep"), "code", None, None)),
        check_vma=False,
    )
```

```python
import functools

import jax
import jax.numpy as jnp
from jax import lax
from jax.experimental import pallas as pl
from jax.experimental.pallas import tpu as pltpu
from jax.sharding import PartitionSpec as P

IN_VMEM = pl.BlockSpec(memory_space=pltpu.VMEM)
IN_SMEM = pl.BlockSpec(memory_space=pltpu.SMEM)
ANYWHERE = pl.BlockSpec(memory_space=pl.ANY)

PAIRED_MEMBERS = 4
KERNEL_VMEM = 8 * 2**20

EARLIER_ROUNDS = (("xor", 1), ("xor", 2), ("xor", 3))
CURRENT_ROUNDS = (("on", 3), ("on", 2), ("on", 1))
REBUILT_ROUNDS = (("on", 1), ("on", 2), ("on", 3))


def target(d, way, n, members):
    return d ^ n if way == "xor" else (d + n) % members


def source(d, way, n, members):
    return d ^ n if way == "xor" else (d + members - n) % members


def targets_of(rounds, members):
    me = lax.axis_index("code")
    return [me] + [target(me, *way, members) for way in rounds]


def sources_of(rounds, members):
    me = lax.axis_index("code")
    return [me] + [source(me, *way, members) for way in rounds]


def plan_kernel(paired, ids_ref, generator_ref, parity_ref, base_ref, table_ref):
    spans, members = generator_ref.shape
    width = base_ref.shape[2]
    first, second = ids_ref[0, 0], ids_ref[0, 1]
    col_first = [generator_ref[j, first] for j in range(spans)]
    col_second = [generator_ref[j, second] for j in range(spans)]
    gram_first = sum(x * x for x in col_first)
    gram_cross = sum(x * y for x, y in zip(col_first, col_second))
    gram_second = sum(y * y for y in col_second)
    determinant = gram_first * gram_second - gram_cross * gram_cross

    def spread(value):
        return jnp.full((1, width), value, jnp.float32)

    def put(row, value):
        table_ref[row : row + 1, :] = value

    over = spread(determinant)
    weights = [
        [spread(gram_second * x - gram_cross * y) / over for x, y in zip(col_first, col_second)],
        [spread(gram_first * y - gram_cross * x) / over for x, y in zip(col_first, col_second)],
    ]
    for k in range(2):
        base_ref[k] = sum(
            weights[k][j] * parity_ref[:, j * width : (j + 1) * width] for j in range(spans)
        )
    from_earlier = from_current = to_rebuilt = range(members)
    if paired:
        from_earlier = sources_of(EARLIER_ROUNDS, members)
        from_current = sources_of(CURRENT_ROUNDS, members)
        to_rebuilt = targets_of(REBUILT_ROUNDS, members)
    for i, c in enumerate(from_earlier):
        column = [generator_ref[j, c] for j in range(spans)]
        alive = jnp.logical_and(first != c, second != c)
        for k in range(2):
            put(
                k * members + i,
                sum(weights[k][j] * jnp.where(alive, column[j], 0.0) for j in range(spans)),
            )
    for i, c in enumerate(from_current):
        for j in range(spans):
            put((2 + j) * members + i, spread(generator_ref[j, c]))
    for i, c in enumerate(to_rebuilt):
        put((2 + spans) * members + i, spread(jnp.where(first == c, 1.0, 0.0)))
    me = lax.axis_index("code")
    lost = jnp.logical_or(first == me, second == me)
    put((3 + spans) * members, spread(jnp.where(lost, 1.0, 0.0)))


def weigh(table_ref, start, rows):
    total = None
    for i, block in enumerate(rows):
        term = table_ref[start + i : start + i + 1, :] * block
        total = term if total is None else total + term
    return total


def rebuilt_for(base_ref, table_ref, rows):
    members = len(rows)
    rebuilt = [base_ref[k] - weigh(table_ref, k * members, rows) for k in range(2)]
    picks = table_ref.shape[0] - 1 - members
    return [
        jnp.where(table_ref[picks + i : picks + i + 1, :] > 0.5, *rebuilt) for i in range(members)
    ]


def rebuild_whole_kernel(base_ref, table_ref, rows_ref, out_ref):
    rows = [rows_ref[c] for c in range(rows_ref.shape[0])]
    for c, block in enumerate(rebuilt_for(base_ref, table_ref, rows)):
        out_ref[c] = block


def parity_whole_kernel(table_ref, rows_ref, out_ref):
    parity_into(out_ref, table_ref, [rows_ref[c] for c in range(rows_ref.shape[0])])


def parity_into(out_ref, table_ref, rows):
    members, width = len(rows), table_ref.shape[1]
    for j in range(out_ref.shape[1] // width):
        out_ref[:, j * width : (j + 1) * width] = weigh(table_ref, (2 + j) * members, rows)


def rebuild_paired_kernel(base_ref, table_ref, *refs):
    rows, outs = refs[: len(refs) // 2], refs[len(refs) // 2 :]
    for out_ref, block in zip(outs, rebuilt_for(base_ref, table_ref, [r[...] for r in rows])):
        out_ref[...] = block


def parity_paired_kernel(table_ref, *refs):
    rows, out_ref, done_ref = refs[:-2], refs[-2], refs[-1]
    parity_into(out_ref, table_ref, [r[...] for r in rows])
    done_ref[...] = jnp.zeros(done_ref.shape, done_ref.dtype)


def settle_kernel(earlier_ref, out_ref):
    out_ref[...] = earlier_ref[...]


def restore_kernel(table_ref, held_back_by, settled_ref, *refs):
    pieces, (out_ref, sems) = refs[:-2], refs[-2:]
    members = len(pieces)
    last = table_ref.shape[0] - 1

    @pl.when(table_ref[last, 0] > 0.5)
    def _():
        half = pieces[0].shape[0] // 2
        copies = [
            pltpu.make_async_copy(piece.at[rows], out_ref.at[c, rows], sems.at[i, k])
            for i, (c, piece) in enumerate(zip(sources_of(REBUILT_ROUNDS, members), pieces))
            for k, rows in enumerate((pl.ds(0, half), pl.ds(half, half)))
        ]
        for copy in copies:
            copy.start()
        for copy in copies:
            copy.wait()


def call(kernel, specs, outs, args, flops, **options):
    total = sum(x.size for x in args) + sum(o.size for o in jax.tree.leaves(outs))
    options.setdefault("out_specs", jax.tree.map(lambda _: IN_VMEM, outs))
    return pl.pallas_call(
        kernel,
        in_specs=specs,
        out_shape=outs,
        compiler_params=pltpu.CompilerParams(vmem_limit_bytes=KERNEL_VMEM),
        cost_estimate=pl.CostEstimate(flops=flops, bytes_accessed=4 * total, transcendentals=0),
        **options,
    )(*args)


def floats(*shape):
    return jax.ShapeDtypeStruct(shape, jnp.float32)


def pass_on(pieces, rounds, members):
    return [
        lax.ppermute(
            piece, "code", [(d, target(d, *way, members)) for d in range(members)]
        )
        for way, piece in zip(rounds, pieces)
    ]


def cut(blocks, order):
    return [lax.dynamic_index_in_dim(blocks, c, 0, keepdims=False) for c in order]


def local(state_slab, previous_slab, previous_parity, generator, failed_ids):
    position = lax.axis_index("code")
    members = lax.axis_size("code")
    slab_rows, width = state_slab.shape[2:]
    spans = generator.shape[0]
    own_rows = slab_rows // members
    blocks = (members, own_rows, width)
    earlier = previous_slab.reshape(blocks)
    current = state_slab.reshape(blocks)
    paired = members == PAIRED_MEMBERS

    base, table = call(
        functools.partial(plan_kernel, paired),
        [IN_SMEM, IN_SMEM, IN_VMEM],
        (floats(2, own_rows, width), floats((3 + spans) * members + 1, width)),
        (failed_ids, generator, previous_parity[0]),
        4 * spans * own_rows * width,
    )
    parity_shape = floats(own_rows, spans * width)
    rebuild_cost = 4 * slab_rows * width
    parity_cost = 2 * spans * slab_rows * width
    if paired:
        block = floats(own_rows, width)
        own, *others = targets_of(EARLIER_ROUNDS, members)
        far = cut(earlier, [others[1], others[2]])
        later, far[0] = lax.optimization_barrier((earlier, far[0]))
        own_earlier, next_earlier = cut(later, [own, others[0]])
        cut_earlier = far[:0] + [next_earlier] + far[0:]
        earlier_rows = pass_on(cut_earlier, EARLIER_ROUNDS, members)
        own_current, *cut_current = cut(current, targets_of(CURRENT_ROUNDS, members))
        outgoing = call(
            rebuild_paired_kernel,
            [IN_VMEM] * (members + 2),
            [block] * members,
            (base, table, own_earlier, *earlier_rows),
            rebuild_cost,
        )
        incoming = pass_on(outgoing[1:], REBUILT_ROUNDS, members)
        current_rows = [own_current, *pass_on(cut_current, CURRENT_ROUNDS, members)]
        new_parity, parity_done = call(
            parity_paired_kernel,
            [IN_VMEM] * (members + 1),
            (parity_shape, floats(8, 128)),
            (table, *current_rows),
            parity_cost,
        )
        settled = call(settle_kernel, [IN_VMEM], floats(*blocks), (earlier,), 0)
        restored_state = call(
            restore_kernel,
            [IN_VMEM, ANYWHERE, ANYWHERE] + [IN_VMEM] * members,
            floats(*blocks),
            (table, parity_done, settled, outgoing[0], *incoming),
            0,
            out_specs=ANYWHERE,
            input_output_aliases={2: 0},
            scratch_shapes=[pltpu.SemaphoreType.DMA((members, 2))],
        )
    else:
        earlier_rows = lax.all_to_all(earlier, "code", 0, 0, tiled=True)
        current_rows = lax.all_to_all(current, "code", 0, 0, tiled=True)
        outgoing = call(
            rebuild_whole_kernel,
            [IN_VMEM] * 3,
            floats(*blocks),
            (base, table, earlier_rows),
            rebuild_cost,
        )
        incoming = lax.all_to_all(outgoing, "code", 0, 0, tiled=True)
        lost = (position == failed_ids[0, 0]) | (position == failed_ids[0, 1])
        restored_state = jnp.where(lost, incoming, earlier)
        new_parity = call(
            parity_whole_kernel,
            [IN_VMEM] * 2,
            parity_shape,
            (table, current_rows),
            parity_cost,
        )
    return (new_parity[None], restored_state.reshape(state_slab.shape))


def solution(mesh):
    placed = (
        P(("grp", "rep"), "code", None, None),
        P(("grp", "rep"), "code", None, None),
        P(("grp", "rep"), "code", None),
        P(),
        P(("grp", "rep"), None),
    )
    return jax.shard_map(
        local,
        mesh=mesh,
        in_specs=placed,
        out_specs=(P(("grp", "rep"), "code", None), P(("grp", "rep"), "code", None, None)),
        check_vma=False,
    )
```

```python
import functools

import jax
import jax.numpy as jnp
from jax import lax
from jax.experimental import pallas as pl
from jax.experimental.pallas import tpu as pltpu
from jax.sharding import PartitionSpec as P

IN_VMEM = pl.BlockSpec(memory_space=pltpu.VMEM)
IN_SMEM = pl.BlockSpec(memory_space=pltpu.SMEM)
ANYWHERE = pl.BlockSpec(memory_space=pl.ANY)

PAIRED_MEMBERS = 4
KERNEL_VMEM = 8 * 2**20

EARLIER_ROUNDS = (("xor", 1), ("xor", 3), ("xor", 2))
CURRENT_ROUNDS = (("on", 3), ("on", 2), ("on", 1))
REBUILT_ROUNDS = (("on", 2), ("on", 1), ("on", 3))


def target(d, way, n, members):
    return d ^ n if way == "xor" else (d + n) % members


def source(d, way, n, members):
    return d ^ n if way == "xor" else (d + members - n) % members


def targets_of(rounds, members):
    me = lax.axis_index("code")
    return [me] + [target(me, *way, members) for way in rounds]


def sources_of(rounds, members):
    me = lax.axis_index("code")
    return [me] + [source(me, *way, members) for way in rounds]


def plan_kernel(paired, ids_ref, generator_ref, parity_ref, base_ref, table_ref):
    spans, members = generator_ref.shape
    width = base_ref.shape[2]
    first, second = ids_ref[0, 0], ids_ref[0, 1]
    col_first = [generator_ref[j, first] for j in range(spans)]
    col_second = [generator_ref[j, second] for j in range(spans)]
    gram_first = sum(x * x for x in col_first)
    gram_cross = sum(x * y for x, y in zip(col_first, col_second))
    gram_second = sum(y * y for y in col_second)
    determinant = gram_first * gram_second - gram_cross * gram_cross

    def spread(value):
        return jnp.full((1, width), value, jnp.float32)

    def put(row, value):
        table_ref[row : row + 1, :] = value

    over = spread(determinant)
    weights = [
        [spread(gram_second * x - gram_cross * y) / over for x, y in zip(col_first, col_second)],
        [spread(gram_first * y - gram_cross * x) / over for x, y in zip(col_first, col_second)],
    ]
    for k in range(2):
        base_ref[k] = sum(
            weights[k][j] * parity_ref[:, j * width : (j + 1) * width] for j in range(spans)
        )
    from_earlier = from_current = to_rebuilt = range(members)
    if paired:
        from_earlier = sources_of(EARLIER_ROUNDS, members)
        from_current = sources_of(CURRENT_ROUNDS, members)
        to_rebuilt = targets_of(REBUILT_ROUNDS, members)
    for i, c in enumerate(from_earlier):
        column = [generator_ref[j, c] for j in range(spans)]
        alive = jnp.logical_and(first != c, second != c)
        for k in range(2):
            put(
                k * members + i,
                sum(weights[k][j] * jnp.where(alive, column[j], 0.0) for j in range(spans)),
            )
    for i, c in enumerate(from_current):
        for j in range(spans):
            put((2 + j) * members + i, spread(generator_ref[j, c]))
    for i, c in enumerate(to_rebuilt):
        put((2 + spans) * members + i, spread(jnp.where(first == c, 1.0, 0.0)))
    me = lax.axis_index("code")
    lost = jnp.logical_or(first == me, second == me)
    put((3 + spans) * members, spread(jnp.where(lost, 1.0, 0.0)))


def weigh(table_ref, start, rows):
    total = None
    for i, block in enumerate(rows):
        term = table_ref[start + i : start + i + 1, :] * block
        total = term if total is None else total + term
    return total


def rebuilt_for(base_ref, table_ref, rows):
    members = len(rows)
    rebuilt = [base_ref[k] - weigh(table_ref, k * members, rows) for k in range(2)]
    picks = table_ref.shape[0] - 1 - members
    return [
        jnp.where(table_ref[picks + i : picks + i + 1, :] > 0.5, *rebuilt) for i in range(members)
    ]


def rebuild_whole_kernel(base_ref, table_ref, rows_ref, out_ref):
    rows = [rows_ref[c] for c in range(rows_ref.shape[0])]
    for c, block in enumerate(rebuilt_for(base_ref, table_ref, rows)):
        out_ref[c] = block


def parity_whole_kernel(table_ref, rows_ref, out_ref):
    parity_into(out_ref, table_ref, [rows_ref[c] for c in range(rows_ref.shape[0])])


def parity_into(out_ref, table_ref, rows):
    members, width = len(rows), table_ref.shape[1]
    for j in range(out_ref.shape[1] // width):
        out_ref[:, j * width : (j + 1) * width] = weigh(table_ref, (2 + j) * members, rows)


def rebuild_paired_kernel(base_ref, table_ref, *refs):
    rows, outs = refs[: len(refs) // 2], refs[len(refs) // 2 :]
    for out_ref, block in zip(outs, rebuilt_for(base_ref, table_ref, [r[...] for r in rows])):
        out_ref[...] = block


def parity_paired_kernel(table_ref, *refs):
    rows, out_ref, done_ref = refs[:-2], refs[-2], refs[-1]
    parity_into(out_ref, table_ref, [r[...] for r in rows])
    done_ref[...] = jnp.zeros(done_ref.shape, done_ref.dtype)


def settle_kernel(earlier_ref, out_ref):
    out_ref[...] = earlier_ref[...]


def restore_kernel(table_ref, held_back_by, settled_ref, *refs):
    pieces, (out_ref, sems) = refs[:-2], refs[-2:]
    members = len(pieces)
    last = table_ref.shape[0] - 1

    @pl.when(table_ref[last, 0] > 0.5)
    def _():
        copies = [
            pltpu.make_async_copy(piece, out_ref.at[c], sems.at[i])
            for i, (c, piece) in enumerate(zip(sources_of(REBUILT_ROUNDS, members), pieces))
        ]
        for copy in copies:
            copy.start()
        for copy in copies:
            copy.wait()


def call(kernel, specs, outs, args, flops, **options):
    total = sum(x.size for x in args) + sum(o.size for o in jax.tree.leaves(outs))
    options.setdefault("out_specs", jax.tree.map(lambda _: IN_VMEM, outs))
    return pl.pallas_call(
        kernel,
        in_specs=specs,
        out_shape=outs,
        compiler_params=pltpu.CompilerParams(vmem_limit_bytes=KERNEL_VMEM),
        cost_estimate=pl.CostEstimate(flops=flops, bytes_accessed=4 * total, transcendentals=0),
        **options,
    )(*args)


def floats(*shape):
    return jax.ShapeDtypeStruct(shape, jnp.float32)


def pass_on(pieces, rounds, members):
    return [
        lax.ppermute(
            piece, "code", [(d, target(d, *way, members)) for d in range(members)]
        )
        for way, piece in zip(rounds, pieces)
    ]


def cut(blocks, order):
    return [lax.dynamic_index_in_dim(blocks, c, 0, keepdims=False) for c in order]


def local(state_slab, previous_slab, previous_parity, generator, failed_ids):
    position = lax.axis_index("code")
    members = lax.axis_size("code")
    slab_rows, width = state_slab.shape[2:]
    spans = generator.shape[0]
    own_rows = slab_rows // members
    blocks = (members, own_rows, width)
    earlier = previous_slab.reshape(blocks)
    current = state_slab.reshape(blocks)
    paired = members == PAIRED_MEMBERS

    base, table = call(
        functools.partial(plan_kernel, paired),
        [IN_SMEM, IN_SMEM, IN_VMEM],
        (floats(2, own_rows, width), floats((3 + spans) * members + 1, width)),
        (failed_ids, generator, previous_parity[0]),
        4 * spans * own_rows * width,
    )
    parity_shape = floats(own_rows, spans * width)
    rebuild_cost = 4 * slab_rows * width
    parity_cost = 2 * spans * slab_rows * width
    if paired:
        block = floats(own_rows, width)
        own, *others = targets_of(EARLIER_ROUNDS, members)
        far = cut(earlier, [others[1], others[2]])
        later, far[0] = lax.optimization_barrier((earlier, far[0]))
        own_earlier, next_earlier = cut(later, [own, others[0]])
        cut_earlier = far[:0] + [next_earlier] + far[0:]
        earlier_rows = pass_on(cut_earlier, EARLIER_ROUNDS, members)
        own_current, *cut_current = cut(current, targets_of(CURRENT_ROUNDS, members))
        outgoing = call(
            rebuild_paired_kernel,
            [IN_VMEM] * (members + 2),
            [block] * members,
            (base, table, own_earlier, *earlier_rows),
            rebuild_cost,
        )
        incoming = pass_on(outgoing[1:], REBUILT_ROUNDS, members)
        current_rows = [own_current, *pass_on(cut_current, CURRENT_ROUNDS, members)]
        new_parity, parity_done = call(
            parity_paired_kernel,
            [IN_VMEM] * (members + 1),
            (parity_shape, floats(8, 128)),
            (table, *current_rows),
            parity_cost,
        )
        settled = call(settle_kernel, [IN_VMEM], floats(*blocks), (earlier,), 0)
        restored_state = call(
            restore_kernel,
            [IN_VMEM, ANYWHERE, ANYWHERE] + [IN_VMEM] * members,
            floats(*blocks),
            (table, parity_done, settled, outgoing[0], *incoming),
            0,
            out_specs=ANYWHERE,
            input_output_aliases={2: 0},
            scratch_shapes=[pltpu.SemaphoreType.DMA((members,))],
        )
    else:
        earlier_rows = lax.all_to_all(earlier, "code", 0, 0, tiled=True)
        current_rows = lax.all_to_all(current, "code", 0, 0, tiled=True)
        outgoing = call(
            rebuild_whole_kernel,
            [IN_VMEM] * 3,
            floats(*blocks),
            (base, table, earlier_rows),
            rebuild_cost,
        )
        incoming = lax.all_to_all(outgoing, "code", 0, 0, tiled=True)
        lost = (position == failed_ids[0, 0]) | (position == failed_ids[0, 1])
        restored_state = jnp.where(lost, incoming, earlier)
        new_parity = call(
            parity_whole_kernel,
            [IN_VMEM] * 2,
            parity_shape,
            (table, current_rows),
            parity_cost,
        )
    return (new_parity[None], restored_state.reshape(state_slab.shape))


def solution(mesh):
    placed = (
        P(("grp", "rep"), "code", None, None),
        P(("grp", "rep"), "code", None, None),
        P(("grp", "rep"), "code", None),
        P(),
        P(("grp", "rep"), None),
    )
    return jax.shard_map(
        local,
        mesh=mesh,
        in_specs=placed,
        out_specs=(P(("grp", "rep"), "code", None), P(("grp", "rep"), "code", None, None)),
        check_vma=False,
    )
```

```python
import functools

import jax
import jax.numpy as jnp
from jax import lax
from jax.experimental import pallas as pl
from jax.experimental.pallas import tpu as pltpu
from jax.sharding import PartitionSpec as P

IN_VMEM = pl.BlockSpec(memory_space=pltpu.VMEM)
IN_SMEM = pl.BlockSpec(memory_space=pltpu.SMEM)
ANYWHERE = pl.BlockSpec(memory_space=pl.ANY)

PAIRED_MEMBERS = 4
KERNEL_VMEM = 8 * 2**20

EARLIER_ROUNDS = (("xor", 1), ("xor", 2), ("xor", 3))
CURRENT_ROUNDS = (("on", 3), ("on", 1), ("on", 2))
REBUILT_ROUNDS = (("on", 1), ("on", 2), ("on", 3))


def target(d, way, n, members):
    return d ^ n if way == "xor" else (d + n) % members


def source(d, way, n, members):
    return d ^ n if way == "xor" else (d + members - n) % members


def targets_of(rounds, members):
    me = lax.axis_index("code")
    return [me] + [target(me, *way, members) for way in rounds]


def sources_of(rounds, members):
    me = lax.axis_index("code")
    return [me] + [source(me, *way, members) for way in rounds]


def plan_kernel(paired, ids_ref, generator_ref, parity_ref, base_ref, table_ref):
    spans, members = generator_ref.shape
    width = base_ref.shape[2]
    first, second = ids_ref[0, 0], ids_ref[0, 1]
    col_first = [generator_ref[j, first] for j in range(spans)]
    col_second = [generator_ref[j, second] for j in range(spans)]
    gram_first = sum(x * x for x in col_first)
    gram_cross = sum(x * y for x, y in zip(col_first, col_second))
    gram_second = sum(y * y for y in col_second)
    determinant = gram_first * gram_second - gram_cross * gram_cross

    def spread(value):
        return jnp.full((1, width), value, jnp.float32)

    def put(row, value):
        table_ref[row : row + 1, :] = value

    over = spread(determinant)
    weights = [
        [spread(gram_second * x - gram_cross * y) / over for x, y in zip(col_first, col_second)],
        [spread(gram_first * y - gram_cross * x) / over for x, y in zip(col_first, col_second)],
    ]
    for k in range(2):
        base_ref[k] = sum(
            weights[k][j] * parity_ref[:, j * width : (j + 1) * width] for j in range(spans)
        )
    from_earlier = from_current = to_rebuilt = range(members)
    if paired:
        from_earlier = sources_of(EARLIER_ROUNDS, members)
        from_current = sources_of(CURRENT_ROUNDS, members)
        to_rebuilt = targets_of(REBUILT_ROUNDS, members)
    for i, c in enumerate(from_earlier):
        column = [generator_ref[j, c] for j in range(spans)]
        alive = jnp.logical_and(first != c, second != c)
        for k in range(2):
            put(
                k * members + i,
                sum(weights[k][j] * jnp.where(alive, column[j], 0.0) for j in range(spans)),
            )
    for i, c in enumerate(from_current):
        for j in range(spans):
            put((2 + j) * members + i, spread(generator_ref[j, c]))
    for i, c in enumerate(to_rebuilt):
        put((2 + spans) * members + i, spread(jnp.where(first == c, 1.0, 0.0)))
    me = lax.axis_index("code")
    lost = jnp.logical_or(first == me, second == me)
    put((3 + spans) * members, spread(jnp.where(lost, 1.0, 0.0)))


def weigh(table_ref, start, rows):
    total = None
    for i, block in enumerate(rows):
        term = table_ref[start + i : start + i + 1, :] * block
        total = term if total is None else total + term
    return total


def rebuilt_for(base_ref, table_ref, rows):
    members = len(rows)
    rebuilt = [base_ref[k] - weigh(table_ref, k * members, rows) for k in range(2)]
    picks = table_ref.shape[0] - 1 - members
    return [
        jnp.where(table_ref[picks + i : picks + i + 1, :] > 0.5, *rebuilt) for i in range(members)
    ]


def rebuild_whole_kernel(base_ref, table_ref, rows_ref, out_ref):
    rows = [rows_ref[c] for c in range(rows_ref.shape[0])]
    for c, block in enumerate(rebuilt_for(base_ref, table_ref, rows)):
        out_ref[c] = block


def parity_whole_kernel(table_ref, rows_ref, out_ref):
    parity_into(out_ref, table_ref, [rows_ref[c] for c in range(rows_ref.shape[0])])


def parity_into(out_ref, table_ref, rows):
    members, width = len(rows), table_ref.shape[1]
    for j in range(out_ref.shape[1] // width):
        out_ref[:, j * width : (j + 1) * width] = weigh(table_ref, (2 + j) * members, rows)


def rebuild_paired_kernel(base_ref, table_ref, *refs):
    rows, outs = refs[: len(refs) // 2], refs[len(refs) // 2 :]
    for out_ref, block in zip(outs, rebuilt_for(base_ref, table_ref, [r[...] for r in rows])):
        out_ref[...] = block


def parity_paired_kernel(table_ref, *refs):
    rows, out_ref, done_ref = refs[:-2], refs[-2], refs[-1]
    parity_into(out_ref, table_ref, [r[...] for r in rows])
    done_ref[...] = jnp.zeros(done_ref.shape, done_ref.dtype)


def settle_kernel(earlier_ref, out_ref):
    out_ref[...] = earlier_ref[...]


def restore_kernel(table_ref, held_back_by, settled_ref, *refs):
    pieces, (out_ref, sems) = refs[:-2], refs[-2:]
    members = len(pieces)
    last = table_ref.shape[0] - 1

    @pl.when(table_ref[last, 0] > 0.5)
    def _():
        copies = [
            pltpu.make_async_copy(piece, out_ref.at[c], sems.at[i])
            for i, (c, piece) in enumerate(zip(sources_of(REBUILT_ROUNDS, members), pieces))
        ]
        for copy in copies:
            copy.start()
        for copy in copies:
            copy.wait()


def call(kernel, specs, outs, args, flops, **options):
    total = sum(x.size for x in args) + sum(o.size for o in jax.tree.leaves(outs))
    options.setdefault("out_specs", jax.tree.map(lambda _: IN_VMEM, outs))
    return pl.pallas_call(
        kernel,
        in_specs=specs,
        out_shape=outs,
        compiler_params=pltpu.CompilerParams(vmem_limit_bytes=KERNEL_VMEM),
        cost_estimate=pl.CostEstimate(flops=flops, bytes_accessed=4 * total, transcendentals=0),
        **options,
    )(*args)


def floats(*shape):
    return jax.ShapeDtypeStruct(shape, jnp.float32)


def pass_on(pieces, rounds, members):
    return [
        lax.ppermute(
            piece, "code", [(d, target(d, *way, members)) for d in range(members)]
        )
        for way, piece in zip(rounds, pieces)
    ]


def cut(blocks, order):
    return [lax.dynamic_index_in_dim(blocks, c, 0, keepdims=False) for c in order]


def local(state_slab, previous_slab, previous_parity, generator, failed_ids):
    position = lax.axis_index("code")
    members = lax.axis_size("code")
    slab_rows, width = state_slab.shape[2:]
    spans = generator.shape[0]
    own_rows = slab_rows // members
    blocks = (members, own_rows, width)
    earlier = previous_slab.reshape(blocks)
    current = state_slab.reshape(blocks)
    paired = members == PAIRED_MEMBERS

    base, table = call(
        functools.partial(plan_kernel, paired),
        [IN_SMEM, IN_SMEM, IN_VMEM],
        (floats(2, own_rows, width), floats((3 + spans) * members + 1, width)),
        (failed_ids, generator, previous_parity[0]),
        4 * spans * own_rows * width,
    )
    parity_shape = floats(own_rows, spans * width)
    rebuild_cost = 4 * slab_rows * width
    parity_cost = 2 * spans * slab_rows * width
    if paired:
        block = floats(own_rows, width)
        own, *others = targets_of(EARLIER_ROUNDS, members)
        far = cut(earlier, [others[1], others[2]])
        later, far[0] = lax.optimization_barrier((earlier, far[0]))
        own_earlier, next_earlier = cut(later, [own, others[0]])
        cut_earlier = far[:0] + [next_earlier] + far[0:]
        earlier_rows = pass_on(cut_earlier, EARLIER_ROUNDS, members)
        own_current, *cut_current = cut(current, targets_of(CURRENT_ROUNDS, members))
        outgoing = call(
            rebuild_paired_kernel,
            [IN_VMEM] * (members + 2),
            [block] * members,
            (base, table, own_earlier, *earlier_rows),
            rebuild_cost,
        )
        incoming = pass_on(outgoing[1:], REBUILT_ROUNDS, members)
        current_rows = [own_current, *pass_on(cut_current, CURRENT_ROUNDS, members)]
        new_parity, parity_done = call(
            parity_paired_kernel,
            [IN_VMEM] * (members + 1),
            (parity_shape, floats(8, 128)),
            (table, *current_rows),
            parity_cost,
        )
        settled = call(settle_kernel, [IN_VMEM], floats(*blocks), (earlier,), 0)
        restored_state = call(
            restore_kernel,
            [IN_VMEM, ANYWHERE, ANYWHERE] + [IN_VMEM] * members,
            floats(*blocks),
            (table, parity_done, settled, outgoing[0], *incoming),
            0,
            out_specs=ANYWHERE,
            input_output_aliases={2: 0},
            scratch_shapes=[pltpu.SemaphoreType.DMA((members,))],
        )
    else:
        earlier_rows = lax.all_to_all(earlier, "code", 0, 0, tiled=True)
        current_rows = lax.all_to_all(current, "code", 0, 0, tiled=True)
        outgoing = call(
            rebuild_whole_kernel,
            [IN_VMEM] * 3,
            floats(*blocks),
            (base, table, earlier_rows),
            rebuild_cost,
        )
        incoming = lax.all_to_all(outgoing, "code", 0, 0, tiled=True)
        lost = (position == failed_ids[0, 0]) | (position == failed_ids[0, 1])
        restored_state = jnp.where(lost, incoming, earlier)
        new_parity = call(
            parity_whole_kernel,
            [IN_VMEM] * 2,
            parity_shape,
            (table, current_rows),
            parity_cost,
        )
    return (new_parity[None], restored_state.reshape(state_slab.shape))


def solution(mesh):
    placed = (
        P(("grp", "rep"), "code", None, None),
        P(("grp", "rep"), "code", None, None),
        P(("grp", "rep"), "code", None),
        P(),
        P(("grp", "rep"), None),
    )
    return jax.shard_map(
        local,
        mesh=mesh,
        in_specs=placed,
        out_specs=(P(("grp", "rep"), "code", None), P(("grp", "rep"), "code", None, None)),
        check_vma=False,
    )
```
